32 devices in a mesh: dp: 8 (over z, y), tensor: 4 (over x, core).
Axes of the slice: x: 2, y: 2, z: 4, core: 2. Of those that a mesh axis runs over, the one named last changes fastest.
Arguments:
- inputs: bfloat16 [16384, 1024], P(('dp', 'tensor')), may hold values from -6 to 6
- qkv_weight: bfloat16 [3, 1024, 1024], P(None, 'dp', 'tensor'), may hold values from -0.25 to 0.25
- qv_bias: bfloat16 [2, 1024], P(None, ('tensor', 'dp')), may hold values from -2 to 2
- proj_weight: bfloat16 [1024, 1024], P('tensor', 'dp'), may hold values from -0.5 to 0.5
- proj_bias: bfloat16 [1024], P('dp'), may hold values from -2 to 2
- fc_weight: bfloat16 [1024, 4096], P('dp', 'tensor'), may hold values from -0.1875 to 0.1875
- fc_bias: bfloat16 [4096], P(('tensor', 'dp')), may hold values from -2 to 2
- out_weight: bfloat16 [4096, 1024], P('tensor', 'dp'), may hold values from -0.1875 to 0.1875
- out_bias: bfloat16 [1024], P('dp'), may hold values from -2 to 2
- attn_norm_gain: bfloat16 [1024], P('dp'), may hold values from 0.5 to 1.5
- attn_norm_bias: bfloat16 [1024], P('dp'), may hold values from -2 to 2
- mlp_norm_gain: bfloat16 [1024], P('dp'), may hold values from 0.5 to 1.5
- mlp_norm_bias: bfloat16 [1024], P('dp'), may hold values from -2 to 2
- cotangent: bfloat16 [16384, 1024], P(('dp', 'tensor')), may hold values from -6 to 6
Outputs:
- outputs: bfloat16 [16384, 1024], P(('dp', 'tensor'))
- grad_inputs: bfloat16 [16384, 1024], P(('dp', 'tensor'))
- grad_qkv_weight: float32 [3, 1024, 1024], P(None, 'dp', 'tensor')
- grad_qv_bias: float32 [2, 1024], P(None, ('tensor', 'dp'))
- grad_proj_weight: float32 [1024, 1024], P('tensor', 'dp')
- grad_proj_bias: float32 [1024], P('dp')
- grad_fc_weight: float32 [1024, 4096], P('dp', 'tensor')
- grad_fc_bias: float32 [4096], P(('tensor', 'dp'))
- grad_out_weight: float32 [4096, 1024], P('tensor', 'dp')
- grad_out_bias: float32 [1024], P('dp')
- grad_attn_norm_gain: float32 [1024], P('dp')
- grad_attn_norm_bias: float32 [1024], P('dp')
- grad_mlp_norm_gain: float32 [1024], P('dp')
- grad_mlp_norm_bias: float32 [1024], P('dp')
The draws below stay inside these ranges and needn't reach their ends.
All inputs are finite; a program needn't handle non-finite values.
Results may differ from the reference program's by a relative error of at most 0.02.
Values may be sent and summed in bfloat16 or wider, within the bound.
No kernel may reach another device: no remote copies, remote signals or barrier semaphores. Data moves between devices by JAX's collectives and lax.ppermute only.
A program may use at most 192 MiB of HBM per device.

```python
import math
import jax
import jax.numpy as jnp
from jax import lax

D = 1024
HEADS = 16
HD = 64
FF = 4096
SEQ = 2048
SEQS = 8
TOKENS = 16384


def spiked(entries, rng, source, target, shards_of, factor):
    owner, partner = [(jnp.arange(entries.shape[dim]) // (entries.shape[dim] // shards_of)).reshape([-1 if axis == dim else 1 for axis in range(entries.ndim)]) for dim in (source, target)]
    chosen = jax.random.permutation(rng, shards_of)[partner]
    strong = (owner == chosen) | (owner == (partner + shards_of // 2) % shards_of)
    return jnp.where(strong, factor * entries, entries)


def level_of(stream_key, extent, pieces, smallest, top_value):
    gain, own = 1.0, jax.random.fold_in(stream_key, 6)
    for dim, blocks in pieces:
        steps = jnp.exp(jax.random.uniform(jax.random.fold_in(own, dim), (blocks,), jnp.float32, smallest / len(pieces), top_value / len(pieces)))
        gain = gain * jnp.repeat(steps, extent[dim] // blocks).reshape([-1 if axis == dim else 1 for axis in range(len(extent))])
    return gain


def gaussian(stream_key, extent, deviation, reach, pieces=(), kind=jnp.bfloat16):
    entries = jax.random.normal(stream_key, extent, jnp.float32) * deviation
    if len(pieces) > 0:
        entries = level_of(stream_key, extent, pieces, -0.22, 0.18) * entries
    return jnp.clip(entries, min=-reach, max=reach).astype(kind)


def bell_draw_with(own_key, shape, width, reach, shards, heavy, kind=jnp.bfloat16):
    entries = width * jax.random.normal(own_key, shape, jnp.float32)
    if shards:
        entries = entries * level_of(own_key, shape, shards, -0.22, 0.18)
    return jnp.clip(spiked(entries, jax.random.fold_in(own_key, 3), *heavy), -reach, reach).astype(kind)


def setup_inputs(seed: int = 0) -> dict:
    keys = jax.random.split(jax.random.key(seed), 15)
    inputs = gaussian(keys[0], (TOKENS, D), 1.0, 6.0, ((0, 32),))
    qkv_weight = gaussian(keys[1], (3, D, D), (D // 2) ** -0.5, 0.25, ((1, 8), (2, 4)))
    qv_bias = gaussian(keys[2], (2, D), 0.3, 2.0, ((1, 32),))
    proj_weight = gaussian(keys[3], (D, D), (D // 8) ** -0.5, 0.5, ((0, 4), (1, 8)))
    proj_bias = gaussian(keys[4], (D,), 0.3, 2.0, ((0, 8),))
    fc_weight = gaussian(keys[5], (D, FF), D ** -0.5, 0.1875, ((0, 8), (1, 4)))
    fc_bias = gaussian(keys[6], (FF,), 0.3, 2.0, ((0, 32),))
    out_weight = gaussian(keys[7], (FF, D), (FF // 4) ** -0.5, 0.1875, ((0, 4), (1, 8)))
    out_bias = gaussian(keys[8], (D,), 0.3, 2.0, ((0, 8),))
    attn_norm_gain = jnp.clip(1.0 + 0.1 * jax.random.normal(keys[9], (D,), jnp.float32), 0.5, 1.5).astype(jnp.bfloat16)
    attn_norm_bias = gaussian(keys[10], (D,), 0.3, 2.0, ((0, 8),))
    mlp_norm_gain = jnp.clip(1.0 + 0.1 * jax.random.normal(keys[11], (D,), jnp.float32), 0.5, 1.5).astype(jnp.bfloat16)
    mlp_norm_bias = gaussian(keys[12], (D,), 0.3, 2.0, ((0, 8),))
    cotangent = bell_draw_with(keys[13], (TOKENS, D), 1.0, 6.0, ((0, 32),), (0, 1, 32, 2.75))
    return dict(inputs=inputs, qkv_weight=qkv_weight, qv_bias=qv_bias, proj_weight=proj_weight, proj_bias=proj_bias, fc_weight=fc_weight, fc_bias=fc_bias, out_weight=out_weight, out_bias=out_bias, attn_norm_gain=attn_norm_gain, attn_norm_bias=attn_norm_bias, mlp_norm_gain=mlp_norm_gain, mlp_norm_bias=mlp_norm_bias, cotangent=cotangent)


EPSILON = 1e-05
NEGATIVE = -1e+30
ROOT_TWO_PI = 0.7978845608028654
HIGHEST = lax.Precision.HIGHEST

@jax.custom_vjp
def low(v):
    return lax.optimization_barrier(v.astype(jnp.bfloat16)).astype(jnp.float32)

@jax.custom_vjp
def low_back(v):
    return v

def low_keep(v):
    return (low(v), None)

def low_pass(kept, grad):
    return (grad,)

def back_keep(v):
    return (v, None)

def back_low(kept, grad):
    return (low(grad),)
low.defvjp(low_keep, low_pass)
low_back.defvjp(back_keep, back_low)

def layer_norm(values, gain_vec, shift_vec):
    average = lax.optimization_barrier(jnp.mean(values, axis=-1, keepdims=True))
    centered = values - average
    spread = lax.optimization_barrier(jnp.mean(centered * centered, axis=-1, keepdims=True))
    return centered * lax.rsqrt(spread + EPSILON) * gain_vec + shift_vec

def gelu_tanh(values):
    return 0.5 * values * (1.0 + jnp.tanh(ROOT_TWO_PI * (values + 0.044715 * values * values * values)))

def attend_block(queries, all_keys, all_values, offset):
    scores = jnp.einsum('qhd,khd->hqk', queries, all_keys, precision=HIGHEST) * (1.0 / math.sqrt(HD))
    row_pos = offset + jnp.arange(queries.shape[0], dtype=jnp.int32)[:, None]
    col_pos = jnp.arange(all_keys.shape[0], dtype=jnp.int32)[None, :]
    scores = low_back(jnp.where(col_pos <= row_pos, scores, NEGATIVE))
    maximum = lax.optimization_barrier(jnp.max(scores, axis=-1, keepdims=True))
    powers = jnp.exp(scores - maximum)
    weights = powers / lax.optimization_barrier(jnp.sum(powers, axis=-1, keepdims=True))
    return jnp.einsum('hqk,khd->qhd', low(weights), all_values, precision=HIGHEST)

def forward(inputs, qkv_weight, qv_bias, proj_weight, proj_bias, fc_weight, fc_bias, out_weight, out_bias, attn_norm_gain, attn_norm_bias, mlp_norm_gain, mlp_norm_bias):
    length = inputs.shape[0]
    normed_one = low(layer_norm(inputs, attn_norm_gain, attn_norm_bias))
    biases = jnp.stack([qv_bias[0], jnp.zeros_like(qv_bias[0]), qv_bias[1]])
    projected = jnp.einsum('sd,jde->jse', normed_one, qkv_weight, precision=HIGHEST) + biases[:, None, :]
    projected = low(low_back(projected))
    shaped = projected.reshape(3, length, HEADS, HD)
    block_rows = min(512, length)
    starts = jnp.arange(length // block_rows, dtype=jnp.int32) * block_rows
    query_blocks = shaped[0].reshape(length // block_rows, block_rows, HEADS, HD)
    block_fn = jax.checkpoint(attend_block)

    def one_block(pairing):
        return block_fn(pairing[0], shaped[1], shaped[2], pairing[1])
    attended = lax.map(one_block, (query_blocks, starts))
    mixed_heads = low(low_back(attended.reshape(length, HEADS * HD)))
    residual = inputs + low_back(jnp.dot(mixed_heads, proj_weight, precision=HIGHEST) + proj_bias)
    normed_two = low(layer_norm(residual, mlp_norm_gain, mlp_norm_bias))
    hidden = low_back(jnp.dot(normed_two, fc_weight, precision=HIGHEST) + fc_bias)
    activated = low(gelu_tanh(hidden))
    return residual + jnp.dot(activated, out_weight, precision=HIGHEST) + out_bias

def reference(inputs, qkv_weight, qv_bias, proj_weight, proj_bias, fc_weight, fc_bias, out_weight, out_bias, attn_norm_gain, attn_norm_bias, mlp_norm_gain, mlp_norm_bias, cotangent):
    params = tuple((member.astype(jnp.float32) for member in (qkv_weight, qv_bias, proj_weight, proj_bias, fc_weight, fc_bias, out_weight, out_bias, attn_norm_gain, attn_norm_bias, mlp_norm_gain, mlp_norm_bias)))
    seq_inputs = inputs.astype(jnp.float32).reshape(SEQS, SEQ, D)
    seq_cotan = cotangent.astype(jnp.float32).reshape(SEQS, SEQ, D)

    def one_sequence(running, pairing):
        result, pullback = jax.vjp(forward, pairing[0], *params)
        gradients = pullback(pairing[1])
        updated = tuple((before + update for before, update in zip(running, gradients[1:])))
        return (updated, (result, gradients[0]))
    zero_grads = tuple((jnp.zeros_like(member) for member in params))
    totals, (results, input_grads) = lax.scan(one_sequence, zero_grads, (seq_inputs, seq_cotan))
    return (results.reshape(TOKENS, D).astype(jnp.bfloat16), input_grads.reshape(TOKENS, D).astype(jnp.bfloat16), totals[0], totals[1], totals[2], totals[3], totals[4], totals[5], totals[6], totals[7], totals[8], totals[9], totals[10], totals[11])
```

```python
import functools

import jax
import jax.numpy as jnp
from jax import lax
from jax.experimental import pallas as pl
from jax.experimental.pallas import tpu as pltpu
from jax.sharding import PartitionSpec as P

HD = 64
PAIR = 2 * HD
EPSILON = 1e-05
NEGATIVE = -1e30
ROOT_TWO_PI = 0.7978845608028654
F32 = jnp.float32
BF16 = jnp.bfloat16
VMEM_LIMIT = 40 * 1024 * 1024


def swap_x(value):
    return lax.ppermute(value, "tensor", [(0, 2), (2, 0), (1, 3), (3, 1)])


def swap_core(value):
    return lax.ppermute(value, "tensor", [(0, 1), (1, 0), (2, 3), (3, 2)])


def dot(a, b, contract, kind=F32):
    return lax.dot_general(a, b, (contract, ((), ())), preferred_element_type=kind)


NN = ((1,), (0,))
NT = ((1,), (1,))
TN = ((0,), (0,))


def normalize(values):
    average = jnp.mean(values, axis=-1, keepdims=True)
    centered = values - average
    spread = jnp.mean(centered * centered, axis=-1, keepdims=True)
    factor = lax.rsqrt(spread + EPSILON)
    return centered * factor, factor


def norm_back(unit, factor, gain, grad):
    scaled = grad * gain
    return factor * (
        scaled
        - jnp.mean(scaled, axis=-1, keepdims=True)
        - unit * jnp.mean(scaled * unit, axis=-1, keepdims=True)
    )


def gelu_both(values):
    squared = values * values
    bent = jnp.tanh(ROOT_TWO_PI * values * (1.0 + 0.044715 * squared))
    half = 0.5 * (1.0 + bent)
    slope = half + 0.5 * values * (1.0 - bent * bent) * ROOT_TWO_PI * (
        1.0 + 3.0 * 0.044715 * squared
    )
    return values * half, slope


def keep_head(block, which):
    lane = lax.broadcasted_iota(jnp.int32, block.shape, 1)
    return jnp.where((lane // HD) == which, block.astype(F32), 0.0).astype(BF16)


def attend_kernel(qkv_ref, mixed_ref, total_ref, peak, sums, acc, *, row0, block):
    count = mixed_ref.shape[0] // block
    lane = lax.broadcasted_iota(jnp.int32, (block, PAIR), 1)
    first = lane < HD
    causal = lax.broadcasted_iota(jnp.int32, (block, block), 1) <= lax.broadcasted_iota(
        jnp.int32, (block, block), 0
    )
    for i in range(count):
        start = row0 + i * block
        queries = qkv_ref[pl.ds(start, block), 0:PAIR].astype(F32) * (HD**-0.5)
        heads = [
            jnp.where(first, queries, 0.0).astype(BF16),
            jnp.where(first, 0.0, queries).astype(BF16),
        ]
        keys = qkv_ref[pl.ds(start, block), PAIR : 2 * PAIR]
        values = qkv_ref[pl.ds(start, block), 2 * PAIR : 3 * PAIR]
        for h in range(2):
            scores = jnp.where(causal, dot(heads[h], keys, NT), NEGATIVE)
            top = jnp.max(scores, axis=-1, keepdims=True)
            powers = jnp.exp(scores - top)
            peak[h] = top
            sums[h] = jnp.sum(powers, axis=-1, keepdims=True)
            acc[h] = dot(powers.astype(BF16), values, NN)

        def step(j, carry):
            at = pl.multiple_of(j * block, block)
            tile_keys = qkv_ref[pl.ds(at, block), PAIR : 2 * PAIR]
            tile_values = qkv_ref[pl.ds(at, block), 2 * PAIR : 3 * PAIR]
            for h in range(2):
                scores = dot(heads[h], tile_keys, NT)
                before = peak[h]
                top = jnp.maximum(before, jnp.max(scores, axis=-1, keepdims=True))
                shrink = jnp.exp(before - top)
                powers = jnp.exp(scores - top)
                peak[h] = top
                sums[h] = sums[h] * shrink + jnp.sum(powers, axis=-1, keepdims=True)
                acc[h] = acc[h] * shrink + dot(powers.astype(BF16), tile_values, NN)
            return carry

        if start:
            lax.fori_loop(0, start // block, step, 0)
        out = jnp.where(first, acc[0] / sums[0], acc[1] / sums[1])
        mixed_ref[i * block : (i + 1) * block, :] = out.astype(BF16)
        total_ref[i * block : (i + 1) * block, :] = jnp.where(
            first, peak[0] + jnp.log(sums[0]), peak[1] + jnp.log(sums[1])
        )


def attend(qkv, row0, rows, block):
    pairs = qkv.shape[1] // (3 * PAIR)
    return pl.pallas_call(
        functools.partial(attend_kernel, row0=row0, block=block),
        grid=(pairs,),
        in_specs=[pl.BlockSpec((row0 + rows, 3 * PAIR), lambda j: (0, j))],
        out_specs=[
            pl.BlockSpec((rows, PAIR), lambda j: (0, j)),
            pl.BlockSpec((rows, PAIR), lambda j: (0, j)),
        ],
        out_shape=[
            jax.ShapeDtypeStruct((rows, pairs * PAIR), BF16),
            jax.ShapeDtypeStruct((rows, pairs * PAIR), F32),
        ],
        scratch_shapes=[
            pltpu.VMEM((2, block, 1), F32),
            pltpu.VMEM((2, block, 1), F32),
            pltpu.VMEM((2, block, PAIR), F32),
        ],
        compiler_params=pltpu.CompilerParams(vmem_limit_bytes=VMEM_LIMIT),
        name="attend_%d" % row0,
    )(qkv)


def attend_back_kernel(
    qkv_ref, mixed_ref, grad_ref, total_ref, *rest, row0, block, has_before
):
    if has_before:
        before_ref, out_ref, key_acc, value_acc, query_acc = rest
    else:
        out_ref, key_acc, value_acc, query_acc = rest
    rows = mixed_ref.shape[0]
    count = rows // block
    lane = lax.broadcasted_iota(jnp.int32, (block, PAIR), 1)
    first = lane < HD
    causal = lax.broadcasted_iota(jnp.int32, (block, block), 0) <= lax.broadcasted_iota(
        jnp.int32, (block, block), 1
    )
    if has_before:
        key_acc[0:row0, :] = before_ref[:, PAIR : 2 * PAIR]
        value_acc[0:row0, :] = before_ref[:, 2 * PAIR : 3 * PAIR]
        key_acc[row0:, :] = jnp.zeros((rows, PAIR), F32)
        value_acc[row0:, :] = jnp.zeros((rows, PAIR), F32)
    else:
        key_acc[...] = jnp.zeros(key_acc.shape, F32)
        value_acc[...] = jnp.zeros(value_acc.shape, F32)
    for i in range(count):
        start = row0 + i * block
        local = slice(i * block, (i + 1) * block)
        queries = qkv_ref[pl.ds(start, block), 0:PAIR].astype(F32) * (HD**-0.5)
        grads = grad_ref[local, :].astype(F32)
        totals = jnp.transpose(total_ref[local, :])
        inner = jnp.transpose(grads * mixed_ref[local, :].astype(F32))
        query_heads, grad_heads, total_rows, inner_rows = [], [], [], []
        for h in range(2):
            mine = first if h == 0 else jnp.logical_not(first)
            query_heads.append(jnp.where(mine, queries, 0.0).astype(BF16))
            grad_heads.append(jnp.where(mine, grads, 0.0).astype(BF16))
            total_rows.append(totals[h * HD : h * HD + 1, :])
            inner_rows.append(jnp.sum(inner[h * HD : (h + 1) * HD, :], axis=0, keepdims=True))

        def tile(at, masked):
            tile_keys = qkv_ref[pl.ds(at, block), PAIR : 2 * PAIR]
            tile_values = qkv_ref[pl.ds(at, block), 2 * PAIR : 3 * PAIR]
            key_sum, value_sum = None, None
            for h in range(2):
                scores = dot(tile_keys, query_heads[h], NT)
                weights = jnp.exp(scores - total_rows[h])
                if masked:
                    weights = jnp.where(causal, weights, 0.0)
                grad_weights = dot(tile_values, grad_heads[h], NT)
                grad_scores = (weights * (grad_weights - inner_rows[h])).astype(BF16)
                value_part = dot(weights.astype(BF16), grad_heads[h], NN)
                key_part = dot(grad_scores, query_heads[h], NN)
                query_part = dot(grad_scores, tile_keys, TN)
                key_sum = key_part if key_sum is None else key_sum + key_part
                value_sum = value_part if value_sum is None else value_sum + value_part
                if masked:
                    query_acc[h] = query_part
                else:
                    query_acc[h] += query_part
            key_acc[pl.ds(at, block), :] += key_sum
            value_acc[pl.ds(at, block), :] += value_sum

        tile(start, True)

        def step(j, carry):
            tile(pl.multiple_of(j * block, block), False)
            return carry

        if start:
            lax.fori_loop(0, start // block, step, 0)
        query_grad = jnp.where(first, query_acc[0], query_acc[1]) * (HD**-0.5)
        out_ref[start : start + block, 0:PAIR] = query_grad.astype(out_ref.dtype)
    if has_before:
        out_ref[0:row0, 0:PAIR] = before_ref[:, 0:PAIR].astype(out_ref.dtype)
    out_ref[:, PAIR : 2 * PAIR] = key_acc[...].astype(out_ref.dtype)
    out_ref[:, 2 * PAIR : 3 * PAIR] = value_acc[...].astype(out_ref.dtype)


def attend_back(qkv, mixed, grads, totals, before, row0, block):
    pairs = qkv.shape[1] // (3 * PAIR)
    rows = mixed.shape[0]
    extent = row0 + rows
    narrow = pl.BlockSpec((rows, PAIR), lambda j: (0, j))
    in_specs = [pl.BlockSpec((extent, 3 * PAIR), lambda j: (0, j)), narrow, narrow, narrow]
    operands = [qkv, mixed, grads, totals]
    if before is not None:
        in_specs.append(pl.BlockSpec((row0, 3 * PAIR), lambda j: (0, j)))
        operands.append(before)
    return pl.pallas_call(
        functools.partial(
            attend_back_kernel, row0=row0, block=block, has_before=before is not None
        ),
        grid=(pairs,),
        in_specs=in_specs,
        out_specs=pl.BlockSpec((extent, 3 * PAIR), lambda j: (0, j)),
        out_shape=jax.ShapeDtypeStruct(
            (extent, pairs * 3 * PAIR), F32 if before is None else BF16
        ),
        scratch_shapes=[
            pltpu.VMEM((extent, PAIR), F32),
            pltpu.VMEM((extent, PAIR), F32),
            pltpu.VMEM((2, block, PAIR), F32),
        ],
        compiler_params=pltpu.CompilerParams(vmem_limit_bytes=VMEM_LIMIT),
        name="attend_back_%d" % row0,
    )(*operands)


def local(
    inputs,
    qkv_weight,
    qv_bias,
    proj_weight,
    proj_bias,
    fc_weight,
    fc_bias,
    out_weight,
    out_bias,
    attn_norm_gain,
    attn_norm_bias,
    mlp_norm_gain,
    mlp_norm_bias,
    cotangent,
):
    width = inputs.shape[1]
    rows = inputs.shape[0]
    share = proj_bias.shape[0]
    parts = width // share
    head_cols = qkv_weight.shape[2]
    pairs = head_cols // PAIR
    qkv_cols = 3 * head_cols
    hidden_cols = fc_weight.shape[1]
    place = lax.axis_index("tensor")
    core = place % 2
    is_low = place < 2
    is_first = core == 0

    def pick_x(low, high):
        return jnp.where(is_low, low, high)

    qv_column = jnp.pad(qv_bias.reshape(-1), (0, share - qv_bias.size))
    vectors = jnp.stack(
        [
            proj_bias,
            out_bias,
            attn_norm_gain,
            attn_norm_bias,
            mlp_norm_gain,
            mlp_norm_bias,
            fc_bias,
            qv_column,
        ],
        axis=1,
    )
    qkv_shard = jnp.transpose(
        qkv_weight.reshape(3, share, pairs, PAIR), (1, 2, 0, 3)
    ).reshape(share, qkv_cols)
    attn_shard = jnp.concatenate(
        [qkv_shard, proj_weight.T, jnp.pad(vectors, ((0, 0), (0, 120)))], axis=1
    )
    attn_all = lax.all_gather(attn_shard, "dp", axis=0, tiled=True)
    mlp_shard = jnp.concatenate([fc_weight, out_weight.T], axis=1)
    mlp_all = lax.all_gather(mlp_shard, "dp", axis=0, tiled=True)

    input_x = swap_x(inputs)
    input_core = swap_core(inputs)
    input_far = swap_core(input_x)
    input_low, input_high = pick_x(inputs, input_x), pick_x(input_x, inputs)
    far_low, far_high = pick_x(input_core, input_far), pick_x(input_far, input_core)
    cot_x = swap_x(cotangent)
    cots = [pick_x(cotangent, cot_x), pick_x(cot_x, cotangent)]
    sequence = jnp.concatenate(
        [
            jnp.where(is_first, input_low, far_low),
            jnp.where(is_first, far_low, input_low),
            jnp.where(is_first, input_high, far_high),
            jnp.where(is_first, far_high, input_high),
        ],
        axis=0,
    )

    attn_sib = swap_core(attn_all)
    columns = attn_all[:, qkv_cols + head_cols : qkv_cols + head_cols + 8].astype(F32).T
    proj_shift, out_shift, gain_one, shift_one, gain_two, shift_two = [
        columns[i][None, :] for i in range(6)
    ]
    fc_shift = jnp.concatenate(
        [columns[6], attn_sib[:, qkv_cols + head_cols + 6].astype(F32)], axis=0
    )[None, :]
    qv_shift = (
        columns[7]
        .reshape(parts, share)[:, : share // 2]
        .reshape(parts, 2, share // 4)
        .transpose(1, 0, 2)
        .reshape(2, head_cols)
    )
    qkv_shift = jnp.stack([qv_shift[0], jnp.zeros_like(qv_shift[0]), qv_shift[1]])
    qkv_shift = qkv_shift.reshape(3, pairs, PAIR).transpose(1, 0, 2).reshape(1, qkv_cols)
    proj_both = jnp.concatenate(
        [
            attn_all[:, qkv_cols : qkv_cols + head_cols],
            attn_sib[:, qkv_cols : qkv_cols + head_cols],
        ],
        axis=1,
    )

    normed_one = (normalize(sequence.astype(F32))[0] * gain_one + shift_one).astype(BF16)
    qkv = (dot(normed_one, attn_all[:, :qkv_cols], NN) + qkv_shift).astype(BF16)

    mlp_sib = swap_core(mlp_all)
    fc_both = jnp.concatenate([mlp_all[:, :hidden_cols], mlp_sib[:, :hidden_cols]], axis=1)
    out_both = jnp.concatenate([mlp_all[:, hidden_cols:], mlp_sib[:, hidden_cols:]], axis=1)

    inputs_two = [input_low, input_high]
    mixed, totals = [], []
    mixed_rows, units, factors, normed_two, acts, grads_hidden = [], [], [], [], [], []
    residuals, out_parts = [], []
    grad_residuals, branches, grad_mixed = [], [], []
    for half in range(2):
        half_mixed, half_totals = attend(qkv, half * 2 * rows, 2 * rows, rows)
        mixed.append(half_mixed)
        totals.append(half_totals)
        two = half_mixed.reshape(2, rows, head_cols)
        mine = jnp.where(is_first, two[0], two[1])
        received = swap_core(jnp.where(is_first, two[1], two[0]))
        both = jnp.concatenate([mine, received], axis=1)
        mixed_rows.append(both)
        part = dot(both, proj_both, NT).astype(BF16)
        residual = (
            inputs_two[half].astype(F32) + part.astype(F32) + swap_x(part).astype(F32) + proj_shift
        )
        residuals.append(residual)
    for half in range(2):
        unit, factor = normalize(residuals[half])
        units.append(unit)
        factors.append(factor)
        normed = (unit * gain_two + shift_two).astype(BF16)
        normed_two.append(normed)
        grad_act = dot(cots[half], out_both, NN).astype(BF16)
        hidden = dot(normed, fc_both, NN) + fc_shift
        act, slope = gelu_both(hidden)
        act = act.astype(BF16)
        grad_hidden = (grad_act.astype(F32) * slope).astype(BF16)
        acts.append(act)
        grads_hidden.append(grad_hidden)
        grad_part = dot(grad_hidden, fc_both, NT).astype(BF16)
        grad_normed = grad_part.astype(F32) + swap_x(grad_part).astype(F32)
        out_parts.append(dot(act, out_both, NT).astype(BF16))
        grad_residual = cots[half].astype(F32) + norm_back(unit, factor, gain_two, grad_normed)
        grad_residuals.append(grad_residual)
        branch = grad_residual.astype(BF16)
        branches.append(branch)
        grad_both = dot(branch, proj_both, NN).astype(BF16)
        mine = grad_both[:, :head_cols]
        received = swap_core(grad_both[:, head_cols:])
        grad_mixed.append(
            jnp.concatenate(
                [jnp.where(is_first, mine, received), jnp.where(is_first, received, mine)], axis=0
            )
        )
        if half == 0:
            vec_two = 0.0
        vec_two = vec_two + jnp.stack(
            [
                jnp.sum(branch.astype(F32), axis=0),
                jnp.sum(cots[half].astype(F32), axis=0),
                jnp.sum(grad_normed * unit, axis=0),
                jnp.sum(grad_normed, axis=0),
            ]
        )

    out_recv = swap_x(pick_x(out_parts[1], out_parts[0]))
    out_mine = pick_x(out_parts[0], out_parts[1])
    outputs = (
        pick_x(residuals[0], residuals[1])
        + out_mine.astype(F32)
        + out_recv.astype(F32)
        + out_shift
    ).astype(BF16)

    act_all = jnp.concatenate(acts, axis=0)
    grad_hidden_all = jnp.concatenate(grads_hidden, axis=0)
    normed_two_all = jnp.concatenate(normed_two, axis=0)
    cot_all = jnp.concatenate(cots, axis=0)
    fc_own = dot(normed_two_all, grad_hidden_all[:, :hidden_cols], TN)
    fc_sib = dot(normed_two_all, grad_hidden_all[:, hidden_cols:], TN).astype(BF16)
    out_own = dot(cot_all, act_all[:, :hidden_cols], TN)
    out_sib = dot(cot_all, act_all[:, hidden_cols:], TN).astype(BF16)
    fc_bias_sums = jnp.sum(grad_hidden_all.astype(F32), axis=0)
    grad_mlp = jnp.concatenate(
        [
            (fc_own + swap_core(fc_sib).astype(F32)).astype(BF16),
            (out_own + swap_core(out_sib).astype(F32)).astype(BF16),
        ],
        axis=1,
    )
    mlp_sum = lax.psum_scatter(grad_mlp, "dp", scatter_dimension=0, tiled=True)

    before = attend_back(qkv, mixed[0], grad_mixed[0], totals[0], None, 0, rows)
    grad_qkv = attend_back(qkv, mixed[1], grad_mixed[1], totals[1], before, 2 * rows, rows)

    branch_all = jnp.concatenate(branches, axis=0)
    mixed_all = jnp.concatenate(mixed_rows, axis=0)
    proj_grad = dot(branch_all, mixed_all, TN)
    proj_grad = proj_grad[:, :head_cols] + swap_core(
        proj_grad[:, head_cols:].astype(BF16)
    ).astype(F32)

    blocks = grad_qkv.reshape(2, 2, rows, qkv_cols)
    block_mine = jnp.where(is_first, blocks[:, 0], blocks[:, 1]).reshape(2 * rows, qkv_cols)
    block_sent = jnp.where(is_first, blocks[:, 1], blocks[:, 0]).reshape(2 * rows, qkv_cols)
    block_recv = swap_core(block_sent)
    z_part = dot(block_mine, attn_all[:, :qkv_cols], NT) + dot(
        block_recv, attn_sib[:, :qkv_cols], NT
    )
    z_low, z_high = z_part[:rows], z_part[rows:]
    z_recv = swap_x(pick_x(z_high, z_low).astype(BF16))
    unit_low, factor_low = normalize(input_low.astype(F32))
    unit_high, factor_high = normalize(input_high.astype(F32))
    vec_one = jnp.stack(
        [
            jnp.sum(z_low * unit_low, axis=0) + jnp.sum(z_high * unit_high, axis=0),
            jnp.sum(z_low, axis=0) + jnp.sum(z_high, axis=0),
        ]
    )
    qkv_grad = dot(normed_one, grad_qkv, TN)
    bias_sums = jnp.sum(grad_qkv.astype(F32), axis=0).reshape(pairs, 3, PAIR)
    qv_sums = jnp.stack([bias_sums[:, 0].reshape(-1), bias_sums[:, 2].reshape(-1)])
    qv_sums = qv_sums.reshape(2, parts, share // 4).transpose(1, 0, 2).reshape(parts, share // 2)
    qv_sums = jnp.pad(qv_sums, ((0, 0), (0, share - share // 2))).reshape(-1)
    fc_bias_grad = fc_bias_sums[:hidden_cols] + swap_core(fc_bias_sums[hidden_cols:])
    vec_grads = jnp.concatenate(
        [0.5 * vec_two[:2], vec_one, 0.5 * vec_two[2:], fc_bias_grad[None], qv_sums[None]], axis=0
    ).T
    grad_attn = jnp.concatenate(
        [
            qkv_grad.astype(BF16),
            proj_grad.astype(BF16),
            jnp.pad(vec_grads, ((0, 0), (0, 120))).astype(BF16),
        ],
        axis=1,
    )
    attn_sum = lax.psum_scatter(grad_attn, "dp", scatter_dimension=0, tiled=True)

    unit = pick_x(unit_low, unit_high)
    factor = pick_x(factor_low, factor_high)
    z_own = pick_x(z_low, z_high) + z_recv.astype(F32)
    grad_inputs = (
        pick_x(grad_residuals[0], grad_residuals[1]) + norm_back(unit, factor, gain_one, z_own)
    ).astype(BF16)

    qkv_out = (
        attn_sum[:, :qkv_cols]
        .astype(F32)
        .reshape(share, pairs, 3, PAIR)
        .transpose(2, 0, 1, 3)
        .reshape(3, share, head_cols)
    )
    proj_out = attn_sum[:, qkv_cols : qkv_cols + head_cols].astype(F32).T
    sums = attn_sum[:, qkv_cols + head_cols : qkv_cols + head_cols + 8].astype(F32).T
    six = lax.psum(sums[:6], "tensor")
    qv_out = sums[7][: share // 2].reshape(2, share // 4)
    fc_out = mlp_sum[:, :hidden_cols].astype(F32)
    out_out = mlp_sum[:, hidden_cols:].astype(F32).T
    return (
        outputs,
        grad_inputs,
        qkv_out,
        qv_out,
        proj_out,
        six[0],
        fc_out,
        sums[6],
        out_out,
        six[1],
        six[2],
        six[3],
        six[4],
        six[5],
    )


def solution(mesh):
    rows = P(("dp", "tensor"), None)
    vector = P("dp")
    wide = P(("tensor", "dp"))
    weights = (
        P(None, "dp", "tensor"),
        P(None, ("tensor", "dp")),
        P("tensor", "dp"),
        vector,
        P("dp", "tensor"),
        wide,
        P("tensor", "dp"),
        vector,
        vector,
        vector,
        vector,
        vector,
    )
    return jax.shard_map(
        local,
        mesh=mesh,
        in_specs=(rows, *weights, rows),
        out_specs=(rows, rows, *weights),
        check_vma=False,
    )
```

```python
import functools

import jax
import jax.numpy as jnp
from jax import lax
from jax.experimental import pallas as pl
from jax.experimental.pallas import tpu as pltpu
from jax.sharding import PartitionSpec as P

HD = 64
PAIR = 2 * HD
EPSILON = 1e-05
NEGATIVE = -1e30
ROOT_TWO_PI = 0.7978845608028654
F32 = jnp.float32
BF16 = jnp.bfloat16
VMEM_LIMIT = 40 * 1024 * 1024


def swap_x(value):
    return lax.ppermute(value, "tensor", [(0, 2), (2, 0), (1, 3), (3, 1)])


def swap_core(value):
    return lax.ppermute(value, "tensor", [(0, 1), (1, 0), (2, 3), (3, 2)])


def dot(a, b, contract, kind=F32):
    return lax.dot_general(a, b, (contract, ((), ())), preferred_element_type=kind)


NN = ((1,), (0,))
NT = ((1,), (1,))
TN = ((0,), (0,))


def normalize(values):
    average = jnp.mean(values, axis=-1, keepdims=True)
    centered = values - average
    spread = jnp.mean(centered * centered, axis=-1, keepdims=True)
    factor = lax.rsqrt(spread + EPSILON)
    return centered * factor, factor


def norm_back(unit, factor, gain, grad):
    scaled = grad * gain
    return factor * (
        scaled
        - jnp.mean(scaled, axis=-1, keepdims=True)
        - unit * jnp.mean(scaled * unit, axis=-1, keepdims=True)
    )


def gelu_both(values):
    squared = values * values
    bent = jnp.tanh(ROOT_TWO_PI * values * (1.0 + 0.044715 * squared))
    half = 0.5 * (1.0 + bent)
    slope = half + 0.5 * values * (1.0 - bent * bent) * ROOT_TWO_PI * (
        1.0 + 3.0 * 0.044715 * squared
    )
    return values * half, slope


def split_heads(block):
    first = lax.broadcasted_iota(jnp.int32, block.shape, 1) < HD
    return [jnp.where(first, block, 0.0).astype(BF16), jnp.where(first, 0.0, block).astype(BF16)]


def attend_kernel(qkv_ref, *rest, row0, block):
    mixed_ref, total_ref, kept, acc = rest[-4:]
    count = mixed_ref.shape[0] // block
    first = lax.broadcasted_iota(jnp.int32, (PAIR, block), 0) < HD
    causal = lax.broadcasted_iota(jnp.int32, (block, block), 0) <= lax.broadcasted_iota(
        jnp.int32, (block, block), 1
    )
    for i in range(count):
        start = row0 + i * block
        heads = split_heads(qkv_ref[pl.ds(start, block), 0:PAIR].astype(F32) * (HD**-0.5))
        keys = qkv_ref[pl.ds(start, block), PAIR : 2 * PAIR]
        tops = []
        for h in range(2):
            scores = jnp.where(causal, dot(keys, heads[h], NT), NEGATIVE)
            kept[h, pl.ds(start, block), :] = scores
            tops.append(jnp.max(scores, axis=0, keepdims=True))

        def score_step(j, tops):
            at = pl.multiple_of(j * block, block)
            tile_keys = qkv_ref[pl.ds(at, block), PAIR : 2 * PAIR]
            found = []
            for h in range(2):
                scores = dot(tile_keys, heads[h], NT)
                kept[h, pl.ds(at, block), :] = scores
                found.append(jnp.maximum(tops[h], jnp.max(scores, axis=0, keepdims=True)))
            return tuple(found)

        tops = lax.fori_loop(0, start // block, score_step, tuple(tops))
        acc[...] = jnp.zeros(acc.shape, F32)

        def value_step(j, sums):
            at = pl.multiple_of(j * block, block)
            tile_values = qkv_ref[pl.ds(at, block), 2 * PAIR : 3 * PAIR]
            found = []
            for h in range(2):
                powers = jnp.exp(kept[h, pl.ds(at, block), :] - tops[h])
                found.append(sums[h] + jnp.sum(powers, axis=0, keepdims=True))
                acc[h] += dot(powers.astype(BF16), tile_values, TN)
            return tuple(found)

        zero = jnp.zeros((1, block), F32)
        sums = lax.fori_loop(0, start // block + 1, value_step, (zero, zero))
        inverse = jnp.transpose(jnp.where(first, 1.0 / sums[0], 1.0 / sums[1]))
        lane = lax.broadcasted_iota(jnp.int32, (block, PAIR), 1) < HD
        local = slice(i * block, (i + 1) * block)
        mixed_ref[local, :] = (jnp.where(lane, acc[0], acc[1]) * inverse).astype(BF16)
        for h in range(2):
            total_ref[0, h : h + 1, local] = tops[h] + jnp.log(sums[h])


def attend(qkv, row0, rows, block, after=()):
    pairs = qkv.shape[1] // (3 * PAIR)
    return pl.pallas_call(
        functools.partial(attend_kernel, row0=row0, block=block),
        grid=(pairs,),
        in_specs=[pl.BlockSpec((row0 + rows, 3 * PAIR), lambda j: (0, j))]
        + [pl.BlockSpec(memory_space=pl.ANY)] * len(after),
        out_specs=[
            pl.BlockSpec((rows, PAIR), lambda j: (0, j)),
            pl.BlockSpec((1, 2, rows), lambda j: (j, 0, 0)),
        ],
        out_shape=[
            jax.ShapeDtypeStruct((rows, pairs * PAIR), BF16),
            jax.ShapeDtypeStruct((pairs, 2, rows), F32),
        ],
        scratch_shapes=[
            pltpu.VMEM((2, row0 + rows, block), F32),
            pltpu.VMEM((2, block, PAIR), F32),
        ],
        compiler_params=pltpu.CompilerParams(vmem_limit_bytes=VMEM_LIMIT),
        name="attend_%d" % row0,
    )(qkv, *after)


def attend_back_kernel(
    qkv_ref, mixed_ref, grad_ref, total_ref, *rest, row0, block, has_before
):
    before_ref = rest[0]
    out_ref, sums_ref, key_acc, value_acc, query_acc = rest[-5:]
    rows = mixed_ref.shape[0]
    count = rows // block
    lane = lax.broadcasted_iota(jnp.int32, (block, PAIR), 1)
    first = lane < HD
    causal = lax.broadcasted_iota(jnp.int32, (block, block), 0) <= lax.broadcasted_iota(
        jnp.int32, (block, block), 1
    )
    if has_before:
        key_acc[0:row0, :] = before_ref[:, PAIR : 2 * PAIR]
        value_acc[0:row0, :] = before_ref[:, 2 * PAIR : 3 * PAIR]
        key_acc[row0:, :] = jnp.zeros((rows, PAIR), F32)
        value_acc[row0:, :] = jnp.zeros((rows, PAIR), F32)
    else:
        key_acc[...] = jnp.zeros(key_acc.shape, F32)
        value_acc[...] = jnp.zeros(value_acc.shape, F32)
    for i in range(count):
        start = row0 + i * block
        local = slice(i * block, (i + 1) * block)
        query_heads = split_heads(
            qkv_ref[pl.ds(start, block), 0:PAIR].astype(F32) * (HD**-0.5)
        )
        grads = grad_ref[local, :].astype(F32)
        grad_heads = split_heads(grads)
        inner = jnp.transpose(grads * mixed_ref[local, :].astype(F32))
        total_rows = [total_ref[0, h : h + 1, local] for h in range(2)]
        inner_rows = [
            jnp.sum(inner[h * HD : (h + 1) * HD, :], axis=0, keepdims=True) for h in range(2)
        ]

        def tile(at, masked):
            tile_keys = qkv_ref[pl.ds(at, block), PAIR : 2 * PAIR]
            tile_values = qkv_ref[pl.ds(at, block), 2 * PAIR : 3 * PAIR]
            key_sum, value_sum = None, None
            for h in range(2):
                scores = dot(tile_keys, query_heads[h], NT)
                weights = jnp.exp(scores - total_rows[h])
                if masked:
                    weights = jnp.where(causal, weights, 0.0)
                grad_weights = dot(tile_values, grad_heads[h], NT)
                grad_scores = (weights * (grad_weights - inner_rows[h])).astype(BF16)
                value_part = dot(weights.astype(BF16), grad_heads[h], NN)
                key_part = dot(grad_scores, query_heads[h], NN)
                query_part = dot(grad_scores, tile_keys, TN)
                key_sum = key_part if key_sum is None else key_sum + key_part
                value_sum = value_part if value_sum is None else value_sum + value_part
                if masked:
                    query_acc[h] = query_part
                else:
                    query_acc[h] += query_part
            key_acc[pl.ds(at, block), :] += key_sum
            value_acc[pl.ds(at, block), :] += value_sum

        tile(start, True)

        def step(j, carry):
            tile(pl.multiple_of(j * block, block), False)
            return carry

        if start:
            lax.fori_loop(0, start // block, step, 0)
        query_grad = jnp.where(first, query_acc[0], query_acc[1]) * (HD**-0.5)
        out_ref[start : start + block, 0:PAIR] = query_grad.astype(out_ref.dtype)
    if has_before:
        out_ref[0:row0, 0:PAIR] = before_ref[:, 0:PAIR].astype(out_ref.dtype)
    out_ref[:, PAIR : 2 * PAIR] = key_acc[...].astype(out_ref.dtype)
    out_ref[:, 2 * PAIR : 3 * PAIR] = value_acc[...].astype(out_ref.dtype)
    sums_ref[...] = jnp.sum(out_ref[...].astype(F32), axis=0, keepdims=True)


def attend_back(qkv, mixed, grads, totals, before, row0, block, after=()):
    pairs = qkv.shape[1] // (3 * PAIR)
    rows = mixed.shape[0]
    extent = row0 + rows
    narrow = pl.BlockSpec((rows, PAIR), lambda j: (0, j))
    in_specs = [
        pl.BlockSpec((extent, 3 * PAIR), lambda j: (0, j)),
        narrow,
        narrow,
        pl.BlockSpec((1, 2, rows), lambda j: (j, 0, 0)),
    ]
    operands = [qkv, mixed, grads, totals]
    if before is not None:
        in_specs.append(pl.BlockSpec((row0, 3 * PAIR), lambda j: (0, j)))
        operands.append(before)
    in_specs += [pl.BlockSpec(memory_space=pl.ANY)] * len(after)
    return pl.pallas_call(
        functools.partial(
            attend_back_kernel, row0=row0, block=block, has_before=before is not None
        ),
        grid=(pairs,),
        in_specs=in_specs,
        out_specs=[
            pl.BlockSpec((extent, 3 * PAIR), lambda j: (0, j)),
            pl.BlockSpec((1, 3 * PAIR), lambda j: (0, j)),
        ],
        out_shape=[
            jax.ShapeDtypeStruct((extent, pairs * 3 * PAIR), F32 if before is None else BF16),
            jax.ShapeDtypeStruct((1, pairs * 3 * PAIR), F32),
        ],
        scratch_shapes=[
            pltpu.VMEM((extent, PAIR), F32),
            pltpu.VMEM((extent, PAIR), F32),
            pltpu.VMEM((2, block, PAIR), F32),
        ],
        compiler_params=pltpu.CompilerParams(vmem_limit_bytes=VMEM_LIMIT),
        name="attend_back_%d" % row0,
    )(*operands, *after)


def project_kernel(rows_ref, vec_ref, shift_ref, weight_ref, normed_ref, out_ref):
    unit, _ = normalize(rows_ref[...].astype(F32))
    normed_ref[...] = (unit * vec_ref[2:3, :] + vec_ref[3:4, :]).astype(BF16)
    out_ref[...] = (dot(normed_ref[...], weight_ref[...], NN) + shift_ref[...]).astype(BF16)


def project(sequence, vectors, shift, weights, block):
    length, width = sequence.shape
    cols = shift.shape[1]
    return pl.pallas_call(
        project_kernel,
        grid=(length // block,),
        in_specs=[
            pl.BlockSpec((block, width), lambda i: (i, 0)),
            pl.BlockSpec(vectors.shape, lambda i: (0, 0)),
            pl.BlockSpec(shift.shape, lambda i: (0, 0)),
            pl.BlockSpec((width, cols), lambda i: (0, 0)),
        ],
        out_specs=[
            pl.BlockSpec((block, width), lambda i: (i, 0)),
            pl.BlockSpec((block, cols), lambda i: (i, 0)),
        ],
        out_shape=[
            jax.ShapeDtypeStruct((length, width), BF16),
            jax.ShapeDtypeStruct((length, cols), BF16),
        ],
        compiler_params=pltpu.CompilerParams(vmem_limit_bytes=VMEM_LIMIT),
        name="project",
    )(sequence, vectors, shift, weights)


def feed_kernel(
    base_ref,
    part_ref,
    recv_ref,
    cot_ref,
    vec_ref,
    shift_own_ref,
    shift_sib_ref,
    fc_own_ref,
    out_own_ref,
    fc_sib_ref,
    out_sib_ref,
    *rest,
    tiles,
):
    residual_ref, normed_ref, act_ref, grad_ref, back_ref, sent_ref, sums_ref = rest[-9:-2]
    back_acc, out_acc = rest[-2:]
    i = pl.program_id(0)
    rows = base_ref.shape[0]

    @pl.when(i == 0)
    def _():
        residual = (
            base_ref[...].astype(F32)
            + part_ref[...].astype(F32)
            + recv_ref[...].astype(F32)
            + vec_ref[0:1, :]
        )
        residual_ref[...] = residual
        unit, _ = normalize(residual)
        normed_ref[...] = (unit * vec_ref[4:5, :] + vec_ref[5:6, :]).astype(BF16)
        back_acc[...] = jnp.zeros(back_acc.shape, F32)
        out_acc[...] = jnp.zeros(out_acc.shape, F32)

    def work(shift_ref, fc_ref, out_ref):
        step = rows // 2
        total = None
        for r in range(2):
            at = slice(r * step, (r + 1) * step)
            hidden = dot(normed_ref[at, :], fc_ref[...], NN) + shift_ref[...]
            grad_act = dot(cot_ref[at, :], out_ref[...], NN)
            act, slope = gelu_both(hidden)
            act = act.astype(BF16)
            grad = (grad_act * slope).astype(BF16)
            act_ref[at, :] = act
            grad_ref[at, :] = grad
            part = jnp.sum(grad.astype(F32), axis=0, keepdims=True)
            total = part if total is None else total + part
            back_acc[at, :] += dot(grad, fc_ref[...], NT)
            out_acc[at, :] += dot(act, out_ref[...], NT)
        sums_ref[...] = total

    @pl.when(i < tiles)
    def _():
        work(shift_own_ref, fc_own_ref, out_own_ref)

    @pl.when(i >= tiles)
    def _():
        work(shift_sib_ref, fc_sib_ref, out_sib_ref)

    @pl.when(i == 2 * tiles - 1)
    def _():
        back_ref[...] = back_acc[...].astype(BF16)
        sent_ref[...] = out_acc[...].astype(BF16)


def feed(base, part, recv, cot, vectors, shift_own, shift_sib, own, sib, after=()):
    rows, width = base.shape
    hidden_cols = shift_own.shape[1]
    tile = min(512, hidden_cols)
    tiles = hidden_cols // tile
    whole = pl.BlockSpec((rows, width), lambda i: (0, 0))

    def low(i):
        return jnp.minimum(i, tiles - 1)

    def high(i):
        return jnp.maximum(i - tiles, 0)

    return pl.pallas_call(
        functools.partial(feed_kernel, tiles=tiles),
        grid=(2 * tiles,),
        in_specs=[
            whole,
            whole,
            whole,
            whole,
            pl.BlockSpec(vectors.shape, lambda i: (0, 0)),
            pl.BlockSpec((1, tile), lambda i: (0, low(i))),
            pl.BlockSpec((1, tile), lambda i: (0, high(i))),
            pl.BlockSpec((width, tile), lambda i: (0, low(i))),
            pl.BlockSpec((width, tile), lambda i: (0, tiles + low(i))),
            pl.BlockSpec((width, tile), lambda i: (0, high(i))),
            pl.BlockSpec((width, tile), lambda i: (0, tiles + high(i))),
        ]
        + [pl.BlockSpec(memory_space=pl.ANY)] * len(after),
        out_specs=[
            whole,
            whole,
            pl.BlockSpec((rows, tile), lambda i: (0, i)),
            pl.BlockSpec((rows, tile), lambda i: (0, i)),
            whole,
            whole,
            pl.BlockSpec((1, tile), lambda i: (0, i)),
        ],
        out_shape=[
            jax.ShapeDtypeStruct((rows, width), F32),
            jax.ShapeDtypeStruct((rows, width), BF16),
            jax.ShapeDtypeStruct((rows, 2 * hidden_cols), BF16),
            jax.ShapeDtypeStruct((rows, 2 * hidden_cols), BF16),
            jax.ShapeDtypeStruct((rows, width), BF16),
            jax.ShapeDtypeStruct((rows, width), BF16),
            jax.ShapeDtypeStruct((1, 2 * hidden_cols), F32),
        ],
        scratch_shapes=[pltpu.VMEM((rows, width), F32), pltpu.VMEM((rows, width), F32)],
        compiler_params=pltpu.CompilerParams(vmem_limit_bytes=VMEM_LIMIT),
        name="feed",
    )(
        base, part, recv, cot, vectors, shift_own, shift_sib, own, own, sib, sib, *after
    )


def swap_dp(value, mask):
    size = lax.axis_size("dp")
    return lax.ppermute(value, "dp", [(i, i ^ mask) for i in range(size)])


def gather_dp(shard):
    size = lax.axis_size("dp")
    if size != 8:
        return lax.all_gather(shard, "dp", axis=0, tiled=True)
    me = lax.axis_index("dp")
    pieces = {0: shard}
    for k in (6, 4, 2):
        pieces[k] = swap_dp(shard, k)
    for k in (0, 2, 4, 6):
        pieces[k + 1] = swap_dp(pieces[k], 1)
    full = jnp.zeros((size,) + shard.shape, shard.dtype)
    for k in (0, 1, 2, 3, 4, 5, 6, 7):
        full = lax.dynamic_update_index_in_dim(full, pieces[k], me ^ k, 0)
    return full.reshape((size * shard.shape[0],) + shard.shape[1:])


def scatter_dp(blocks, kind):
    size = blocks.shape[0]
    if size != 8:
        return lax.psum_scatter(blocks.astype(kind), "dp", scatter_dimension=0).astype(F32)
    me = lax.axis_index("dp")

    def block(k):
        return lax.dynamic_index_in_dim(blocks, me ^ k, 0, keepdims=False)

    sums = {}
    for k in (6, 4, 2, 0):
        received = swap_dp(block(k + 1).astype(kind), 1)
        sums[k] = block(k).astype(F32) + received.astype(F32)
    result = sums[0]
    for k in (6, 4, 2):
        result = result + swap_dp(sums[k].astype(kind), k).astype(F32)
    return result


def local(
    inputs,
    qkv_weight,
    qv_bias,
    proj_weight,
    proj_bias,
    fc_weight,
    fc_bias,
    out_weight,
    out_bias,
    attn_norm_gain,
    attn_norm_bias,
    mlp_norm_gain,
    mlp_norm_bias,
    cotangent,
):
    width = inputs.shape[1]
    rows = inputs.shape[0]
    share = proj_bias.shape[0]
    parts = width // share
    head_cols = qkv_weight.shape[2]
    pairs = head_cols // PAIR
    qkv_cols = 3 * head_cols
    hidden_cols = fc_weight.shape[1]
    place = lax.axis_index("tensor")
    core = place % 2
    is_low = place < 2
    is_first = core == 0

    def pick_x(low, high):
        return jnp.where(is_low, low, high)

    qv_column = jnp.pad(qv_bias.reshape(-1), (0, share - qv_bias.size))
    vectors = jnp.stack(
        [
            proj_bias,
            out_bias,
            attn_norm_gain,
            attn_norm_bias,
            mlp_norm_gain,
            mlp_norm_bias,
            fc_bias,
            qv_column,
        ],
        axis=1,
    )
    qkv_shard = jnp.transpose(
        qkv_weight.reshape(3, share, pairs, PAIR), (1, 2, 0, 3)
    ).reshape(share, qkv_cols)
    attn_shard = jnp.concatenate(
        [qkv_shard, proj_weight.T, jnp.pad(vectors, ((0, 0), (0, 120)))], axis=1
    )
    attn_all = gather_dp(attn_shard)
    mlp_shard = jnp.concatenate([fc_weight, out_weight.T], axis=1)
    mlp_all = lax.all_gather(mlp_shard, "dp", axis=0, tiled=True)

    input_x = swap_x(inputs)
    input_core = swap_core(inputs)
    input_far = swap_core(input_x)
    input_low, input_high = pick_x(inputs, input_x), pick_x(input_x, inputs)
    far_low, far_high = pick_x(input_core, input_far), pick_x(input_far, input_core)
    cot_x = swap_x(cotangent)
    cots = [pick_x(cotangent, cot_x), pick_x(cot_x, cotangent)]
    sequence = jnp.concatenate(
        [
            jnp.where(is_first, input_low, far_low),
            jnp.where(is_first, far_low, input_low),
            jnp.where(is_first, input_high, far_high),
            jnp.where(is_first, far_high, input_high),
        ],
        axis=0,
    )

    attn_sib = swap_core(attn_all)
    columns = attn_all[:, qkv_cols + head_cols : qkv_cols + head_cols + 8].astype(F32).T
    out_shift, gain_one, gain_two = columns[1:2], columns[2:3], columns[4:5]
    fc_shift_own = columns[6:7]
    fc_shift_sib = attn_sib[:, qkv_cols + head_cols + 6].astype(F32)[None, :]
    qv_shift = (
        columns[7]
        .reshape(parts, share)[:, : share // 2]
        .reshape(parts, 2, share // 4)
        .transpose(1, 0, 2)
        .reshape(2, head_cols)
    )
    qkv_shift = jnp.stack([qv_shift[0], jnp.zeros_like(qv_shift[0]), qv_shift[1]])
    qkv_shift = qkv_shift.reshape(3, pairs, PAIR).transpose(1, 0, 2).reshape(1, qkv_cols)
    proj_both = jnp.concatenate(
        [
            attn_all[:, qkv_cols : qkv_cols + head_cols],
            attn_sib[:, qkv_cols : qkv_cols + head_cols],
        ],
        axis=1,
    )

    normed_one, qkv = project(sequence, columns, qkv_shift, attn_all, rows)
    mlp_sib = swap_core(mlp_all)

    inputs_two = [input_low, input_high]
    mixed, totals, mixed_rows, parts_two, received_two = [], [], [], [], []
    for half in range(2):
        half_mixed, half_totals = attend(
            qkv, half * 2 * rows, 2 * rows, rows, after=tuple(parts_two)
        )
        mixed.append(half_mixed)
        totals.append(half_totals)
        two = half_mixed.reshape(2, rows, head_cols)
        mine = jnp.where(is_first, two[0], two[1])
        received = swap_core(jnp.where(is_first, two[1], two[0]))
        both = jnp.concatenate([mine, received], axis=1)
        mixed_rows.append(both)
        part = dot(both, proj_both, NT).astype(BF16)
        parts_two.append(part)
        received_two.append(swap_x(part))
    residuals, normed_two, acts, grads_hidden, backs, out_parts = [], [], [], [], [], []
    fc_bias_sums = 0.0
    for half in range(2):
        residual, normed, act, grad_hidden, back, out_part, sums = feed(
            inputs_two[half],
            parts_two[half],
            received_two[half],
            cots[half],
            columns,
            fc_shift_own,
            fc_shift_sib,
            mlp_all,
            mlp_sib,
            after=(parts_two[1],),
        )
        residuals.append(residual)
        normed_two.append(normed)
        acts.append(act)
        grads_hidden.append(grad_hidden)
        backs.append(back)
        out_parts.append(out_part)
        fc_bias_sums = fc_bias_sums + sums[0]
    back_recv = [swap_x(back) for back in backs]

    act_all = jnp.concatenate(acts, axis=0)
    grad_hidden_all = jnp.concatenate(grads_hidden, axis=0)
    normed_two_all = jnp.concatenate(normed_two, axis=0)
    cot_all = jnp.concatenate(cots, axis=0)
    fc_sib = dot(normed_two_all, grad_hidden_all[:, hidden_cols:], TN).astype(BF16)
    fc_recv = swap_core(fc_sib)
    out_sib = dot(cot_all, act_all[:, hidden_cols:], TN).astype(BF16)
    out_recv = swap_core(out_sib)
    fc_own = dot(normed_two_all, grad_hidden_all[:, :hidden_cols], TN)
    out_own = dot(cot_all, act_all[:, :hidden_cols], TN)
    grad_mlp = jnp.concatenate(
        [
            (fc_own + fc_recv.astype(F32)).astype(BF16),
            (out_own + out_recv.astype(F32)).astype(BF16),
        ],
        axis=1,
    )
    mlp_sum = lax.psum_scatter(grad_mlp, "dp", scatter_dimension=0, tiled=True)

    grad_residuals, branches = [], []
    vec_two = 0.0
    before = None
    for half in range(2):
        grad_normed = backs[half].astype(F32) + back_recv[half].astype(F32)
        unit, factor = normalize(residuals[half])
        grad_residual = cots[half].astype(F32) + norm_back(unit, factor, gain_two, grad_normed)
        grad_residuals.append(grad_residual)
        branch = grad_residual.astype(BF16)
        branches.append(branch)
        grad_both = dot(branch, proj_both, NN).astype(BF16)
        mine = grad_both[:, :head_cols]
        received = swap_core(grad_both[:, head_cols:])
        grad_mixed = jnp.concatenate(
            [jnp.where(is_first, mine, received), jnp.where(is_first, received, mine)], axis=0
        )
        vec_two = vec_two + jnp.stack(
            [
                jnp.sum(branch.astype(F32), axis=0),
                jnp.sum(cots[half].astype(F32), axis=0),
                jnp.sum(grad_normed * unit, axis=0),
                jnp.sum(grad_normed, axis=0),
            ]
        )
        before, qkv_sums = attend_back(
            qkv,
            mixed[half],
            grad_mixed,
            totals[half],
            before,
            half * 2 * rows,
            rows,
            after=(grad_mlp,),
        )
    grad_qkv = before

    out_sent, _ = lax.optimization_barrier((pick_x(out_parts[1], out_parts[0]), back_recv[1]))
    out_recv = swap_x(out_sent)
    out_mine = pick_x(out_parts[0], out_parts[1])
    outputs = (
        pick_x(residuals[0], residuals[1])
        + out_mine.astype(F32)
        + out_recv.astype(F32)
        + out_shift
    ).astype(BF16)

    branch_all = jnp.concatenate(branches, axis=0)
    mixed_all = jnp.concatenate(mixed_rows, axis=0)
    proj_grad = dot(branch_all, mixed_all, TN)
    proj_grad = proj_grad[:, :head_cols] + swap_core(
        proj_grad[:, head_cols:].astype(BF16)
    ).astype(F32)

    blocks = grad_qkv.reshape(2, 2, rows, qkv_cols)
    block_mine = jnp.where(is_first, blocks[:, 0], blocks[:, 1]).reshape(2 * rows, qkv_cols)
    block_sent = jnp.where(is_first, blocks[:, 1], blocks[:, 0]).reshape(2 * rows, qkv_cols)
    block_recv = swap_core(block_sent)
    z_part = dot(block_mine, attn_all[:, :qkv_cols], NT) + dot(
        block_recv, attn_sib[:, :qkv_cols], NT
    )
    z_low, z_high = z_part[:rows], z_part[rows:]
    z_recv = swap_x(pick_x(z_high, z_low).astype(BF16))
    unit_low, factor_low = normalize(input_low.astype(F32))
    unit_high, factor_high = normalize(input_high.astype(F32))
    vec_one = jnp.stack(
        [
            jnp.sum(z_low * unit_low, axis=0) + jnp.sum(z_high * unit_high, axis=0),
            jnp.sum(z_low, axis=0) + jnp.sum(z_high, axis=0),
        ]
    )
    qkv_grad = dot(normed_one, grad_qkv, TN)
    bias_sums = qkv_sums.reshape(pairs, 3, PAIR)
    qv_sums = jnp.stack([bias_sums[:, 0].reshape(-1), bias_sums[:, 2].reshape(-1)])
    qv_sums = qv_sums.reshape(2, parts, share // 4).transpose(1, 0, 2).reshape(parts, share // 2)
    qv_sums = jnp.pad(qv_sums, ((0, 0), (0, share - share // 2))).reshape(-1)
    fc_bias_grad = fc_bias_sums[:hidden_cols] + swap_core(fc_bias_sums[hidden_cols:])
    vec_grads = jnp.concatenate(
        [0.5 * vec_two[:2], vec_one, 0.5 * vec_two[2:], fc_bias_grad[None], qv_sums[None]], axis=0
    )
    grad_attn = jnp.concatenate([qkv_grad.astype(BF16), proj_grad.astype(BF16)], axis=1)
    attn_sum = scatter_dp(grad_attn.reshape(parts, share, -1), BF16)
    sums = scatter_dp(vec_grads.reshape(8, parts, share).transpose(1, 0, 2), F32)

    unit = pick_x(unit_low, unit_high)
    factor = pick_x(factor_low, factor_high)
    z_own = pick_x(z_low, z_high) + z_recv.astype(F32)
    grad_inputs = (
        pick_x(grad_residuals[0], grad_residuals[1]) + norm_back(unit, factor, gain_one, z_own)
    ).astype(BF16)

    qkv_out = (
        attn_sum[:, :qkv_cols]
        .reshape(share, pairs, 3, PAIR)
        .transpose(2, 0, 1, 3)
        .reshape(3, share, head_cols)
    )
    proj_out = attn_sum[:, qkv_cols:].T
    six = lax.psum(sums[:6], "tensor")
    qv_out = sums[7][: share // 2].reshape(2, share // 4)
    fc_out = mlp_sum[:, :hidden_cols].astype(F32)
    out_out = mlp_sum[:, hidden_cols:].astype(F32).T
    return (
        outputs,
        grad_inputs,
        qkv_out,
        qv_out,
        proj_out,
        six[0],
        fc_out,
        sums[6],
        out_out,
        six[1],
        six[2],
        six[3],
        six[4],
        six[5],
    )


def solution(mesh):
    rows = P(("dp", "tensor"), None)
    vector = P("dp")
    wide = P(("tensor", "dp"))
    weights = (
        P(None, "dp", "tensor"),
        P(None, ("tensor", "dp")),
        P("tensor", "dp"),
        vector,
        P("dp", "tensor"),
        wide,
        P("tensor", "dp"),
        vector,
        vector,
        vector,
        vector,
        vector,
    )
    return jax.shard_map(
        local,
        mesh=mesh,
        in_specs=(rows, *weights, rows),
        out_specs=(rows, rows, *weights),
        check_vma=False,
    )
```

```python
import functools

import jax
import jax.numpy as jnp
from jax import lax
from jax.experimental import pallas as pl
from jax.experimental.pallas import tpu as pltpu
from jax.sharding import PartitionSpec as P

HD = 64
PAIR = 2 * HD
EPSILON = 1e-05
NEGATIVE = -1e30
ROOT_TWO_PI = 0.7978845608028654
F32 = jnp.float32
BF16 = jnp.bfloat16
MIB = 1024 * 1024
ANY_SPACE = pl.BlockSpec(memory_space=pl.ANY)


def params(mib):
    return pltpu.CompilerParams(vmem_limit_bytes=mib * MIB)


def cost(micros):
    return pl.CostEstimate(
        flops=int(micros * 1.1e9), bytes_accessed=int(micros * 1e6), transcendentals=0
    )


def swap_x(value):
    return lax.ppermute(value, "tensor", [(0, 2), (2, 0), (1, 3), (3, 1)])


def swap_core(value):
    return lax.ppermute(value, "tensor", [(0, 1), (1, 0), (2, 3), (3, 2)])


def dot(a, b, contract, kind=F32):
    return lax.dot_general(a, b, (contract, ((), ())), preferred_element_type=kind)


NN = ((1,), (0,))
NT = ((1,), (1,))
TN = ((0,), (0,))


def normalize(values):
    average = jnp.mean(values, axis=-1, keepdims=True)
    centered = values - average
    spread = jnp.mean(centered * centered, axis=-1, keepdims=True)
    factor = lax.rsqrt(spread + EPSILON)
    return centered * factor, factor


def norm_back(unit, factor, gain, grad):
    scaled = grad * gain
    return factor * (
        scaled
        - jnp.mean(scaled, axis=-1, keepdims=True)
        - unit * jnp.mean(scaled * unit, axis=-1, keepdims=True)
    )


def gelu_both(values):
    squared = values * values
    bent = jnp.tanh(ROOT_TWO_PI * values * (1.0 + 0.044715 * squared))
    half = 0.5 * (1.0 + bent)
    slope = half + 0.5 * values * (1.0 - bent * bent) * ROOT_TWO_PI * (
        1.0 + 3.0 * 0.044715 * squared
    )
    return values * half, slope


def split_heads(block):
    first = lax.broadcasted_iota(jnp.int32, block.shape, 1) < HD
    return [jnp.where(first, block, 0.0).astype(BF16), jnp.where(first, 0.0, block).astype(BF16)]


def attend_kernel(qkv_ref, *rest, row0, block):
    mixed_ref, total_ref, kept, acc = rest[-4:]
    count = mixed_ref.shape[0] // block
    first = lax.broadcasted_iota(jnp.int32, (PAIR, block), 0) < HD
    causal = lax.broadcasted_iota(jnp.int32, (block, block), 0) <= lax.broadcasted_iota(
        jnp.int32, (block, block), 1
    )
    for i in range(count):
        start = row0 + i * block
        heads = split_heads(qkv_ref[pl.ds(start, block), 0:PAIR].astype(F32) * (HD**-0.5))
        keys = qkv_ref[pl.ds(start, block), PAIR : 2 * PAIR]
        tops = []
        for h in range(2):
            scores = jnp.where(causal, dot(keys, heads[h], NT), NEGATIVE)
            kept[h, pl.ds(start, block), :] = scores
            tops.append(jnp.max(scores, axis=0, keepdims=True))

        def score_step(j, tops):
            at = pl.multiple_of(j * block, block)
            tile_keys = qkv_ref[pl.ds(at, block), PAIR : 2 * PAIR]
            found = []
            for h in range(2):
                scores = dot(tile_keys, heads[h], NT)
                kept[h, pl.ds(at, block), :] = scores
                found.append(jnp.maximum(tops[h], jnp.max(scores, axis=0, keepdims=True)))
            return tuple(found)

        tops = lax.fori_loop(0, start // block, score_step, tuple(tops))
        acc[...] = jnp.zeros(acc.shape, F32)

        def value_step(j, sums):
            at = pl.multiple_of(j * block, block)
            tile_values = qkv_ref[pl.ds(at, block), 2 * PAIR : 3 * PAIR]
            found = []
            for h in range(2):
                powers = jnp.exp(kept[h, pl.ds(at, block), :] - tops[h])
                found.append(sums[h] + jnp.sum(powers, axis=0, keepdims=True))
                acc[h] += dot(powers.astype(BF16), tile_values, TN)
            return tuple(found)

        zero = jnp.zeros((1, block), F32)
        sums = lax.fori_loop(0, start // block + 1, value_step, (zero, zero))
        inverse = jnp.transpose(jnp.where(first, 1.0 / sums[0], 1.0 / sums[1]))
        lane = lax.broadcasted_iota(jnp.int32, (block, PAIR), 1) < HD
        local = slice(i * block, (i + 1) * block)
        mixed_ref[local, :] = (jnp.where(lane, acc[0], acc[1]) * inverse).astype(BF16)
        for h in range(2):
            total_ref[0, h : h + 1, local] = tops[h] + jnp.log(sums[h])


def attend(qkv, row0, rows, block, after=()):
    pairs = qkv.shape[1] // (3 * PAIR)
    return pl.pallas_call(
        functools.partial(attend_kernel, row0=row0, block=block),
        grid=(pairs,),
        in_specs=[pl.BlockSpec((row0 + rows, 3 * PAIR), lambda j: (0, j))]
        + [ANY_SPACE] * len(after),
        out_specs=[
            pl.BlockSpec((rows, PAIR), lambda j: (0, j)),
            pl.BlockSpec((1, 2, rows), lambda j: (j, 0, 0)),
        ],
        out_shape=[
            jax.ShapeDtypeStruct((rows, pairs * PAIR), BF16),
            jax.ShapeDtypeStruct((pairs, 2, rows), F32),
        ],
        scratch_shapes=[
            pltpu.VMEM((2, row0 + rows, block), F32),
            pltpu.VMEM((2, block, PAIR), F32),
        ],
        compiler_params=params(24),
        cost_estimate=cost(16 if row0 else 6),
        name="attend_%d" % row0,
    )(qkv, *after)


def attend_back_kernel(
    qkv_ref, mixed_ref, grad_ref, total_ref, *rest, row0, block, has_before
):
    before_ref = rest[0]
    out_ref, sums_ref, key_acc, value_acc, query_acc = rest[-5:]
    rows = mixed_ref.shape[0]
    count = rows // block
    lane = lax.broadcasted_iota(jnp.int32, (block, PAIR), 1)
    first = lane < HD
    causal = lax.broadcasted_iota(jnp.int32, (block, block), 0) <= lax.broadcasted_iota(
        jnp.int32, (block, block), 1
    )
    if has_before:
        key_acc[0:row0, :] = before_ref[:, PAIR : 2 * PAIR]
        value_acc[0:row0, :] = before_ref[:, 2 * PAIR : 3 * PAIR]
        key_acc[row0:, :] = jnp.zeros((rows, PAIR), F32)
        value_acc[row0:, :] = jnp.zeros((rows, PAIR), F32)
    else:
        key_acc[...] = jnp.zeros(key_acc.shape, F32)
        value_acc[...] = jnp.zeros(value_acc.shape, F32)
    for i in range(count):
        start = row0 + i * block
        local = slice(i * block, (i + 1) * block)
        query_heads = split_heads(
            qkv_ref[pl.ds(start, block), 0:PAIR].astype(F32) * (HD**-0.5)
        )
        grads = grad_ref[local, :].astype(F32)
        grad_heads = split_heads(grads)
        inner = jnp.transpose(grads * mixed_ref[local, :].astype(F32))
        total_rows = [total_ref[0, h : h + 1, local] for h in range(2)]
        inner_rows = [
            jnp.sum(inner[h * HD : (h + 1) * HD, :], axis=0, keepdims=True) for h in range(2)
        ]

        def tile(at, masked):
            tile_keys = qkv_ref[pl.ds(at, block), PAIR : 2 * PAIR]
            tile_values = qkv_ref[pl.ds(at, block), 2 * PAIR : 3 * PAIR]
            key_sum, value_sum = None, None
            for h in range(2):
                scores = dot(tile_keys, query_heads[h], NT)
                weights = jnp.exp(scores - total_rows[h])
                if masked:
                    weights = jnp.where(causal, weights, 0.0)
                grad_weights = dot(tile_values, grad_heads[h], NT)
                grad_scores = (weights * (grad_weights - inner_rows[h])).astype(BF16)
                value_part = dot(weights.astype(BF16), grad_heads[h], NN)
                key_part = dot(grad_scores, query_heads[h], NN)
                query_part = dot(grad_scores, tile_keys, TN)
                key_sum = key_part if key_sum is None else key_sum + key_part
                value_sum = value_part if value_sum is None else value_sum + value_part
                if masked:
                    query_acc[h] = query_part
                else:
                    query_acc[h] += query_part
            key_acc[pl.ds(at, block), :] += key_sum
            value_acc[pl.ds(at, block), :] += value_sum

        tile(start, True)

        def step(j, carry):
            tile(pl.multiple_of(j * block, block), False)
            return carry

        if start:
            lax.fori_loop(0, start // block, step, 0)
        query_grad = jnp.where(first, query_acc[0], query_acc[1]) * (HD**-0.5)
        out_ref[start : start + block, 0:PAIR] = query_grad.astype(out_ref.dtype)
    if has_before:
        out_ref[0:row0, 0:PAIR] = before_ref[:, 0:PAIR].astype(out_ref.dtype)
    out_ref[:, PAIR : 2 * PAIR] = key_acc[...].astype(out_ref.dtype)
    out_ref[:, 2 * PAIR : 3 * PAIR] = value_acc[...].astype(out_ref.dtype)
    sums_ref[...] = jnp.sum(out_ref[...].astype(F32), axis=0, keepdims=True)


def attend_back(qkv, mixed, grads, totals, before, row0, block, pair, pairs, after=()):
    rows = mixed.shape[0]
    extent = row0 + rows
    narrow = pl.BlockSpec((rows, PAIR), lambda j: (0, pair + j))
    in_specs = [
        pl.BlockSpec((extent, 3 * PAIR), lambda j: (0, pair + j)),
        narrow,
        narrow,
        pl.BlockSpec((1, 2, rows), lambda j: (pair + j, 0, 0)),
    ]
    operands = [qkv, mixed, grads, totals]
    if before is not None:
        in_specs.append(pl.BlockSpec((row0, 3 * PAIR), lambda j: (0, pair + j)))
        operands.append(before)
    in_specs += [ANY_SPACE] * len(after)
    return pl.pallas_call(
        functools.partial(
            attend_back_kernel, row0=row0, block=block, has_before=before is not None
        ),
        grid=(pairs,),
        in_specs=in_specs,
        out_specs=[
            pl.BlockSpec((extent, 3 * PAIR), lambda j: (0, j)),
            pl.BlockSpec((1, 3 * PAIR), lambda j: (0, j)),
        ],
        out_shape=[
            jax.ShapeDtypeStruct((extent, pairs * 3 * PAIR), F32 if before is None else BF16),
            jax.ShapeDtypeStruct((1, pairs * 3 * PAIR), F32),
        ],
        scratch_shapes=[
            pltpu.VMEM((extent, PAIR), F32),
            pltpu.VMEM((extent, PAIR), F32),
            pltpu.VMEM((2, block, PAIR), F32),
        ],
        compiler_params=params(32),
        cost_estimate=cost(5.5 * pairs if before is None else 13 * pairs),
        name="attend_back_%d_%d" % (row0, pair),
    )(*operands, *after)


def norm_two_kernel(
    back_ref, recv_ref, residual_ref, cot_ref, vec_ref, proj_ref, *rest, steps
):
    grad_ref, branch_ref, both_ref, sums_ref = rest[-4:]
    z = back_ref[...].astype(F32) + recv_ref[...].astype(F32)
    unit, factor = normalize(residual_ref[...])
    cot = cot_ref[...].astype(F32)
    grad = cot + norm_back(unit, factor, vec_ref[4:5, :], z)
    grad_ref[...] = grad
    branch = grad.astype(BF16)
    branch_ref[...] = branch
    both_ref[...] = dot(branch, proj_ref[...], NN).astype(BF16)

    @pl.when(pl.program_id(0) == 0)
    def _():
        sums_ref[...] = jnp.zeros(sums_ref.shape, F32)

    for at, part in enumerate((branch.astype(F32), cot, z * unit, z)):
        sums_ref[at : at + 1, :] += jnp.sum(part, axis=0, keepdims=True)


def norm_two(back, recv, residual, cot, vectors, proj, after=()):
    rows, width = back.shape
    steps = 2
    block = rows // steps
    strip = pl.BlockSpec((block, width), lambda i: (i, 0))
    return pl.pallas_call(
        functools.partial(norm_two_kernel, steps=steps),
        grid=(steps,),
        in_specs=[
            strip,
            strip,
            strip,
            strip,
            pl.BlockSpec(vectors.shape, lambda i: (0, 0)),
            pl.BlockSpec(proj.shape, lambda i: (0, 0)),
        ]
        + [ANY_SPACE] * len(after),
        out_specs=[
            strip,
            strip,
            pl.BlockSpec((block, proj.shape[1]), lambda i: (i, 0)),
            pl.BlockSpec((8, width), lambda i: (0, 0)),
        ],
        out_shape=[
            jax.ShapeDtypeStruct((rows, width), F32),
            jax.ShapeDtypeStruct((rows, width), BF16),
            jax.ShapeDtypeStruct((rows, proj.shape[1]), BF16),
            jax.ShapeDtypeStruct((8, width), F32),
        ],
        compiler_params=params(16),
        cost_estimate=cost(4),
        name="norm_two",
    )(back, recv, residual, cot, vectors, proj, *after)


def norm_one_kernel(*refs, terms):
    place_ref, low_ref, high_ref = refs[:3]
    grads, weights = refs[3 : 3 + terms], refs[3 + terms : 3 + 2 * terms]
    own_ref, sent_ref, sums_ref = refs[-3:]
    i = pl.program_id(0)
    z = None
    for grad_ref, weight_ref in zip(grads, weights):
        part = dot(grad_ref[...], weight_ref[...], NT)
        z = part if z is None else z + part
    rows = jnp.where(i == 0, low_ref[...].astype(F32), high_ref[...].astype(F32))
    unit, _ = normalize(rows)

    @pl.when(i == 0)
    def _():
        sums_ref[...] = jnp.zeros(sums_ref.shape, F32)

    sums_ref[0:1, :] += jnp.sum(z * unit, axis=0, keepdims=True)
    sums_ref[1:2, :] += jnp.sum(z, axis=0, keepdims=True)

    @pl.when(i == place_ref[0])
    def _():
        own_ref[...] = z

    @pl.when(i != place_ref[0])
    def _():
        sent_ref[...] = z.astype(BF16)


def norm_one(place, low, high, grads, weights, after=()):
    rows, width = low.shape
    cols = grads[0].shape[1]
    whole = pl.BlockSpec((rows, width), lambda i: (0, 0))
    weight_specs = [
        pl.BlockSpec((width, cols), functools.partial(lambda at, i: (0, at), at))
        for _, at in weights
    ]
    return pl.pallas_call(
        functools.partial(norm_one_kernel, terms=len(grads)),
        grid=(2,),
        in_specs=[pl.BlockSpec(memory_space=pltpu.SMEM), whole, whole]
        + [pl.BlockSpec((rows, cols), lambda i: (i, 0))] * len(grads)
        + weight_specs
        + [ANY_SPACE] * len(after),
        out_specs=[whole, whole, pl.BlockSpec((8, width), lambda i: (0, 0))],
        out_shape=[
            jax.ShapeDtypeStruct((rows, width), F32),
            jax.ShapeDtypeStruct((rows, width), BF16),
            jax.ShapeDtypeStruct((8, width), F32),
        ],
        compiler_params=params(32),
        cost_estimate=cost(8),
        name="norm_one",
    )(place, low, high, *grads, *[weight for weight, _ in weights], *after)


def tie_kernel(value_ref, *rest):
    pass


def tie(value, *after):
    return pl.pallas_call(
        tie_kernel,
        in_specs=[ANY_SPACE] * (1 + len(after)),
        out_specs=ANY_SPACE,
        out_shape=jax.ShapeDtypeStruct(value.shape, value.dtype),
        input_output_aliases={0: 0},
        cost_estimate=cost(0.1),
        name="tie",
    )(value, *after)


def place_kernel(me_ref, *refs):
    full_ref, side_ref, sems = refs[-3:]
    parts = sems.shape[0] // 2
    rows, side_rows = full_ref.shape[0] // parts, side_ref.shape[0] // parts
    copies = []
    for k in range(parts):
        at = lax.bitwise_xor(me_ref[0], k)
        copies.append(
            pltpu.make_async_copy(
                refs[k].at[pl.ds(0, rows)],
                full_ref.at[pl.ds(pl.multiple_of(at * rows, rows), rows)],
                sems.at[2 * k],
            )
        )
        copies.append(
            pltpu.make_async_copy(
                refs[k].at[pl.ds(rows, side_rows)],
                side_ref.at[pl.ds(pl.multiple_of(at * side_rows, side_rows), side_rows)],
                sems.at[2 * k + 1],
            )
        )
    for copy in copies:
        copy.start()
    for copy in copies:
        copy.wait()


def place_shares(me, pieces, side_rows, after):
    total, cols = pieces[0].shape
    parts, kind = len(pieces), pieces[0].dtype
    return pl.pallas_call(
        place_kernel,
        in_specs=[pl.BlockSpec(memory_space=pltpu.SMEM)] + [ANY_SPACE] * (parts + len(after)),
        out_specs=[ANY_SPACE, ANY_SPACE],
        out_shape=[
            jax.ShapeDtypeStruct((parts * (total - side_rows), cols), kind),
            jax.ShapeDtypeStruct((parts * side_rows, cols), kind),
        ],
        scratch_shapes=[pltpu.SemaphoreType.DMA((2 * parts,))],
        cost_estimate=cost(3),
        name="place_shares",
    )(me.reshape(1).astype(jnp.int32), *pieces, *after)


def project_kernel(rows_ref, vec_ref, shift_ref, weight_ref, *rest):
    normed_ref, out_ref = rest[-2:]
    unit, _ = normalize(rows_ref[...].astype(F32))
    normed_ref[...] = (unit * vec_ref[2:3, :] + vec_ref[3:4, :]).astype(BF16)
    out_ref[...] = (dot(normed_ref[...], weight_ref[...], NN) + shift_ref[...]).astype(BF16)


def project(sequence, vectors, shift, weights, block, after=()):
    length, width = sequence.shape
    cols = shift.shape[1]
    return pl.pallas_call(
        project_kernel,
        grid=(length // block,),
        in_specs=[
            pl.BlockSpec((block, width), lambda i: (i, 0)),
            pl.BlockSpec(vectors.shape, lambda i: (0, 0)),
            pl.BlockSpec(shift.shape, lambda i: (0, 0)),
            pl.BlockSpec((width, cols), lambda i: (0, 0)),
        ]
        + [ANY_SPACE] * len(after),
        out_specs=[
            pl.BlockSpec((block, width), lambda i: (i, 0)),
            pl.BlockSpec((block, cols), lambda i: (i, 0)),
        ],
        out_shape=[
            jax.ShapeDtypeStruct((length, width), BF16),
            jax.ShapeDtypeStruct((length, cols), BF16),
        ],
        compiler_params=params(20),
        cost_estimate=cost(6),
        name="project",
    )(sequence, vectors, shift, weights, *after)


def feed_kernel(
    base_ref,
    part_ref,
    recv_ref,
    cot_ref,
    vec_ref,
    shift_own_ref,
    shift_sib_ref,
    fc_own_ref,
    out_own_ref,
    fc_sib_ref,
    out_sib_ref,
    *rest,
    tiles,
):
    residual_ref, normed_ref, act_ref, grad_ref, back_ref, sent_ref, sums_ref = rest[-9:-2]
    back_acc, out_acc = rest[-2:]
    i = pl.program_id(0)
    rows = base_ref.shape[0]

    @pl.when(i == 0)
    def _():
        residual = (
            base_ref[...].astype(F32)
            + part_ref[...].astype(F32)
            + recv_ref[...].astype(F32)
            + vec_ref[0:1, :]
        )
        residual_ref[...] = residual
        unit, _ = normalize(residual)
        normed_ref[...] = (unit * vec_ref[4:5, :] + vec_ref[5:6, :]).astype(BF16)
        back_acc[...] = jnp.zeros(back_acc.shape, F32)
        out_acc[...] = jnp.zeros(out_acc.shape, F32)

    def work(shift_ref, fc_ref, out_ref):
        step = rows // 2
        total = None
        for r in range(2):
            at = slice(r * step, (r + 1) * step)
            hidden = dot(normed_ref[at, :], fc_ref[...], NN) + shift_ref[...]
            grad_act = dot(cot_ref[at, :], out_ref[...], NN)
            act, slope = gelu_both(hidden)
            act = act.astype(BF16)
            grad = (grad_act * slope).astype(BF16)
            act_ref[at, :] = act
            grad_ref[at, :] = grad
            part = jnp.sum(grad.astype(F32), axis=0, keepdims=True)
            total = part if total is None else total + part
            back_acc[at, :] += dot(grad, fc_ref[...], NT)
            out_acc[at, :] += dot(act, out_ref[...], NT)
        sums_ref[...] = total

    @pl.when(i < tiles)
    def _():
        work(shift_own_ref, fc_own_ref, out_own_ref)

    @pl.when(i >= tiles)
    def _():
        work(shift_sib_ref, fc_sib_ref, out_sib_ref)

    @pl.when(i == 2 * tiles - 1)
    def _():
        back_ref[...] = back_acc[...].astype(BF16)
        sent_ref[...] = out_acc[...].astype(BF16)


def feed(base, part, recv, cot, vectors, shift_own, shift_sib, own, sib, after=()):
    rows, width = base.shape
    hidden_cols = shift_own.shape[1]
    tile = min(512, hidden_cols)
    tiles = hidden_cols // tile
    whole = pl.BlockSpec((rows, width), lambda i: (0, 0))

    def low(i):
        return jnp.minimum(i, tiles - 1)

    def high(i):
        return jnp.maximum(i - tiles, 0)

    return pl.pallas_call(
        functools.partial(feed_kernel, tiles=tiles),
        grid=(2 * tiles,),
        in_specs=[
            whole,
            whole,
            whole,
            whole,
            pl.BlockSpec(vectors.shape, lambda i: (0, 0)),
            pl.BlockSpec((1, tile), lambda i: (0, low(i))),
            pl.BlockSpec((1, tile), lambda i: (0, high(i))),
            pl.BlockSpec((width, tile), lambda i: (0, low(i))),
            pl.BlockSpec((width, tile), lambda i: (0, tiles + low(i))),
            pl.BlockSpec((width, tile), lambda i: (0, high(i))),
            pl.BlockSpec((width, tile), lambda i: (0, tiles + high(i))),
        ]
        + [ANY_SPACE] * len(after),
        out_specs=[
            whole,
            whole,
            pl.BlockSpec((rows, tile), lambda i: (0, i)),
            pl.BlockSpec((rows, tile), lambda i: (0, i)),
            whole,
            whole,
            pl.BlockSpec((1, tile), lambda i: (0, i)),
        ],
        out_shape=[
            jax.ShapeDtypeStruct((rows, width), F32),
            jax.ShapeDtypeStruct((rows, width), BF16),
            jax.ShapeDtypeStruct((rows, 2 * hidden_cols), BF16),
            jax.ShapeDtypeStruct((rows, 2 * hidden_cols), BF16),
            jax.ShapeDtypeStruct((rows, width), BF16),
            jax.ShapeDtypeStruct((rows, width), BF16),
            jax.ShapeDtypeStruct((1, 2 * hidden_cols), F32),
        ],
        scratch_shapes=[pltpu.VMEM((rows, width), F32), pltpu.VMEM((rows, width), F32)],
        compiler_params=params(40),
        cost_estimate=cost(16),
        name="feed",
    )(
        base, part, recv, cot, vectors, shift_own, shift_sib, own, own, sib, sib, *after
    )


def swap_dp(value, mask):
    size = lax.axis_size("dp")
    return lax.ppermute(value, "dp", [(i, i ^ mask) for i in range(size)])


def gather_dp(shard, side_rows, after):
    size = lax.axis_size("dp")
    if size != 8:
        rows, cols = shard.shape[0] - side_rows, shard.shape[1]
        full = lax.all_gather(shard, "dp", axis=0)
        return full[:, :rows].reshape(-1, cols), full[:, rows:].reshape(-1, cols)
    pieces = {0: shard}
    for k in (6, 4, 2):
        pieces[k] = swap_dp(shard, k)
    for k in (0, 2, 4, 6):
        pieces[k + 1] = swap_dp(pieces[k], 1)
    shares = [pieces[k] for k in range(size)]
    return place_shares(lax.axis_index("dp"), shares, side_rows, after)


def scatter_start(blocks, kind):
    size = blocks.shape[0]
    if size != 8:
        return blocks, None, blocks
    y = lax.axis_index("dp") % 2
    views = blocks.reshape((size // 2, 2) + blocks.shape[1:])
    sent = lax.dynamic_index_in_dim(views, 1 - y, 1, keepdims=False).astype(kind)
    kept = lax.dynamic_index_in_dim(views, y, 1, keepdims=False)
    return sent, swap_dp(sent, 1), kept


def scatter_finish(received, kept, fill=None, after_y=(), after_z=()):
    if received is None:
        if fill is not None:
            kept = jnp.concatenate([kept, fill[1].astype(kept.dtype)], axis=1)
        return lax.psum_scatter(kept.astype(BF16), "dp", scatter_dimension=0).astype(F32)
    sums = kept.astype(F32) + tie(received, *after_y).astype(F32)
    if fill is not None:
        sums = jnp.concatenate([sums, fill[1] + fill[0]], axis=1)
    z = lax.axis_index("dp") // 2
    result = lax.dynamic_index_in_dim(sums, z, 0, keepdims=False)
    for k in (3, 2, 1):
        sent = lax.dynamic_index_in_dim(sums, z ^ k, 0, keepdims=False).astype(BF16)
        result = result + tie(swap_dp(sent, 2 * k), *after_z).astype(F32)
    return result


def local(
    inputs,
    qkv_weight,
    qv_bias,
    proj_weight,
    proj_bias,
    fc_weight,
    fc_bias,
    out_weight,
    out_bias,
    attn_norm_gain,
    attn_norm_bias,
    mlp_norm_gain,
    mlp_norm_bias,
    cotangent,
):
    width = inputs.shape[1]
    rows = inputs.shape[0]
    share = proj_bias.shape[0]
    parts = width // share
    head_cols = qkv_weight.shape[2]
    pairs = head_cols // PAIR
    qkv_cols = 3 * head_cols
    hidden_cols = fc_weight.shape[1]
    place = lax.axis_index("tensor")
    core = place % 2
    is_low = place < 2
    is_first = core == 0

    def pick_x(low, high):
        return jnp.where(is_low, low, high)

    mlp_shard = jnp.concatenate([fc_weight, out_weight.T], axis=1)
    mlp_all = lax.all_gather(mlp_shard, "dp", axis=0, tiled=True)
    qv_row = jnp.pad(qv_bias.reshape(-1), (0, share - qv_bias.size))
    vectors = jnp.stack(
        [
            proj_bias,
            out_bias,
            attn_norm_gain,
            attn_norm_bias,
            mlp_norm_gain,
            mlp_norm_bias,
            fc_bias,
            qv_row,
        ]
    )
    qkv_shard = jnp.transpose(
        qkv_weight.reshape(3, share, pairs, PAIR), (1, 2, 0, 3)
    ).reshape(share, qkv_cols)
    attn_shard = jnp.concatenate([qkv_shard, proj_weight.T], axis=1)
    side_rows = 16
    vectors = jnp.pad(
        vectors.reshape(1, -1), ((0, side_rows - 1), (0, attn_shard.shape[1] - vectors.size))
    )
    attn_shard = jnp.concatenate([attn_shard, vectors], axis=0)

    input_x = swap_x(inputs)
    input_core = swap_core(inputs)
    input_far = swap_core(input_x)
    input_low, input_high = pick_x(inputs, input_x), pick_x(input_x, inputs)
    far_low, far_high = pick_x(input_core, input_far), pick_x(input_far, input_core)
    cot_x = swap_x(cotangent)
    cots = [pick_x(cotangent, cot_x), pick_x(cot_x, cotangent)]
    sequence = jnp.concatenate(
        [
            jnp.where(is_first, input_low, far_low),
            jnp.where(is_first, far_low, input_low),
            jnp.where(is_first, input_high, far_high),
            jnp.where(is_first, far_high, input_high),
        ],
        axis=0,
    )

    attn_all, vectors = gather_dp(attn_shard, side_rows, (sequence,))
    attn_sib = swap_core(attn_all)
    vectors = vectors.reshape(parts, side_rows, -1)[:, 0, : 8 * share]
    vectors = vectors.reshape(parts, 8, share).transpose(1, 0, 2).reshape(8, width)
    columns = vectors.astype(F32)
    out_shift, gain_one = columns[1:2], columns[2:3]
    fc_shift_own = columns[6:7]
    fc_shift_sib = swap_core(vectors[6:7]).astype(F32)
    qv_shift = (
        columns[7]
        .reshape(parts, share)[:, : share // 2]
        .reshape(parts, 2, share // 4)
        .transpose(1, 0, 2)
        .reshape(2, head_cols)
    )
    qkv_shift = jnp.stack([qv_shift[0], jnp.zeros_like(qv_shift[0]), qv_shift[1]])
    qkv_shift = qkv_shift.reshape(3, pairs, PAIR).transpose(1, 0, 2).reshape(1, qkv_cols)
    proj_both = jnp.concatenate(
        [
            attn_all[:, qkv_cols : qkv_cols + head_cols],
            attn_sib[:, qkv_cols : qkv_cols + head_cols],
        ],
        axis=1,
    )

    normed_one, qkv = project(
        sequence, columns, qkv_shift, attn_all, rows, after=(cots[0], cots[1])
    )

    inputs_two = [input_low, input_high]
    mixed, totals, mixed_rows, parts_two, received_two = [], [], [], [], []
    for half in range(2):
        half_mixed, half_totals = attend(
            qkv, half * 2 * rows, 2 * rows, rows, after=tuple(parts_two)
        )
        mixed.append(half_mixed)
        totals.append(half_totals)
        two = half_mixed.reshape(2, rows, head_cols)
        mine = jnp.where(is_first, two[0], two[1])
        received = swap_core(jnp.where(is_first, two[1], two[0]))
        both = jnp.concatenate([mine, received], axis=1)
        mixed_rows.append(both)
        part = dot(both, proj_both, NT).astype(BF16)
        parts_two.append(part)
        received_two.append(swap_x(part))
    mlp_all = tie(mlp_all, received_two[0], mixed[1])
    mlp_sib = swap_core(mlp_all)
    residuals, normed_two, acts, grads_hidden, backs, out_parts = [], [], [], [], [], []
    fc_bias_sums = 0.0
    for half in range(2):
        residual, normed, act, grad_hidden, back, out_part, sums = feed(
            inputs_two[half],
            parts_two[half],
            received_two[half],
            cots[half],
            columns,
            fc_shift_own,
            fc_shift_sib,
            mlp_all,
            mlp_sib,
            after=(parts_two[1],),
        )
        residuals.append(residual)
        normed_two.append(normed)
        acts.append(act)
        grads_hidden.append(grad_hidden)
        backs.append(back)
        out_parts.append(out_part)
        fc_bias_sums = fc_bias_sums + sums[0]
    back_recv = [swap_x(back) for back in backs]

    act_all = jnp.concatenate(acts, axis=0)
    grad_hidden_all = jnp.concatenate(grads_hidden, axis=0)
    normed_two_all = tie(jnp.concatenate(normed_two, axis=0), back_recv[0])
    cot_all = tie(jnp.concatenate(cots, axis=0), back_recv[0])
    fc_sib = dot(normed_two_all, grad_hidden_all[:, hidden_cols:], TN).astype(BF16)
    fc_recv = swap_core(fc_sib)
    out_sib = dot(cot_all, act_all[:, hidden_cols:], TN).astype(BF16)
    out_recv = swap_core(out_sib)
    fc_own = dot(normed_two_all, grad_hidden_all[:, :hidden_cols], TN)
    out_own = dot(cot_all, act_all[:, :hidden_cols], TN)
    grad_mlp = jnp.concatenate(
        [
            (fc_own + fc_recv.astype(F32)).astype(BF16),
            (out_own + out_recv.astype(F32)).astype(BF16),
        ],
        axis=1,
    )
    mlp_sum = lax.psum_scatter(grad_mlp, "dp", scatter_dimension=0, tiled=True)

    grad_residuals, branches, grads_mixed = [], [], []
    for half in range(2):
        grad_residual, branch, grad_both, sums_two = norm_two(
            backs[half],
            back_recv[half],
            residuals[half],
            cots[half],
            columns,
            proj_both,
            after=(grad_mlp,) if half == 0 else (grad_mlp, low_grads),
        )
        grad_residuals.append(grad_residual)
        branches.append(branch)
        mine = grad_both[:, :head_cols]
        received = swap_core(grad_both[:, head_cols:])
        grads_mixed.append(
            jnp.concatenate(
                [jnp.where(is_first, mine, received), jnp.where(is_first, received, mine)], axis=0
            )
        )
        vec_two = sums_two if half == 0 else vec_two + sums_two
        if half == 0:
            low_grads, _ = attend_back(
                qkv, mixed[0], grads_mixed[0], totals[0], None, 0, rows, 0, pairs
            )
    branch_all = jnp.concatenate(branches, axis=0)
    mixed_all = jnp.concatenate(mixed_rows, axis=0)
    proj_grad = dot(branch_all, mixed_all, TN)
    proj_grad = proj_grad[:, :head_cols] + swap_core(
        proj_grad[:, head_cols:].astype(BF16)
    ).astype(F32)

    out_sent = tie(pick_x(out_parts[1], out_parts[0]), low_grads)
    out_recv = swap_x(out_sent)

    grads_own, grads_received, bias_sums, exchanges = [], [], [], []
    after = ()
    for pair in range(pairs):
        grad_pair, pair_sums = attend_back(
            qkv,
            mixed[1],
            grads_mixed[1],
            totals[1],
            low_grads,
            2 * rows,
            rows,
            pair,
            1,
            after=after,
        )
        bias_sums.append(pair_sums.reshape(3, PAIR))
        blocks = grad_pair.reshape(2, 2, rows, 3 * PAIR)
        mine = jnp.where(is_first, blocks[:, 0], blocks[:, 1])
        sent = jnp.where(is_first, blocks[:, 1], blocks[:, 0])
        grads_own.append(mine.reshape(2 * rows, 3 * PAIR))
        received = swap_core(sent.reshape(2 * rows, 3 * PAIR))
        grads_received.append(received)
        grad_weight = dot(normed_one, grad_pair, TN).astype(BF16)
        if pair == 0:
            grad_weight = jnp.concatenate([grad_weight, proj_grad.astype(BF16)], axis=1)
            out_recv = tie(out_recv, grad_pair)
        exchanges.append(scatter_start(grad_weight.reshape(parts, share, -1), BF16))
        after = (exchanges[pair][0], out_recv)

    z_own, z_sent, vec_one = norm_one(
        (place // 2).reshape(1),
        input_low,
        input_high,
        grads_own + grads_received,
        [(attn_all, pair) for pair in range(pairs)] + [(attn_sib, pair) for pair in range(pairs)],
        after=(exchanges[-1][0],),
    )
    z_recv = swap_x(z_sent)
    vec_two = vec_two + swap_core(vec_two)

    bias_sums = jnp.stack(bias_sums)
    qv_sums = jnp.stack([bias_sums[:, 0].reshape(-1), bias_sums[:, 2].reshape(-1)])
    qv_sums = qv_sums.reshape(2, parts, share // 4).transpose(1, 0, 2).reshape(parts, share // 2)
    qv_sums = jnp.pad(qv_sums, ((0, 0), (0, share - share // 2))).reshape(-1)
    fc_bias_grad = fc_bias_sums[:hidden_cols] + swap_core(fc_bias_sums[hidden_cols:])
    vec_grads = jnp.concatenate(
        [vec_two[:2], vec_one[:2], vec_two[2:4], fc_bias_grad[None], qv_sums[None]], axis=0
    )
    vec_blocks = vec_grads.reshape(8, parts, share).transpose(1, 0, 2)
    wide = ((0, 0), (0, 8), (0, 3 * PAIR - share))
    vec_blocks = jnp.pad(vec_blocks, wide)
    _, vec_received, vec_kept = scatter_start(vec_blocks, F32)
    sums = []
    for pair in range(pairs):
        _, received, kept = exchanges[pair]
        if pair < pairs - 1:
            fill, after_y, after_z = None, grads_received[-1:], (z_sent,)
        else:
            fill, after_y, after_z = (vec_received, vec_kept), (z_sent,), (z_recv,)
        sums.append(scatter_finish(received, kept, fill, after_y, after_z))

    out_mine = pick_x(out_parts[0], out_parts[1])
    outputs = (
        pick_x(residuals[0], residuals[1])
        + out_mine.astype(F32)
        + out_recv.astype(F32)
        + out_shift
    ).astype(BF16)

    unit, factor = normalize(inputs.astype(F32))
    z_own = z_own + z_recv.astype(F32)
    grad_inputs = (
        pick_x(grad_residuals[0], grad_residuals[1]) + norm_back(unit, factor, gain_one, z_own)
    ).astype(BF16)

    qkv_out = jnp.stack([part[:share, : 3 * PAIR] for part in sums], axis=1)
    qkv_out = (
        qkv_out.reshape(share, pairs, 3, PAIR).transpose(2, 0, 1, 3).reshape(3, share, head_cols)
    )
    proj_out = sums[0][:share, 3 * PAIR : 3 * PAIR + head_cols].T
    six = sums[-1][share:, :share]
    one = six[2:4]
    two = (
        one
        + swap_core(one)
        + swap_x(one)
        + lax.ppermute(one, "tensor", [(i, i ^ 3) for i in range(4)])
    )
    qv_out = six[7][: share // 2].reshape(2, share // 4)
    fc_out = mlp_sum[:, :hidden_cols].astype(F32)
    out_out = mlp_sum[:, hidden_cols:].astype(F32).T
    return (
        outputs,
        grad_inputs,
        qkv_out,
        qv_out,
        proj_out,
        six[0],
        fc_out,
        six[6],
        out_out,
        six[1],
        two[0],
        two[1],
        six[4],
        six[5],
    )


def solution(mesh):
    rows = P(("dp", "tensor"), None)
    vector = P("dp")
    wide = P(("tensor", "dp"))
    weights = (
        P(None, "dp", "tensor"),
        P(None, ("tensor", "dp")),
        P("tensor", "dp"),
        vector,
        P("dp", "tensor"),
        wide,
        P("tensor", "dp"),
        vector,
        vector,
        vector,
        vector,
        vector,
    )
    return jax.shard_map(
        local,
        mesh=mesh,
        in_specs=(rows, *weights, rows),
        out_specs=(rows, rows, *weights),
        check_vma=False,
    )
```

```python
import functools

import jax
import jax.numpy as jnp
from jax import lax
from jax.experimental import pallas as pl
from jax.experimental.pallas import tpu as pltpu
from jax.sharding import PartitionSpec as P

HD = 64
PAIR = 2 * HD
EPSILON = 1e-05
NEGATIVE = -1e30
ROOT_TWO_PI = 0.7978845608028654
F32 = jnp.float32
BF16 = jnp.bfloat16
MIB = 1024 * 1024
SCALE = 0.25
ANY_SPACE = pl.BlockSpec(memory_space=pl.ANY)
SCALARS = pl.BlockSpec(memory_space=pltpu.SMEM)


def params(mib):
    return pltpu.CompilerParams(vmem_limit_bytes=mib * MIB)


def cost(micros):
    return pl.CostEstimate(
        flops=int(micros * SCALE * 1.1e9),
        bytes_accessed=int(micros * SCALE * 1e6),
        transcendentals=0,
    )


def swap_x(value):
    return lax.ppermute(value, "tensor", [(0, 2), (2, 0), (1, 3), (3, 1)])


def swap_core(value):
    return lax.ppermute(value, "tensor", [(0, 1), (1, 0), (2, 3), (3, 2)])


def dot(a, b, contract, kind=F32):
    return lax.dot_general(a, b, (contract, ((), ())), preferred_element_type=kind)


NN = ((1,), (0,))
NT = ((1,), (1,))
TN = ((0,), (0,))


def normalize(values):
    average = jnp.mean(values, axis=-1, keepdims=True)
    centered = values - average
    spread = jnp.mean(centered * centered, axis=-1, keepdims=True)
    factor = lax.rsqrt(spread + EPSILON)
    return centered * factor, factor


def norm_back(unit, factor, gain, grad):
    scaled = grad * gain
    return factor * (
        scaled
        - jnp.mean(scaled, axis=-1, keepdims=True)
        - unit * jnp.mean(scaled * unit, axis=-1, keepdims=True)
    )


def gelu_both(values):
    squared = values * values
    bent = jnp.tanh(ROOT_TWO_PI * values * (1.0 + 0.044715 * squared))
    half = 0.5 * (1.0 + bent)
    slope = half + 0.5 * values * (1.0 - bent * bent) * ROOT_TWO_PI * (
        1.0 + 3.0 * 0.044715 * squared
    )
    return values * half, slope


def split_heads(block):
    first = lax.broadcasted_iota(jnp.int32, block.shape, 1) < HD
    return [jnp.where(first, block, 0.0).astype(BF16), jnp.where(first, 0.0, block).astype(BF16)]


def attend_kernel(qkv_ref, *rest, row0, block):
    mixed_ref, total_ref, kept, acc = rest[-4:]
    count = mixed_ref.shape[0] // block
    first = lax.broadcasted_iota(jnp.int32, (PAIR, block), 0) < HD
    causal = lax.broadcasted_iota(jnp.int32, (block, block), 0) <= lax.broadcasted_iota(
        jnp.int32, (block, block), 1
    )
    for i in range(count):
        start = row0 + i * block
        heads = split_heads(qkv_ref[pl.ds(start, block), 0:PAIR].astype(F32) * (HD**-0.5))
        keys = qkv_ref[pl.ds(start, block), PAIR : 2 * PAIR]
        tops = []
        for h in range(2):
            scores = jnp.where(causal, dot(keys, heads[h], NT), NEGATIVE)
            kept[h, pl.ds(start, block), :] = scores
            tops.append(jnp.max(scores, axis=0, keepdims=True))

        def score_step(j, tops):
            at = pl.multiple_of(j * block, block)
            tile_keys = qkv_ref[pl.ds(at, block), PAIR : 2 * PAIR]
            found = []
            for h in range(2):
                scores = dot(tile_keys, heads[h], NT)
                kept[h, pl.ds(at, block), :] = scores
                found.append(jnp.maximum(tops[h], jnp.max(scores, axis=0, keepdims=True)))
            return tuple(found)

        tops = lax.fori_loop(0, start // block, score_step, tuple(tops))
        acc[...] = jnp.zeros(acc.shape, F32)

        def value_step(j, sums):
            at = pl.multiple_of(j * block, block)
            tile_values = qkv_ref[pl.ds(at, block), 2 * PAIR : 3 * PAIR]
            found = []
            for h in range(2):
                powers = jnp.exp(kept[h, pl.ds(at, block), :] - tops[h])
                found.append(sums[h] + jnp.sum(powers, axis=0, keepdims=True))
                acc[h] += dot(powers.astype(BF16), tile_values, TN)
            return tuple(found)

        zero = jnp.zeros((1, block), F32)
        sums = lax.fori_loop(0, start // block + 1, value_step, (zero, zero))
        inverse = jnp.transpose(jnp.where(first, 1.0 / sums[0], 1.0 / sums[1]))
        lane = lax.broadcasted_iota(jnp.int32, (block, PAIR), 1) < HD
        local = slice(i * block, (i + 1) * block)
        mixed_ref[local, :] = (jnp.where(lane, acc[0], acc[1]) * inverse).astype(BF16)
        for h in range(2):
            total_ref[0, h : h + 1, local] = tops[h] + jnp.log(sums[h])


def attend(qkv, row0, rows, block, after=()):
    pairs = qkv.shape[1] // (3 * PAIR)
    return pl.pallas_call(
        functools.partial(attend_kernel, row0=row0, block=block),
        grid=(pairs,),
        in_specs=[pl.BlockSpec((row0 + rows, 3 * PAIR), lambda j: (0, j))]
        + [ANY_SPACE] * len(after),
        out_specs=[
            pl.BlockSpec((rows, PAIR), lambda j: (0, j)),
            pl.BlockSpec((1, 2, rows), lambda j: (j, 0, 0)),
        ],
        out_shape=[
            jax.ShapeDtypeStruct((rows, pairs * PAIR), BF16),
            jax.ShapeDtypeStruct((pairs, 2, rows), F32),
        ],
        scratch_shapes=[
            pltpu.VMEM((2, row0 + rows, block), F32),
            pltpu.VMEM((2, block, PAIR), F32),
        ],
        compiler_params=params(24),
        cost_estimate=cost(16 if row0 else 6),
        name="attend_%d" % row0,
    )(qkv, *after)


def attend_back_kernel(
    core_ref, qkv_ref, mixed_ref, grad_ref, total_ref, *rest, row0, block, has_before
):
    before_ref = rest[0]
    sent_ref = None
    if has_before:
        out_ref, sums_ref, sent_ref, key_acc, value_acc, query_acc = rest[-6:]
    else:
        out_ref, sums_ref, key_acc, value_acc, query_acc = rest[-5:]
    rows = mixed_ref.shape[0]
    count = rows // block
    lane = lax.broadcasted_iota(jnp.int32, (block, PAIR), 1)
    first = lane < HD
    causal = lax.broadcasted_iota(jnp.int32, (block, block), 0) <= lax.broadcasted_iota(
        jnp.int32, (block, block), 1
    )
    if has_before:
        key_acc[0:row0, :] = before_ref[:, PAIR : 2 * PAIR]
        value_acc[0:row0, :] = before_ref[:, 2 * PAIR : 3 * PAIR]
        key_acc[row0:, :] = jnp.zeros((rows, PAIR), F32)
        value_acc[row0:, :] = jnp.zeros((rows, PAIR), F32)
    else:
        key_acc[...] = jnp.zeros(key_acc.shape, F32)
        value_acc[...] = jnp.zeros(value_acc.shape, F32)
    for i in range(count):
        start = row0 + i * block
        local = slice(i * block, (i + 1) * block)
        query_heads = split_heads(
            qkv_ref[pl.ds(start, block), 0:PAIR].astype(F32) * (HD**-0.5)
        )
        grads = grad_ref[local, :].astype(F32)
        grad_heads = split_heads(grads)
        inner = jnp.transpose(grads * mixed_ref[local, :].astype(F32))
        total_rows = [total_ref[0, h : h + 1, local] for h in range(2)]
        inner_rows = [
            jnp.sum(inner[h * HD : (h + 1) * HD, :], axis=0, keepdims=True) for h in range(2)
        ]

        def tile(at, masked):
            tile_keys = qkv_ref[pl.ds(at, block), PAIR : 2 * PAIR]
            tile_values = qkv_ref[pl.ds(at, block), 2 * PAIR : 3 * PAIR]
            key_sum, value_sum = None, None
            for h in range(2):
                scores = dot(tile_keys, query_heads[h], NT)
                weights = jnp.exp(scores - total_rows[h])
                if masked:
                    weights = jnp.where(causal, weights, 0.0)
                grad_weights = dot(tile_values, grad_heads[h], NT)
                grad_scores = (weights * (grad_weights - inner_rows[h])).astype(BF16)
                value_part = dot(weights.astype(BF16), grad_heads[h], NN)
                key_part = dot(grad_scores, query_heads[h], NN)
                query_part = dot(grad_scores, tile_keys, TN)
                key_sum = key_part if key_sum is None else key_sum + key_part
                value_sum = value_part if value_sum is None else value_sum + value_part
                if masked:
                    query_acc[h] = query_part
                else:
                    query_acc[h] += query_part
            key_acc[pl.ds(at, block), :] += key_sum
            value_acc[pl.ds(at, block), :] += value_sum

        tile(start, True)

        def step(j, carry):
            tile(pl.multiple_of(j * block, block), False)
            return carry

        if start:
            lax.fori_loop(0, start // block, step, 0)
        query_grad = jnp.where(first, query_acc[0], query_acc[1]) * (HD**-0.5)
        out_ref[start : start + block, 0:PAIR] = query_grad.astype(out_ref.dtype)
    if has_before:
        out_ref[0:row0, 0:PAIR] = before_ref[:, 0:PAIR].astype(out_ref.dtype)
    out_ref[:, PAIR : 2 * PAIR] = key_acc[...].astype(out_ref.dtype)
    out_ref[:, 2 * PAIR : 3 * PAIR] = value_acc[...].astype(out_ref.dtype)
    sums_ref[...] = jnp.sum(out_ref[...].astype(F32), axis=0, keepdims=True)
    if has_before:
        size = sent_ref.shape[0] // 2
        for half in range(2):
            at = pl.multiple_of((2 * half + 1 - core_ref[0]) * size, size)
            sent_ref[half * size : (half + 1) * size, :] = out_ref[pl.ds(at, size), :]


def attend_back(qkv, mixed, grads, totals, before, row0, block, pair, pairs, after=(), core=None):
    rows = mixed.shape[0]
    extent = row0 + rows
    narrow = pl.BlockSpec((rows, PAIR), lambda j: (0, pair + j))
    in_specs = [
        SCALARS,
        pl.BlockSpec((extent, 3 * PAIR), lambda j: (0, pair + j)),
        narrow,
        narrow,
        pl.BlockSpec((1, 2, rows), lambda j: (pair + j, 0, 0)),
    ]
    core = jnp.zeros((), jnp.int32) if core is None else core
    operands = [core.reshape(1).astype(jnp.int32), qkv, mixed, grads, totals]
    if before is not None:
        in_specs.append(pl.BlockSpec((row0, 3 * PAIR), lambda j: (0, pair + j)))
        operands.append(before)
    in_specs += [ANY_SPACE] * len(after)
    return pl.pallas_call(
        functools.partial(
            attend_back_kernel, row0=row0, block=block, has_before=before is not None
        ),
        grid=(pairs,),
        in_specs=in_specs,
        out_specs=[
            pl.BlockSpec((extent, 3 * PAIR), lambda j: (0, j)),
            pl.BlockSpec((1, 3 * PAIR), lambda j: (0, j)),
        ]
        + ([] if before is None else [pl.BlockSpec((extent // 2, 3 * PAIR), lambda j: (0, j))]),
        out_shape=[
            jax.ShapeDtypeStruct((extent, pairs * 3 * PAIR), F32 if before is None else BF16),
            jax.ShapeDtypeStruct((1, pairs * 3 * PAIR), F32),
        ]
        + (
            []
            if before is None
            else [jax.ShapeDtypeStruct((extent // 2, pairs * 3 * PAIR), BF16)]
        ),
        scratch_shapes=[
            pltpu.VMEM((extent, PAIR), F32),
            pltpu.VMEM((extent, PAIR), F32),
            pltpu.VMEM((2, block, PAIR), F32),
        ],
        compiler_params=params(32),
        cost_estimate=cost(5.5 * pairs if before is None else 13 * pairs),
        name="attend_back_%d_%d" % (row0, pair),
    )(*operands, *after)


def norm_two_kernel(
    back_ref, recv_ref, residual_ref, cot_ref, vec_ref, proj_ref, *rest, steps
):
    grad_ref, branch_ref, both_ref, sums_ref = rest[-4:]
    z = back_ref[...].astype(F32) + recv_ref[...].astype(F32)
    unit, factor = normalize(residual_ref[...])
    cot = cot_ref[...].astype(F32)
    grad = cot + norm_back(unit, factor, vec_ref[4:5, :], z)
    grad_ref[...] = grad
    branch = grad.astype(BF16)
    branch_ref[...] = branch
    both_ref[...] = dot(branch, proj_ref[...], NN).astype(BF16)

    @pl.when(pl.program_id(0) == 0)
    def _():
        sums_ref[...] = jnp.zeros(sums_ref.shape, F32)

    for at, part in enumerate((branch.astype(F32), cot, z * unit, z)):
        sums_ref[at : at + 1, :] += jnp.sum(part, axis=0, keepdims=True)


def norm_two(back, recv, residual, cot, vectors, proj, after=()):
    rows, width = back.shape
    steps = 2
    block = rows // steps
    strip = pl.BlockSpec((block, width), lambda i: (i, 0))
    return pl.pallas_call(
        functools.partial(norm_two_kernel, steps=steps),
        grid=(steps,),
        in_specs=[
            strip,
            strip,
            strip,
            strip,
            pl.BlockSpec(vectors.shape, lambda i: (0, 0)),
            pl.BlockSpec(proj.shape, lambda i: (0, 0)),
        ]
        + [ANY_SPACE] * len(after),
        out_specs=[
            strip,
            strip,
            pl.BlockSpec((block, proj.shape[1]), lambda i: (i, 0)),
            pl.BlockSpec((8, width), lambda i: (0, 0)),
        ],
        out_shape=[
            jax.ShapeDtypeStruct((rows, width), F32),
            jax.ShapeDtypeStruct((rows, width), BF16),
            jax.ShapeDtypeStruct((rows, proj.shape[1]), BF16),
            jax.ShapeDtypeStruct((8, width), F32),
        ],
        compiler_params=params(16),
        cost_estimate=cost(4),
        name="norm_two",
    )(back, recv, residual, cot, vectors, proj, *after)


def norm_one_kernel(place_ref, low_ref, high_ref, *refs, terms):
    grads, weights = refs[:terms], refs[terms : 2 * terms]
    own_ref, sent_ref, sums_ref = refs[-3:]
    i = pl.program_id(0)
    z = None
    for grad_ref, weight_ref in zip(grads, weights):
        part = dot(grad_ref[...], weight_ref[...], NT)
        z = part if z is None else z + part
    rows = jnp.where(i == 0, low_ref[...].astype(F32), high_ref[...].astype(F32))
    unit, _ = normalize(rows)

    @pl.when(i == 0)
    def _():
        sums_ref[...] = jnp.zeros(sums_ref.shape, F32)

    sums_ref[0:1, :] += jnp.sum(z * unit, axis=0, keepdims=True)
    sums_ref[1:2, :] += jnp.sum(z, axis=0, keepdims=True)

    @pl.when(i == place_ref[0])
    def _():
        own_ref[...] = z

    @pl.when(i != place_ref[0])
    def _():
        sent_ref[...] = z.astype(BF16)


def norm_one(places, low, high, full, received, own_weights, sib_weights, after=()):
    rows, width = low.shape
    pairs = len(full)
    cols = full[0].shape[1]
    whole = pl.BlockSpec((rows, width), lambda i, at: (0, 0))
    weight_specs = [
        pl.BlockSpec((width, cols), functools.partial(lambda pair, i, at: (0, pair), pair))
        for pair in range(pairs)
    ]
    return pl.pallas_call(
        functools.partial(norm_one_kernel, terms=2 * pairs),
        grid_spec=pltpu.PrefetchScalarGridSpec(
            num_scalar_prefetch=1,
            grid=(2,),
            in_specs=[whole, whole]
            + [pl.BlockSpec((rows, cols), lambda i, at: (2 * i + at[1], 0))] * pairs
            + [pl.BlockSpec((rows, cols), lambda i, at: (i, 0))] * pairs
            + weight_specs * 2
            + [ANY_SPACE] * len(after),
            out_specs=[whole, whole, pl.BlockSpec((8, width), lambda i, at: (0, 0))],
        ),
        out_shape=[
            jax.ShapeDtypeStruct((rows, width), F32),
            jax.ShapeDtypeStruct((rows, width), BF16),
            jax.ShapeDtypeStruct((8, width), F32),
        ],
        compiler_params=params(32),
        cost_estimate=cost(8),
        name="norm_one",
    )(
        places,
        low,
        high,
        *full,
        *received,
        *[own_weights] * pairs,
        *[sib_weights] * pairs,
        *after,
    )


def tie_kernel(value_ref, *rest):
    pass


def tie(value, *after):
    return pl.pallas_call(
        tie_kernel,
        in_specs=[ANY_SPACE] * (1 + len(after)),
        out_specs=ANY_SPACE,
        out_shape=jax.ShapeDtypeStruct(value.shape, value.dtype),
        input_output_aliases={0: 0},
        cost_estimate=cost(0.1),
        name="tie",
    )(value, *after)


def place_kernel(me_ref, *refs, parts, side_rows):
    full_ref = refs[-1]
    rows = refs[0].shape[0] - side_rows
    for k in range(parts):
        at = lax.bitwise_xor(me_ref[0], k)
        full_ref[pl.ds(pl.multiple_of(at * rows, rows), rows), :] = refs[k][0:rows, :]
        side = pl.multiple_of(parts * rows + at * side_rows, side_rows)
        full_ref[pl.ds(side, side_rows), :] = refs[k][rows:, :]


def place_shares(me, pieces, side_rows, after):
    total, cols = pieces[0].shape
    parts, kind = len(pieces), pieces[0].dtype
    return pl.pallas_call(
        functools.partial(place_kernel, parts=parts, side_rows=side_rows),
        grid=(1,),
        in_specs=[SCALARS]
        + [pl.BlockSpec((total, cols), lambda i: (0, 0))] * parts
        + [ANY_SPACE] * len(after),
        out_specs=pl.BlockSpec((parts * total, cols), lambda i: (0, 0)),
        out_shape=jax.ShapeDtypeStruct((parts * total, cols), kind),
        compiler_params=params(16),
        cost_estimate=cost(3),
        name="place_shares",
    )(me.reshape(1).astype(jnp.int32), *pieces, *after)


def feed_grads_kernel(*refs, tiles, received):
    normed, cots, grads, acts = refs[0:2], refs[2:4], refs[4:6], refs[6:8]
    out_ref = refs[-1]
    i = pl.program_id(0)

    def work(left, right):
        total = dot(left[0][...], right[0][...], TN) + dot(left[1][...], right[1][...], TN)
        if received:
            total = total + refs[8][...].astype(F32)
        out_ref[...] = total.astype(BF16)

    @pl.when(i < tiles)
    def _():
        work(normed, grads)

    @pl.when(i >= tiles)
    def _():
        work(cots, acts)


def feed_grads(normed, cots, grads, acts, first, received, after=()):
    rows, width = normed[0].shape
    hidden_cols = grads[0].shape[1] // 2
    tile = min(512, hidden_cols)
    tiles = hidden_cols // tile
    base = first // tile
    whole = pl.BlockSpec((rows, width), lambda i: (0, 0))
    grad_spec = pl.BlockSpec((rows, tile), lambda i: (0, base + jnp.minimum(i, tiles - 1)))
    act_spec = pl.BlockSpec((rows, tile), lambda i: (0, base + jnp.maximum(i - tiles, 0)))
    out_spec = pl.BlockSpec((width, tile), lambda i: (0, i))
    return pl.pallas_call(
        functools.partial(feed_grads_kernel, tiles=tiles, received=received is not None),
        grid=(2 * tiles,),
        in_specs=[whole] * 4
        + [grad_spec] * 2
        + [act_spec] * 2
        + ([] if received is None else [out_spec])
        + [ANY_SPACE] * len(after),
        out_specs=out_spec,
        out_shape=jax.ShapeDtypeStruct((width, 2 * hidden_cols), BF16),
        compiler_params=params(32),
        cost_estimate=cost(6),
        name="feed_grads",
    )(*normed, *cots, *grads, *acts, *([] if received is None else [received]), *after)


def weight_grads_kernel(y_ref, normed_ref, grad_ref, *refs, with_proj):
    kept_ref, sent_ref = refs[-2:]
    share = kept_ref.shape[1]
    total = dot(normed_ref[...], grad_ref[...], TN)
    if with_proj:
        low_ref, high_ref, low_mixed_ref, high_mixed_ref, recv_ref = refs[:5]
        proj = dot(low_ref[...], low_mixed_ref[...], TN) + dot(
            high_ref[...], high_mixed_ref[...], TN
        )
        proj = proj + recv_ref[...].astype(F32)
        total = jnp.concatenate([total, proj], axis=1)
    even, odd = total[:share], total[share:]
    stays = y_ref[0] == 0
    kept_ref[0] = jnp.where(stays, even, odd)
    sent_ref[0] = jnp.where(stays, odd, even).astype(BF16)


def weight_grads(y, normed, grads, proj, after=()):
    length, width = normed.shape
    cols = grads.shape[1]
    steps, share = 4, width // 8
    in_specs = [
        SCALARS,
        pl.BlockSpec((length, 2 * share), lambda i: (0, i)),
        pl.BlockSpec((length, cols), lambda i: (0, 0)),
    ]
    operands = [y.reshape(1).astype(jnp.int32), normed, grads]
    total = cols
    if proj is not None:
        branches, mixed, received = proj
        rows, head_cols = mixed[0].shape
        total += head_cols
        in_specs += [pl.BlockSpec((rows, 2 * share), lambda i: (0, i))] * 2
        in_specs += [pl.BlockSpec((rows, head_cols), lambda i: (0, 0))] * 2
        in_specs += [pl.BlockSpec((2 * share, head_cols), lambda i: (i, 0))]
        operands += [*branches, *mixed, received]
    return pl.pallas_call(
        functools.partial(weight_grads_kernel, with_proj=proj is not None),
        grid=(steps,),
        in_specs=in_specs + [ANY_SPACE] * len(after),
        out_specs=[pl.BlockSpec((1, share, total), lambda i: (i, 0, 0))] * 2,
        out_shape=[
            jax.ShapeDtypeStruct((steps, share, total), F32),
            jax.ShapeDtypeStruct((steps, share, total), BF16),
        ],
        compiler_params=params(24),
        cost_estimate=cost(4),
        name="weight_grads",
    )(*operands, *after)


def finish_kernel(*refs, pairs, counts):
    qkv_ref, proj_ref, side_ref = refs[-3:]
    at = 0
    for pair in range(pairs):
        total = refs[at][...].astype(F32)
        for part in range(1, counts[pair]):
            total = total + refs[at + part][...].astype(F32)
        at += counts[pair]
        share = qkv_ref.shape[1]
        for j in range(3):
            qkv_ref[j, :, pair * PAIR : (pair + 1) * PAIR] = total[:share, j * PAIR : (j + 1) * PAIR]
        if pair == 0:
            proj_ref[...] = jnp.transpose(total[:share, 3 * PAIR :])
        if pair == pairs - 1:
            side_ref[...] = total[share:, : 3 * PAIR]


def finish(terms, share, head_cols, side_rows, after=()):
    pairs = len(terms)
    flat = [term for pair in terms for term in pair]
    return pl.pallas_call(
        functools.partial(
            finish_kernel, pairs=pairs, counts=[len(pair) for pair in terms]
        ),
        grid=(1,),
        in_specs=[pl.BlockSpec(term.shape, lambda i: (0, 0)) for term in flat]
        + [ANY_SPACE] * len(after),
        out_specs=[
            pl.BlockSpec((3, share, head_cols), lambda i: (0, 0, 0)),
            pl.BlockSpec((head_cols, share), lambda i: (0, 0)),
            pl.BlockSpec((side_rows, 3 * PAIR), lambda i: (0, 0)),
        ],
        out_shape=[
            jax.ShapeDtypeStruct((3, share, head_cols), F32),
            jax.ShapeDtypeStruct((head_cols, share), F32),
            jax.ShapeDtypeStruct((side_rows, 3 * PAIR), F32),
        ],
        compiler_params=params(16),
        cost_estimate=cost(3),
        name="finish",
    )(*flat, *after)


def project_kernel(rows_ref, vec_ref, shift_ref, weight_ref, *rest):
    normed_ref, out_ref = rest[-2:]
    unit, _ = normalize(rows_ref[...].astype(F32))
    normed_ref[...] = (unit * vec_ref[2:3, :] + vec_ref[3:4, :]).astype(BF16)
    out_ref[...] = (dot(normed_ref[...], weight_ref[...], NN) + shift_ref[...]).astype(BF16)


def project(sequence, vectors, shift, weights, block, after=()):
    length, width = sequence.shape
    cols = shift.shape[1]
    return pl.pallas_call(
        project_kernel,
        grid=(length // block,),
        in_specs=[
            pl.BlockSpec((block, width), lambda i: (i, 0)),
            pl.BlockSpec(vectors.shape, lambda i: (0, 0)),
            pl.BlockSpec(shift.shape, lambda i: (0, 0)),
            pl.BlockSpec((width, cols), lambda i: (0, 0)),
        ]
        + [ANY_SPACE] * len(after),
        out_specs=[
            pl.BlockSpec((block, width), lambda i: (i, 0)),
            pl.BlockSpec((block, cols), lambda i: (i, 0)),
        ],
        out_shape=[
            jax.ShapeDtypeStruct((length, width), BF16),
            jax.ShapeDtypeStruct((length, cols), BF16),
        ],
        compiler_params=params(20),
        cost_estimate=cost(6),
        name="project",
    )(sequence, vectors, shift, weights, *after)


def feed_kernel(
    base_ref,
    part_ref,
    recv_ref,
    cot_ref,
    vec_ref,
    shift_own_ref,
    shift_sib_ref,
    fc_own_ref,
    out_own_ref,
    fc_sib_ref,
    out_sib_ref,
    *rest,
    tiles,
):
    residual_ref, normed_ref, act_ref, grad_ref, back_ref, sent_ref, sums_ref = rest[-9:-2]
    back_acc, out_acc = rest[-2:]
    i = pl.program_id(0)
    rows = base_ref.shape[0]

    @pl.when(i == 0)
    def _():
        residual = (
            base_ref[...].astype(F32)
            + part_ref[...].astype(F32)
            + recv_ref[...].astype(F32)
            + vec_ref[0:1, :]
        )
        residual_ref[...] = residual
        unit, _ = normalize(residual)
        normed_ref[...] = (unit * vec_ref[4:5, :] + vec_ref[5:6, :]).astype(BF16)
        back_acc[...] = jnp.zeros(back_acc.shape, F32)
        out_acc[...] = jnp.zeros(out_acc.shape, F32)

    def work(shift_ref, fc_ref, out_ref):
        step = rows // 2
        total = None
        for r in range(2):
            at = slice(r * step, (r + 1) * step)
            hidden = dot(normed_ref[at, :], fc_ref[...], NN) + shift_ref[...]
            grad_act = dot(cot_ref[at, :], out_ref[...], NN)
            act, slope = gelu_both(hidden)
            act = act.astype(BF16)
            grad = (grad_act * slope).astype(BF16)
            act_ref[at, :] = act
            grad_ref[at, :] = grad
            part = jnp.sum(grad.astype(F32), axis=0, keepdims=True)
            total = part if total is None else total + part
            back_acc[at, :] += dot(grad, fc_ref[...], NT)
            out_acc[at, :] += dot(act, out_ref[...], NT)
        sums_ref[...] = total

    @pl.when(i < tiles)
    def _():
        work(shift_own_ref, fc_own_ref, out_own_ref)

    @pl.when(i >= tiles)
    def _():
        work(shift_sib_ref, fc_sib_ref, out_sib_ref)

    @pl.when(i == 2 * tiles - 1)
    def _():
        back_ref[...] = back_acc[...].astype(BF16)
        sent_ref[...] = out_acc[...].astype(BF16)


def feed(base, part, recv, cot, vectors, shift_own, shift_sib, own, sib, after=()):
    rows, width = base.shape
    hidden_cols = shift_own.shape[1]
    tile = min(512, hidden_cols)
    tiles = hidden_cols // tile
    whole = pl.BlockSpec((rows, width), lambda i: (0, 0))

    def low(i):
        return jnp.minimum(i, tiles - 1)

    def high(i):
        return jnp.maximum(i - tiles, 0)

    return pl.pallas_call(
        functools.partial(feed_kernel, tiles=tiles),
        grid=(2 * tiles,),
        in_specs=[
            whole,
            whole,
            whole,
            whole,
            pl.BlockSpec(vectors.shape, lambda i: (0, 0)),
            pl.BlockSpec((1, tile), lambda i: (0, low(i))),
            pl.BlockSpec((1, tile), lambda i: (0, high(i))),
            pl.BlockSpec((width, tile), lambda i: (0, low(i))),
            pl.BlockSpec((width, tile), lambda i: (0, tiles + low(i))),
            pl.BlockSpec((width, tile), lambda i: (0, high(i))),
            pl.BlockSpec((width, tile), lambda i: (0, tiles + high(i))),
        ]
        + [ANY_SPACE] * len(after),
        out_specs=[
            whole,
            whole,
            pl.BlockSpec((rows, tile), lambda i: (0, i)),
            pl.BlockSpec((rows, tile), lambda i: (0, i)),
            whole,
            whole,
            pl.BlockSpec((1, tile), lambda i: (0, i)),
        ],
        out_shape=[
            jax.ShapeDtypeStruct((rows, width), F32),
            jax.ShapeDtypeStruct((rows, width), BF16),
            jax.ShapeDtypeStruct((rows, 2 * hidden_cols), BF16),
            jax.ShapeDtypeStruct((rows, 2 * hidden_cols), BF16),
            jax.ShapeDtypeStruct((rows, width), BF16),
            jax.ShapeDtypeStruct((rows, width), BF16),
            jax.ShapeDtypeStruct((1, 2 * hidden_cols), F32),
        ],
        scratch_shapes=[pltpu.VMEM((rows, width), F32), pltpu.VMEM((rows, width), F32)],
        compiler_params=params(40),
        cost_estimate=cost(16),
        name="feed",
    )(
        base, part, recv, cot, vectors, shift_own, shift_sib, own, own, sib, sib, *after
    )


def swap_dp(value, mask):
    size = lax.axis_size("dp")
    return lax.ppermute(value, "dp", [(i, i ^ mask) for i in range(size)])


def gather_dp(shard, side_rows, after):
    size = lax.axis_size("dp")
    if size != 8:
        rows, cols = shard.shape[0] - side_rows, shard.shape[1]
        full = lax.all_gather(shard, "dp", axis=0)
        return jnp.concatenate(
            [full[:, :rows].reshape(-1, cols), full[:, rows:].reshape(-1, cols)], axis=0
        )
    pieces = {0: shard}
    for k in (6, 4, 2):
        pieces[k] = swap_dp(shard, k)
    for k in (0, 2, 4, 6):
        pieces[k + 1] = swap_dp(pieces[k], 1)
    after = after((pieces[6], pieces[4], pieces[2]))
    shares = [pieces[k] for k in range(size)]
    return place_shares(lax.axis_index("dp"), shares, side_rows, after)


def scatter_y(sent, parts):
    return swap_dp(sent, 1) if parts == 8 else None


def scatter_z(kept, sent, received, side, parts):
    if parts != 8:
        whole = jnp.concatenate([kept, sent.astype(F32)], axis=1)
        whole = whole.reshape(parts, -1, whole.shape[2])
        if side is not None:
            whole = jnp.concatenate([whole, side], axis=1)
        return [lax.psum_scatter(whole.astype(BF16), "dp", scatter_dimension=0)]
    sums = kept + received.astype(F32)
    if side is not None:
        sums = jnp.concatenate([sums, side], axis=1)
    z = lax.axis_index("dp") // 2
    terms = [lax.dynamic_index_in_dim(sums, z, 0, keepdims=False)]
    for k in (3, 2, 1):
        sent = lax.dynamic_index_in_dim(sums, z ^ k, 0, keepdims=False).astype(BF16)
        terms.append(swap_dp(sent, 2 * k))
    return terms


def local(
    inputs,
    qkv_weight,
    qv_bias,
    proj_weight,
    proj_bias,
    fc_weight,
    fc_bias,
    out_weight,
    out_bias,
    attn_norm_gain,
    attn_norm_bias,
    mlp_norm_gain,
    mlp_norm_bias,
    cotangent,
):
    width = inputs.shape[1]
    rows = inputs.shape[0]
    share = proj_bias.shape[0]
    parts = width // share
    head_cols = qkv_weight.shape[2]
    pairs = head_cols // PAIR
    qkv_cols = 3 * head_cols
    hidden_cols = fc_weight.shape[1]
    place = lax.axis_index("tensor")
    core = place % 2
    is_low = place < 2
    is_first = core == 0

    def pick_x(low, high):
        return jnp.where(is_low, low, high)

    mlp_shard = jnp.concatenate([fc_weight, out_weight.T], axis=1)
    mlp_all = lax.all_gather(mlp_shard, "dp", axis=0, tiled=True)
    qv_row = jnp.pad(qv_bias.reshape(-1), (0, share - qv_bias.size))
    vectors = jnp.stack(
        [
            proj_bias,
            out_bias,
            attn_norm_gain,
            attn_norm_bias,
            mlp_norm_gain,
            mlp_norm_bias,
            fc_bias,
            qv_row,
        ]
    )
    qkv_shard = jnp.transpose(
        qkv_weight.reshape(3, share, pairs, PAIR), (1, 2, 0, 3)
    ).reshape(share, qkv_cols)
    attn_shard = jnp.concatenate([qkv_shard, proj_weight.T], axis=1)
    side_rows = 16
    vectors = jnp.pad(
        vectors.reshape(1, -1), ((0, side_rows - 1), (0, attn_shard.shape[1] - vectors.size))
    )
    attn_shard = jnp.concatenate([attn_shard, vectors], axis=0)

    input_x_sent = swap_x(inputs)
    input_core = swap_core(inputs)
    cot_x = swap_x(cotangent)
    blocks = []

    def assemble(late):
        input_x = tie(input_x_sent, *late)
        input_far = swap_core(input_x)
        low, high = pick_x(inputs, input_x), pick_x(input_x, inputs)
        far_low, far_high = pick_x(input_core, input_far), pick_x(input_far, input_core)
        sequence = jnp.concatenate(
            [
                jnp.where(is_first, low, far_low),
                jnp.where(is_first, far_low, low),
                jnp.where(is_first, high, far_high),
                jnp.where(is_first, far_high, high),
            ],
            axis=0,
        )
        blocks.extend([low, high, sequence])
        return (sequence, cot_x)

    if parts == 8:
        attn_all = gather_dp(attn_shard, side_rows, assemble)
    else:
        attn_all = gather_dp(attn_shard, side_rows, ())
        assemble((attn_all,))
    input_low, input_high, sequence = blocks
    attn_sib = swap_core(attn_all)
    vectors = attn_all[width:].reshape(parts, side_rows, -1)[:, 0, : 8 * share]
    vectors = vectors.reshape(parts, 8, share).transpose(1, 0, 2).reshape(8, width)
    columns = vectors.astype(F32)
    out_shift, gain_one = columns[1:2], columns[2:3]
    fc_shift_own = columns[6:7]
    fc_shift_sib = attn_sib[width:].reshape(parts, side_rows, -1)[:, 0, 6 * share : 7 * share]
    fc_shift_sib = fc_shift_sib.reshape(1, width).astype(F32)
    qv_shift = (
        columns[7]
        .reshape(parts, share)[:, : share // 2]
        .reshape(parts, 2, share // 4)
        .transpose(1, 0, 2)
        .reshape(2, head_cols)
    )
    qkv_shift = jnp.stack([qv_shift[0], jnp.zeros_like(qv_shift[0]), qv_shift[1]])
    qkv_shift = qkv_shift.reshape(3, pairs, PAIR).transpose(1, 0, 2).reshape(1, qkv_cols)
    proj_both = jnp.concatenate(
        [
            attn_all[:width, qkv_cols : qkv_cols + head_cols],
            attn_sib[:width, qkv_cols : qkv_cols + head_cols],
        ],
        axis=1,
    )

    normed_one, qkv = project(sequence, columns, qkv_shift, attn_all, rows)
    cots = [pick_x(cotangent, cot_x), pick_x(cot_x, cotangent)]

    inputs_two = [input_low, input_high]
    mixed, totals, mixed_own, mixed_sib, parts_two, received_two = [], [], [], [], [], []
    for half in range(2):
        half_mixed, half_totals = attend(
            qkv, half * 2 * rows, 2 * rows, rows, after=tuple(parts_two)
        )
        mixed.append(half_mixed)
        totals.append(half_totals)
        two = half_mixed.reshape(2, rows, head_cols)
        mine = jnp.where(is_first, two[0], two[1])
        received = swap_core(jnp.where(is_first, two[1], two[0]))
        both = jnp.concatenate([mine, received], axis=1)
        mixed_own.append(mine)
        mixed_sib.append(received)
        part = dot(both, proj_both, NT).astype(BF16)
        parts_two.append(part)
        received_two.append(swap_x(part))
    mlp_all = tie(mlp_all, received_two[0], parts_two[1])
    mlp_sib = swap_core(mlp_all)
    residuals, normed_two, acts, grads_hidden, backs, out_parts = [], [], [], [], [], []
    fc_bias_sums = 0.0
    for half in range(2):
        residual, normed, act, grad_hidden, back, out_part, sums = feed(
            inputs_two[half],
            parts_two[half],
            received_two[half],
            cots[half],
            columns,
            fc_shift_own,
            fc_shift_sib,
            mlp_all,
            mlp_sib,
            after=(parts_two[1],),
        )
        residuals.append(residual)
        normed_two.append(normed)
        acts.append(act)
        grads_hidden.append(grad_hidden)
        backs.append(back)
        out_parts.append(out_part)
        fc_bias_sums = fc_bias_sums + sums[0]
    back_recv = [swap_x(back) for back in backs]

    sib_grads = feed_grads(
        normed_two, cots, grads_hidden, acts, hidden_cols, None, after=(back_recv[0],)
    )
    grad_mlp = feed_grads(normed_two, cots, grads_hidden, acts, 0, swap_core(sib_grads))
    mlp_sum = lax.psum_scatter(grad_mlp, "dp", scatter_dimension=0, tiled=True)

    grad_residuals, branches, grads_mixed = [], [], []
    for half in range(2):
        grad_residual, branch, grad_both, sums_two = norm_two(
            backs[half],
            back_recv[half],
            residuals[half],
            cots[half],
            columns,
            proj_both,
            after=(grad_mlp,) if half == 0 else (grad_mlp, low_grads),
        )
        grad_residuals.append(grad_residual)
        branches.append(branch)
        mine = grad_both[:, :head_cols]
        received = swap_core(grad_both[:, head_cols:])
        grads_mixed.append(
            jnp.concatenate(
                [jnp.where(is_first, mine, received), jnp.where(is_first, received, mine)], axis=0
            )
        )
        vec_two = sums_two if half == 0 else vec_two + sums_two
        if half == 0:
            low_grads, _ = attend_back(
                qkv, mixed[0], grads_mixed[0], totals[0], None, 0, rows, 0, pairs
            )
    proj_sib = dot(branches[0], mixed_sib[0], TN) + dot(branches[1], mixed_sib[1], TN)
    proj_received = swap_core(proj_sib.astype(BF16))

    out_sent = tie(pick_x(out_parts[1], out_parts[0]), low_grads)
    out_recv = swap_x(out_sent)

    y = lax.axis_index("dp") % 2 if parts == 8 else jnp.zeros((), jnp.int32)
    place_ids = jnp.stack([place // 2, core]).astype(jnp.int32)
    full_grads, grads_received, side_sums, exchanges = [], [], [], []
    after = ()
    for pair in range(pairs):
        grad_pair, pair_sums, grad_sent = attend_back(
            qkv,
            mixed[1],
            grads_mixed[1],
            totals[1],
            low_grads,
            2 * rows,
            rows,
            pair,
            1,
            after=after,
            core=core,
        )
        full_grads.append(grad_pair)
        side_sums.append(pair_sums)
        grads_received.append(swap_core(grad_sent))
        proj = (branches, mixed_own, proj_received) if pair == 0 else None
        if pair == 0:
            out_recv = tie(out_recv, grad_pair)
        arrived = () if pair == 0 or parts != 8 else (exchanges[-1][2],)
        kept, sent = weight_grads(y, normed_one, grad_pair, proj, after=arrived)
        received = scatter_y(sent, parts) if pair < pairs - 1 else None
        exchanges.append((kept, sent, received))
        after = (sent, out_recv)

    z_own, z_sent, vec_one = norm_one(
        place_ids,
        input_low,
        input_high,
        full_grads,
        grads_received,
        attn_all,
        attn_sib,
        after=(exchanges[-1][1],),
    )
    z_recv = swap_x(z_sent)
    vec_two = vec_two + swap_core(vec_two)
    fc_bias_grad = fc_bias_sums[:hidden_cols] + swap_core(fc_bias_sums[hidden_cols:])

    vec_grads = jnp.concatenate(
        [
            vec_two[:2],
            vec_one[:2],
            vec_two[2:4],
            fc_bias_grad[None],
            jnp.zeros((1, width), F32),
        ],
        axis=0,
    )
    vec_blocks = vec_grads.reshape(8, parts, share).transpose(1, 0, 2)
    vec_blocks = jnp.pad(vec_blocks, ((0, 0), (0, 0), (0, 3 * PAIR - share)))
    pair_rows = jnp.pad(jnp.concatenate(side_sums, axis=0), ((0, 8 - pairs), (0, 0)))
    side = jnp.concatenate(
        [vec_blocks, jnp.broadcast_to(pair_rows[None], (parts, 8, 3 * PAIR))], axis=1
    )
    if parts == 8:
        views = side.reshape((parts // 2, 2) + side.shape[1:])
        side_kept = lax.dynamic_index_in_dim(views, y, 1, keepdims=False)
        side_sent = lax.dynamic_index_in_dim(views, 1 - y, 1, keepdims=False)
        side = side_kept + swap_dp(side_sent, 1)
    terms = []
    for pair in range(pairs):
        kept, sent, received = exchanges[pair]
        last = pair == pairs - 1
        if last:
            received = scatter_y(tie(sent, z_sent), parts)
        terms.append(scatter_z(kept, sent, received, side if last else None, parts))

    out_recv = tie(out_recv, z_sent)
    out_mine = pick_x(out_parts[0], out_parts[1])
    outputs = (
        pick_x(residuals[0], residuals[1])
        + out_mine.astype(F32)
        + out_recv.astype(F32)
        + out_shift
    ).astype(BF16)
    fc_out = mlp_sum[:, :hidden_cols].astype(F32)
    out_out = mlp_sum[:, hidden_cols:].astype(F32).T

    unit, factor = normalize(inputs.astype(F32))
    z_recv = tie(z_recv, *[term for pair in terms for term in pair[1:]])
    z_own = z_own + z_recv.astype(F32)
    grad_inputs = (
        pick_x(grad_residuals[0], grad_residuals[1]) + norm_back(unit, factor, gain_one, z_own)
    ).astype(BF16)

    qkv_out, proj_out, six = finish(
        terms, share, head_cols, side_rows, after=(outputs, grad_inputs, fc_out, out_out)
    )
    one = six[2:4, :share]
    two = (
        one
        + swap_core(one)
        + swap_x(one)
        + lax.ppermute(one, "tensor", [(i, i ^ 3) for i in range(4)])
    )
    piece = share // 4
    start = lax.axis_index("dp") * piece
    mine = lax.dynamic_index_in_dim(six[8 : 8 + pairs], start // PAIR, 0, keepdims=False)
    qv_out = lax.dynamic_slice_in_dim(mine.reshape(3, PAIR), start % PAIR, piece, 1)[0::2]
    return (
        outputs,
        grad_inputs,
        qkv_out,
        qv_out,
        proj_out,
        six[0, :share],
        fc_out,
        six[6, :share],
        out_out,
        six[1, :share],
        two[0],
        two[1],
        six[4, :share],
        six[5, :share],
    )


def solution(mesh):
    rows = P(("dp", "tensor"), None)
    vector = P("dp")
    wide = P(("tensor", "dp"))
    weights = (
        P(None, "dp", "tensor"),
        P(None, ("tensor", "dp")),
        P("tensor", "dp"),
        vector,
        P("dp", "tensor"),
        wide,
        P("tensor", "dp"),
        vector,
        vector,
        vector,
        vector,
        vector,
    )
    return jax.shard_map(
        local,
        mesh=mesh,
        in_specs=(rows, *weights, rows),
        out_specs=(rows, rows, *weights),
        check_vma=False,
    )
```

```python
import functools

import jax
import jax.numpy as jnp
from jax import lax
from jax.experimental import pallas as pl
from jax.experimental.pallas import tpu as pltpu
from jax.sharding import PartitionSpec as P

HD = 64
PAIR = 2 * HD
EPSILON = 1e-05
NEGATIVE = -1e30
ROOT_TWO_PI = 0.7978845608028654
F32 = jnp.float32
BF16 = jnp.bfloat16
MIB = 1024 * 1024
SCALE = 0.25
ANY_SPACE = pl.BlockSpec(memory_space=pl.ANY)
SCALARS = pl.BlockSpec(memory_space=pltpu.SMEM)


def params():
    return pltpu.CompilerParams(vmem_limit_bytes=60 * MIB)


def cost(micros):
    return pl.CostEstimate(
        flops=int(micros * SCALE * 1.1e9),
        bytes_accessed=int(micros * SCALE * 1e6),
        transcendentals=0,
    )


def swap_x(value):
    return lax.ppermute(value, "tensor", [(0, 2), (2, 0), (1, 3), (3, 1)])


def swap_core(value):
    return lax.ppermute(value, "tensor", [(0, 1), (1, 0), (2, 3), (3, 2)])


def dot(a, b, contract, kind=F32):
    return lax.dot_general(a, b, (contract, ((), ())), preferred_element_type=kind)


NN = ((1,), (0,))
NT = ((1,), (1,))
TN = ((0,), (0,))


def normalize(values):
    average = jnp.mean(values, axis=-1, keepdims=True)
    centered = values - average
    spread = jnp.mean(centered * centered, axis=-1, keepdims=True)
    factor = lax.rsqrt(spread + EPSILON)
    return centered * factor, factor


def norm_back(unit, factor, gain, grad):
    scaled = grad * gain
    return factor * (
        scaled
        - jnp.mean(scaled, axis=-1, keepdims=True)
        - unit * jnp.mean(scaled * unit, axis=-1, keepdims=True)
    )


def gelu_both(values):
    squared = values * values
    bent = jnp.tanh(ROOT_TWO_PI * values * (1.0 + 0.044715 * squared))
    half = 0.5 * (1.0 + bent)
    slope = half + 0.5 * values * (1.0 - bent * bent) * ROOT_TWO_PI * (
        1.0 + 3.0 * 0.044715 * squared
    )
    return values * half, slope


def split_heads(block):
    first = lax.broadcasted_iota(jnp.int32, block.shape, 1) < HD
    return [jnp.where(first, block, 0.0).astype(BF16), jnp.where(first, 0.0, block).astype(BF16)]


def attend_kernel(qkv_ref, *rest, row0, block):
    mixed_ref, total_ref, kept, acc = rest[-4:]
    count = mixed_ref.shape[0] // block
    first = lax.broadcasted_iota(jnp.int32, (PAIR, block), 0) < HD
    causal = lax.broadcasted_iota(jnp.int32, (block, block), 0) <= lax.broadcasted_iota(
        jnp.int32, (block, block), 1
    )
    for i in range(count):
        start = row0 + i * block
        heads = split_heads(qkv_ref[pl.ds(start, block), 0:PAIR].astype(F32) * (HD**-0.5))
        keys = qkv_ref[pl.ds(start, block), PAIR : 2 * PAIR]
        tops = []
        for h in range(2):
            scores = jnp.where(causal, dot(keys, heads[h], NT), NEGATIVE)
            kept[h, pl.ds(start, block), :] = scores
            tops.append(jnp.max(scores, axis=0, keepdims=True))

        def score_step(j, tops):
            at = pl.multiple_of(j * block, block)
            tile_keys = qkv_ref[pl.ds(at, block), PAIR : 2 * PAIR]
            found = []
            for h in range(2):
                scores = dot(tile_keys, heads[h], NT)
                kept[h, pl.ds(at, block), :] = scores
                found.append(jnp.maximum(tops[h], jnp.max(scores, axis=0, keepdims=True)))
            return tuple(found)

        tops = lax.fori_loop(0, start // block, score_step, tuple(tops))
        acc[...] = jnp.zeros(acc.shape, F32)

        def value_step(j, sums):
            at = pl.multiple_of(j * block, block)
            tile_values = qkv_ref[pl.ds(at, block), 2 * PAIR : 3 * PAIR]
            found = []
            for h in range(2):
                powers = jnp.exp(kept[h, pl.ds(at, block), :] - tops[h])
                found.append(sums[h] + jnp.sum(powers, axis=0, keepdims=True))
                acc[h] += dot(powers.astype(BF16), tile_values, TN)
            return tuple(found)

        zero = jnp.zeros((1, block), F32)
        sums = lax.fori_loop(0, start // block + 1, value_step, (zero, zero))
        inverse = jnp.transpose(jnp.where(first, 1.0 / sums[0], 1.0 / sums[1]))
        lane = lax.broadcasted_iota(jnp.int32, (block, PAIR), 1) < HD
        local = slice(i * block, (i + 1) * block)
        mixed_ref[local, :] = (jnp.where(lane, acc[0], acc[1]) * inverse).astype(BF16)
        for h in range(2):
            total_ref[0, h : h + 1, local] = tops[h] + jnp.log(sums[h])


def attend(qkv, row0, rows, block, after=()):
    pairs = qkv.shape[1] // (3 * PAIR)
    return pl.pallas_call(
        functools.partial(attend_kernel, row0=row0, block=block),
        grid=(pairs,),
        in_specs=[pl.BlockSpec((row0 + rows, 3 * PAIR), lambda j: (0, j))]
        + [ANY_SPACE] * len(after),
        out_specs=[
            pl.BlockSpec((rows, PAIR), lambda j: (0, j)),
            pl.BlockSpec((1, 2, rows), lambda j: (j, 0, 0)),
        ],
        out_shape=[
            jax.ShapeDtypeStruct((rows, pairs * PAIR), BF16),
            jax.ShapeDtypeStruct((pairs, 2, rows), F32),
        ],
        scratch_shapes=[
            pltpu.VMEM((2, row0 + rows, block), F32),
            pltpu.VMEM((2, block, PAIR), F32),
        ],
        compiler_params=params(),
        cost_estimate=cost(16 if row0 else 6),
        name="attend_%d" % row0,
    )(qkv, *after)


def attend_back_kernel(
    core_ref, qkv_ref, mixed_ref, grad_ref, total_ref, *rest, row0, block, has_before
):
    before_ref = rest[0]
    sent_ref = None
    if has_before:
        out_ref, sums_ref, sent_ref, key_acc, value_acc, query_acc = rest[-6:]
    else:
        out_ref, sums_ref, key_acc, value_acc, query_acc = rest[-5:]
    rows = mixed_ref.shape[0]
    count = rows // block
    lane = lax.broadcasted_iota(jnp.int32, (block, PAIR), 1)
    first = lane < HD
    causal = lax.broadcasted_iota(jnp.int32, (block, block), 0) <= lax.broadcasted_iota(
        jnp.int32, (block, block), 1
    )
    if has_before:
        key_acc[0:row0, :] = before_ref[:, PAIR : 2 * PAIR]
        value_acc[0:row0, :] = before_ref[:, 2 * PAIR : 3 * PAIR]
        key_acc[row0:, :] = jnp.zeros((rows, PAIR), F32)
        value_acc[row0:, :] = jnp.zeros((rows, PAIR), F32)
    else:
        key_acc[...] = jnp.zeros(key_acc.shape, F32)
        value_acc[...] = jnp.zeros(value_acc.shape, F32)
    for i in range(count):
        start = row0 + i * block
        local = slice(i * block, (i + 1) * block)
        query_heads = split_heads(
            qkv_ref[pl.ds(start, block), 0:PAIR].astype(F32) * (HD**-0.5)
        )
        grads = grad_ref[local, :].astype(F32)
        grad_heads = split_heads(grads)
        inner = jnp.transpose(grads * mixed_ref[local, :].astype(F32))
        total_rows = [total_ref[0, h : h + 1, local] for h in range(2)]
        inner_rows = [
            jnp.sum(inner[h * HD : (h + 1) * HD, :], axis=0, keepdims=True) for h in range(2)
        ]

        def tile(at, masked):
            tile_keys = qkv_ref[pl.ds(at, block), PAIR : 2 * PAIR]
            tile_values = qkv_ref[pl.ds(at, block), 2 * PAIR : 3 * PAIR]
            key_sum, value_sum = None, None
            for h in range(2):
                scores = dot(tile_keys, query_heads[h], NT)
                weights = jnp.exp(scores - total_rows[h])
                if masked:
                    weights = jnp.where(causal, weights, 0.0)
                grad_weights = dot(tile_values, grad_heads[h], NT)
                grad_scores = (weights * (grad_weights - inner_rows[h])).astype(BF16)
                value_part = dot(weights.astype(BF16), grad_heads[h], NN)
                key_part = dot(grad_scores, query_heads[h], NN)
                query_part = dot(grad_scores, tile_keys, TN)
                key_sum = key_part if key_sum is None else key_sum + key_part
                value_sum = value_part if value_sum is None else value_sum + value_part
                if masked:
                    query_acc[h] = query_part
                else:
                    query_acc[h] += query_part
            key_acc[pl.ds(at, block), :] += key_sum
            value_acc[pl.ds(at, block), :] += value_sum

        tile(start, True)

        def step(j, carry):
            tile(pl.multiple_of(j * block, block), False)
            return carry

        if start:
            lax.fori_loop(0, start // block, step, 0)
        query_grad = jnp.where(first, query_acc[0], query_acc[1]) * (HD**-0.5)
        out_ref[start : start + block, 0:PAIR] = query_grad.astype(out_ref.dtype)
    if has_before:
        out_ref[0:row0, 0:PAIR] = before_ref[:, 0:PAIR].astype(out_ref.dtype)
    out_ref[:, PAIR : 2 * PAIR] = key_acc[...].astype(out_ref.dtype)
    out_ref[:, 2 * PAIR : 3 * PAIR] = value_acc[...].astype(out_ref.dtype)
    sums_ref[...] = jnp.sum(out_ref[...].astype(F32), axis=0, keepdims=True)
    if has_before:
        size = sent_ref.shape[0] // 2
        for half in range(2):
            at = pl.multiple_of((2 * half + 1 - core_ref[0]) * size, size)
            sent_ref[half * size : (half + 1) * size, :] = out_ref[pl.ds(at, size), :]


def attend_back(qkv, mixed, grads, totals, before, row0, block, pair, pairs, after=(), core=None):
    rows = mixed.shape[0]
    extent = row0 + rows
    narrow = pl.BlockSpec((rows, PAIR), lambda j: (0, pair + j))
    in_specs = [
        SCALARS,
        pl.BlockSpec((extent, 3 * PAIR), lambda j: (0, pair + j)),
        narrow,
        narrow,
        pl.BlockSpec((1, 2, rows), lambda j: (pair + j, 0, 0)),
    ]
    core = jnp.zeros((), jnp.int32) if core is None else core
    operands = [core.reshape(1).astype(jnp.int32), qkv, mixed, grads, totals]
    if before is not None:
        in_specs.append(pl.BlockSpec((row0, 3 * PAIR), lambda j: (0, pair + j)))
        operands.append(before)
    in_specs += [ANY_SPACE] * len(after)
    return pl.pallas_call(
        functools.partial(
            attend_back_kernel, row0=row0, block=block, has_before=before is not None
        ),
        grid=(pairs,),
        in_specs=in_specs,
        out_specs=[
            pl.BlockSpec((extent, 3 * PAIR), lambda j: (0, j)),
            pl.BlockSpec((1, 3 * PAIR), lambda j: (0, j)),
        ]
        + ([] if before is None else [pl.BlockSpec((extent // 2, 3 * PAIR), lambda j: (0, j))]),
        out_shape=[
            jax.ShapeDtypeStruct((extent, pairs * 3 * PAIR), F32 if before is None else BF16),
            jax.ShapeDtypeStruct((1, pairs * 3 * PAIR), F32),
        ]
        + (
            []
            if before is None
            else [jax.ShapeDtypeStruct((extent // 2, pairs * 3 * PAIR), BF16)]
        ),
        scratch_shapes=[
            pltpu.VMEM((extent, PAIR), F32),
            pltpu.VMEM((extent, PAIR), F32),
            pltpu.VMEM((2, block, PAIR), F32),
        ],
        compiler_params=params(),
        cost_estimate=cost(5.5 * pairs if before is None else 13 * pairs),
        name="attend_back_%d_%d" % (row0, pair),
    )(*operands, *after)


def norm_two_kernel(
    back_ref, recv_ref, residual_ref, cot_ref, vec_ref, proj_ref, *rest, steps
):
    grad_ref, branch_ref, both_ref, sums_ref = rest[-4:]
    z = back_ref[...].astype(F32) + recv_ref[...].astype(F32)
    unit, factor = normalize(residual_ref[...])
    cot = cot_ref[...].astype(F32)
    grad = cot + norm_back(unit, factor, vec_ref[4:5, :], z)
    grad_ref[...] = grad
    branch = grad.astype(BF16)
    branch_ref[...] = branch
    both_ref[...] = dot(branch, proj_ref[...], NN).astype(BF16)

    @pl.when(pl.program_id(0) == 0)
    def _():
        sums_ref[...] = jnp.zeros(sums_ref.shape, F32)

    for at, part in enumerate((branch.astype(F32), cot, z * unit, z)):
        sums_ref[at : at + 1, :] += jnp.sum(part, axis=0, keepdims=True)


def norm_two(back, recv, residual, cot, vectors, proj, after=()):
    rows, width = back.shape
    steps = 2
    block = rows // steps
    strip = pl.BlockSpec((block, width), lambda i: (i, 0))
    return pl.pallas_call(
        functools.partial(norm_two_kernel, steps=steps),
        grid=(steps,),
        in_specs=[
            strip,
            strip,
            strip,
            strip,
            pl.BlockSpec(vectors.shape, lambda i: (0, 0)),
            pl.BlockSpec(proj.shape, lambda i: (0, 0)),
        ]
        + [ANY_SPACE] * len(after),
        out_specs=[
            strip,
            strip,
            pl.BlockSpec((block, proj.shape[1]), lambda i: (i, 0)),
            pl.BlockSpec((8, width), lambda i: (0, 0)),
        ],
        out_shape=[
            jax.ShapeDtypeStruct((rows, width), F32),
            jax.ShapeDtypeStruct((rows, width), BF16),
            jax.ShapeDtypeStruct((rows, proj.shape[1]), BF16),
            jax.ShapeDtypeStruct((8, width), F32),
        ],
        compiler_params=params(),
        cost_estimate=cost(4),
        name="norm_two",
    )(back, recv, residual, cot, vectors, proj, *after)


def norm_one_kernel(place_ref, low_ref, high_ref, *refs, terms):
    grads, weights = refs[:terms], refs[terms : 2 * terms]
    own_ref, sent_ref, sums_ref = refs[-3:]
    i = pl.program_id(0)
    z = None
    for grad_ref, weight_ref in zip(grads, weights):
        part = dot(grad_ref[...], weight_ref[...], NT)
        z = part if z is None else z + part
    rows = jnp.where(i == 0, low_ref[...].astype(F32), high_ref[...].astype(F32))
    unit, _ = normalize(rows)

    @pl.when(i == 0)
    def _():
        sums_ref[...] = jnp.zeros(sums_ref.shape, F32)

    sums_ref[0:1, :] += jnp.sum(z * unit, axis=0, keepdims=True)
    sums_ref[1:2, :] += jnp.sum(z, axis=0, keepdims=True)

    @pl.when(i == place_ref[0])
    def _():
        own_ref[...] = z

    @pl.when(i != place_ref[0])
    def _():
        sent_ref[...] = z.astype(BF16)


def norm_one(places, low, high, full, received, own_weights, sib_weights, after=()):
    rows, width = low.shape
    pairs = len(full)
    cols = full[0].shape[1]
    whole = pl.BlockSpec((rows, width), lambda i, at: (0, 0))
    weight_specs = [
        pl.BlockSpec((width, cols), functools.partial(lambda pair, i, at: (0, pair), pair))
        for pair in range(pairs)
    ]
    return pl.pallas_call(
        functools.partial(norm_one_kernel, terms=2 * pairs),
        grid_spec=pltpu.PrefetchScalarGridSpec(
            num_scalar_prefetch=1,
            grid=(2,),
            in_specs=[whole, whole]
            + [pl.BlockSpec((rows, cols), lambda i, at: (2 * i + at[1], 0))] * pairs
            + [pl.BlockSpec((rows, cols), lambda i, at: (i, 0))] * pairs
            + weight_specs * 2
            + [ANY_SPACE] * len(after),
            out_specs=[whole, whole, pl.BlockSpec((8, width), lambda i, at: (0, 0))],
        ),
        out_shape=[
            jax.ShapeDtypeStruct((rows, width), F32),
            jax.ShapeDtypeStruct((rows, width), BF16),
            jax.ShapeDtypeStruct((8, width), F32),
        ],
        compiler_params=params(),
        cost_estimate=cost(8),
        name="norm_one",
    )(
        places,
        low,
        high,
        *full,
        *received,
        *[own_weights] * pairs,
        *[sib_weights] * pairs,
        *after,
    )


def tie_kernel(value_ref, *rest):
    pass


def tie(value, *after):
    return pl.pallas_call(
        tie_kernel,
        in_specs=[ANY_SPACE] * (1 + len(after)),
        out_specs=ANY_SPACE,
        out_shape=jax.ShapeDtypeStruct(value.shape, value.dtype),
        input_output_aliases={0: 0},
        cost_estimate=cost(0.1),
        name="tie",
    )(value, *after)


def place_kernel(me_ref, *refs, parts, side_rows):
    full_ref = refs[-1]
    rows = refs[0].shape[0] - side_rows
    for k in range(parts):
        at = lax.bitwise_xor(me_ref[0], k)
        full_ref[pl.ds(pl.multiple_of(at * rows, rows), rows), :] = refs[k][0:rows, :]
        if side_rows:
            side = pl.multiple_of(parts * rows + at * side_rows, side_rows)
            full_ref[pl.ds(side, side_rows), :] = refs[k][rows:, :]


def place_shares(me, pieces, side_rows, after):
    total, cols = pieces[0].shape
    parts, kind = len(pieces), pieces[0].dtype
    return pl.pallas_call(
        functools.partial(place_kernel, parts=parts, side_rows=side_rows),
        grid=(1,),
        in_specs=[SCALARS]
        + [pl.BlockSpec((total, cols), lambda i: (0, 0))] * parts
        + [ANY_SPACE] * len(after),
        out_specs=pl.BlockSpec((parts * total, cols), lambda i: (0, 0)),
        out_shape=jax.ShapeDtypeStruct((parts * total, cols), kind),
        compiler_params=params(),
        cost_estimate=cost(3),
        name="place_shares",
    )(me.reshape(1).astype(jnp.int32), *pieces, *after)


def feed_grads_kernel(*refs, tiles, received):
    normed, cots, grads, acts = refs[0:2], refs[2:4], refs[4:6], refs[6:8]
    out_ref = refs[-1]
    i = pl.program_id(0)

    def work(left, right):
        total = dot(left[0][...], right[0][...], TN) + dot(left[1][...], right[1][...], TN)
        if received:
            total = total + refs[8][...].astype(F32)
        out_ref[...] = total.astype(BF16)

    @pl.when(i < tiles)
    def _():
        work(normed, grads)

    @pl.when(i >= tiles)
    def _():
        work(cots, acts)


def feed_grads(normed, cots, grads, acts, first, received, after=()):
    rows, width = normed[0].shape
    hidden_cols = grads[0].shape[1] // 2
    tile = min(512, hidden_cols)
    tiles = hidden_cols // tile
    base = first // tile
    whole = pl.BlockSpec((rows, width), lambda i: (0, 0))
    grad_spec = pl.BlockSpec((rows, tile), lambda i: (0, base + jnp.minimum(i, tiles - 1)))
    act_spec = pl.BlockSpec((rows, tile), lambda i: (0, base + jnp.maximum(i - tiles, 0)))
    out_spec = pl.BlockSpec((width, tile), lambda i: (0, i))
    return pl.pallas_call(
        functools.partial(feed_grads_kernel, tiles=tiles, received=received is not None),
        grid=(2 * tiles,),
        in_specs=[whole] * 4
        + [grad_spec] * 2
        + [act_spec] * 2
        + ([] if received is None else [out_spec])
        + [ANY_SPACE] * len(after),
        out_specs=out_spec,
        out_shape=jax.ShapeDtypeStruct((width, 2 * hidden_cols), BF16),
        compiler_params=params(),
        cost_estimate=cost(6),
        name="feed_grads",
    )(*normed, *cots, *grads, *acts, *([] if received is None else [received]), *after)


def weight_grads_kernel(y_ref, normed_ref, grad_ref, *refs, with_proj):
    kept_ref, sent_ref = refs[-2:]
    share = kept_ref.shape[1]
    total = dot(normed_ref[...], grad_ref[...], TN)
    if with_proj:
        low_ref, high_ref, low_mixed_ref, high_mixed_ref, recv_ref = refs[:5]
        proj = dot(low_ref[...], low_mixed_ref[...], TN) + dot(
            high_ref[...], high_mixed_ref[...], TN
        )
        proj = proj + recv_ref[...].astype(F32)
        total = jnp.concatenate([total, proj], axis=1)
    even, odd = total[:share], total[share:]
    stays = y_ref[0] == 0
    kept_ref[0] = jnp.where(stays, even, odd)
    sent_ref[0] = jnp.where(stays, odd, even).astype(BF16)


def weight_grads(y, normed, grads, proj, after=()):
    length, width = normed.shape
    cols = grads.shape[1]
    steps, share = 4, width // 8
    in_specs = [
        SCALARS,
        pl.BlockSpec((length, 2 * share), lambda i: (0, i)),
        pl.BlockSpec((length, cols), lambda i: (0, 0)),
    ]
    operands = [y.reshape(1).astype(jnp.int32), normed, grads]
    total = cols
    if proj is not None:
        branches, mixed, received = proj
        rows, head_cols = mixed[0].shape
        total += head_cols
        in_specs += [pl.BlockSpec((rows, 2 * share), lambda i: (0, i))] * 2
        in_specs += [pl.BlockSpec((rows, head_cols), lambda i: (0, 0))] * 2
        in_specs += [pl.BlockSpec((2 * share, head_cols), lambda i: (i, 0))]
        operands += [*branches, *mixed, received]
    return pl.pallas_call(
        functools.partial(weight_grads_kernel, with_proj=proj is not None),
        grid=(steps,),
        in_specs=in_specs + [ANY_SPACE] * len(after),
        out_specs=[pl.BlockSpec((1, share, total), lambda i: (i, 0, 0))] * 2,
        out_shape=[
            jax.ShapeDtypeStruct((steps, share, total), F32),
            jax.ShapeDtypeStruct((steps, share, total), BF16),
        ],
        compiler_params=params(),
        cost_estimate=cost(4),
        name="weight_grads",
    )(*operands, *after)


def finish_kernel(*refs, pairs, counts):
    qkv_ref, proj_ref, side_ref, fc_ref, out_ref = refs[-5:]
    feed_ref = refs[sum(counts)]
    hidden_cols = fc_ref.shape[1]
    fc_ref[...] = feed_ref[:, :hidden_cols].astype(F32)
    out_ref[...] = jnp.transpose(feed_ref[:, hidden_cols:].astype(F32))
    at = 0
    for pair in range(pairs):
        total = refs[at][...].astype(F32)
        for part in range(1, counts[pair]):
            total = total + refs[at + part][...].astype(F32)
        at += counts[pair]
        share = qkv_ref.shape[1]
        for j in range(3):
            qkv_ref[j, :, pair * PAIR : (pair + 1) * PAIR] = total[:share, j * PAIR : (j + 1) * PAIR]
        if pair == 0:
            proj_ref[...] = jnp.transpose(total[:share, 3 * PAIR :])
        if pair == pairs - 1:
            side_ref[...] = total[share:, : 3 * PAIR]


def finish(terms, feed_sum, share, head_cols, side_rows, after=()):
    pairs = len(terms)
    flat = [term for pair in terms for term in pair]
    hidden_cols = feed_sum.shape[1] // 2
    return pl.pallas_call(
        functools.partial(
            finish_kernel, pairs=pairs, counts=[len(pair) for pair in terms]
        ),
        grid=(1,),
        in_specs=[pl.BlockSpec(term.shape, lambda i: (0, 0)) for term in flat + [feed_sum]]
        + [ANY_SPACE] * len(after),
        out_specs=[
            pl.BlockSpec((3, share, head_cols), lambda i: (0, 0, 0)),
            pl.BlockSpec((head_cols, share), lambda i: (0, 0)),
            pl.BlockSpec((side_rows, 3 * PAIR), lambda i: (0, 0)),
            pl.BlockSpec((share, hidden_cols), lambda i: (0, 0)),
            pl.BlockSpec((hidden_cols, share), lambda i: (0, 0)),
        ],
        out_shape=[
            jax.ShapeDtypeStruct((3, share, head_cols), F32),
            jax.ShapeDtypeStruct((head_cols, share), F32),
            jax.ShapeDtypeStruct((side_rows, 3 * PAIR), F32),
            jax.ShapeDtypeStruct((share, hidden_cols), F32),
            jax.ShapeDtypeStruct((hidden_cols, share), F32),
        ],
        compiler_params=params(),
        cost_estimate=cost(3),
        name="finish",
    )(*flat, feed_sum, *after)


def project_kernel(rows_ref, vec_ref, shift_ref, weight_ref, *rest):
    normed_ref, out_ref = rest[-2:]
    unit, _ = normalize(rows_ref[...].astype(F32))
    normed_ref[...] = (unit * vec_ref[2:3, :] + vec_ref[3:4, :]).astype(BF16)
    out_ref[...] = (dot(normed_ref[...], weight_ref[...], NN) + shift_ref[...]).astype(BF16)


def project(sequence, vectors, shift, weights, block, after=()):
    length, width = sequence.shape
    cols = shift.shape[1]
    return pl.pallas_call(
        project_kernel,
        grid=(length // block,),
        in_specs=[
            pl.BlockSpec((block, width), lambda i: (i, 0)),
            pl.BlockSpec(vectors.shape, lambda i: (0, 0)),
            pl.BlockSpec(shift.shape, lambda i: (0, 0)),
            pl.BlockSpec((width, cols), lambda i: (0, 0)),
        ]
        + [ANY_SPACE] * len(after),
        out_specs=[
            pl.BlockSpec((block, width), lambda i: (i, 0)),
            pl.BlockSpec((block, cols), lambda i: (i, 0)),
        ],
        out_shape=[
            jax.ShapeDtypeStruct((length, width), BF16),
            jax.ShapeDtypeStruct((length, cols), BF16),
        ],
        compiler_params=params(),
        cost_estimate=cost(6),
        name="project",
    )(sequence, vectors, shift, weights, *after)


def feed_kernel(
    base_ref,
    part_ref,
    recv_ref,
    cot_ref,
    vec_ref,
    shift_own_ref,
    shift_sib_ref,
    fc_own_ref,
    out_own_ref,
    fc_sib_ref,
    out_sib_ref,
    *rest,
    tiles,
):
    residual_ref, normed_ref, act_ref, grad_ref, back_ref, sent_ref, sums_ref = rest[-9:-2]
    back_acc, out_acc = rest[-2:]
    i = pl.program_id(0)
    rows = base_ref.shape[0]

    @pl.when(i == 0)
    def _():
        residual = (
            base_ref[...].astype(F32)
            + part_ref[...].astype(F32)
            + recv_ref[...].astype(F32)
            + vec_ref[0:1, :]
        )
        residual_ref[...] = residual
        unit, _ = normalize(residual)
        normed_ref[...] = (unit * vec_ref[4:5, :] + vec_ref[5:6, :]).astype(BF16)
        back_acc[...] = jnp.zeros(back_acc.shape, F32)
        out_acc[...] = jnp.zeros(out_acc.shape, F32)

    def work(shift_ref, fc_ref, out_ref):
        step = rows // 2
        total = None
        for r in range(2):
            at = slice(r * step, (r + 1) * step)
            hidden = dot(normed_ref[at, :], fc_ref[...], NN) + shift_ref[...]
            grad_act = dot(cot_ref[at, :], out_ref[...], NN)
            act, slope = gelu_both(hidden)
            act = act.astype(BF16)
            grad = (grad_act * slope).astype(BF16)
            act_ref[at, :] = act
            grad_ref[at, :] = grad
            part = jnp.sum(grad.astype(F32), axis=0, keepdims=True)
            total = part if total is None else total + part
            back_acc[at, :] += dot(grad, fc_ref[...], NT)
            out_acc[at, :] += dot(act, out_ref[...], NT)
        sums_ref[...] = total

    @pl.when(i < tiles)
    def _():
        work(shift_own_ref, fc_own_ref, out_own_ref)

    @pl.when(i >= tiles)
    def _():
        work(shift_sib_ref, fc_sib_ref, out_sib_ref)

    @pl.when(i == 2 * tiles - 1)
    def _():
        back_ref[...] = back_acc[...].astype(BF16)
        sent_ref[...] = out_acc[...].astype(BF16)


def feed(base, part, recv, cot, vectors, shift_own, shift_sib, own, sib, after=()):
    rows, width = base.shape
    hidden_cols = shift_own.shape[1]
    tile = min(512, hidden_cols)
    tiles = hidden_cols // tile
    whole = pl.BlockSpec((rows, width), lambda i: (0, 0))

    def low(i):
        return jnp.minimum(i, tiles - 1)

    def high(i):
        return jnp.maximum(i - tiles, 0)

    return pl.pallas_call(
        functools.partial(feed_kernel, tiles=tiles),
        grid=(2 * tiles,),
        in_specs=[
            whole,
            whole,
            whole,
            whole,
            pl.BlockSpec(vectors.shape, lambda i: (0, 0)),
            pl.BlockSpec((1, tile), lambda i: (0, low(i))),
            pl.BlockSpec((1, tile), lambda i: (0, high(i))),
            pl.BlockSpec((width, tile), lambda i: (0, low(i))),
            pl.BlockSpec((width, tile), lambda i: (0, tiles + low(i))),
            pl.BlockSpec((width, tile), lambda i: (0, high(i))),
            pl.BlockSpec((width, tile), lambda i: (0, tiles + high(i))),
        ]
        + [ANY_SPACE] * len(after),
        out_specs=[
            whole,
            whole,
            pl.BlockSpec((rows, tile), lambda i: (0, i)),
            pl.BlockSpec((rows, tile), lambda i: (0, i)),
            whole,
            whole,
            pl.BlockSpec((1, tile), lambda i: (0, i)),
        ],
        out_shape=[
            jax.ShapeDtypeStruct((rows, width), F32),
            jax.ShapeDtypeStruct((rows, width), BF16),
            jax.ShapeDtypeStruct((rows, 2 * hidden_cols), BF16),
            jax.ShapeDtypeStruct((rows, 2 * hidden_cols), BF16),
            jax.ShapeDtypeStruct((rows, width), BF16),
            jax.ShapeDtypeStruct((rows, width), BF16),
            jax.ShapeDtypeStruct((1, 2 * hidden_cols), F32),
        ],
        scratch_shapes=[pltpu.VMEM((rows, width), F32), pltpu.VMEM((rows, width), F32)],
        compiler_params=params(),
        cost_estimate=cost(16),
        name="feed",
    )(
        base, part, recv, cot, vectors, shift_own, shift_sib, own, own, sib, sib, *after
    )


def swap_dp(value, mask):
    size = lax.axis_size("dp")
    return lax.ppermute(value, "dp", [(i, i ^ mask) for i in range(size)])


def gather_z(shard):
    return {k: swap_dp(shard, k) for k in (6, 4, 2)}


def gather_whole(shard, side_rows):
    rows, cols = shard.shape[0] - side_rows, shard.shape[1]
    full = lax.all_gather(shard, "dp", axis=0)
    return jnp.concatenate(
        [full[:, :rows].reshape(-1, cols), full[:, rows:].reshape(-1, cols)], axis=0
    )


def scatter_y(sent, parts):
    return swap_dp(sent, 1) if parts == 8 else None


def scatter_z(kept, sent, received, side, parts):
    if parts != 8:
        whole = jnp.concatenate([kept, sent.astype(F32)], axis=1)
        whole = whole.reshape(parts, -1, whole.shape[2])
        if side is not None:
            whole = jnp.concatenate([whole, side], axis=1)
        return [lax.psum_scatter(whole.astype(BF16), "dp", scatter_dimension=0)]
    sums = kept + received.astype(F32)
    if side is not None:
        sums = jnp.concatenate([sums, side], axis=1)
    z = lax.axis_index("dp") // 2
    terms = [lax.dynamic_index_in_dim(sums, z, 0, keepdims=False)]
    for k in (3, 2, 1):
        sent = lax.dynamic_index_in_dim(sums, z ^ k, 0, keepdims=False).astype(BF16)
        terms.append(swap_dp(sent, 2 * k))
    return terms


def local(
    inputs,
    qkv_weight,
    qv_bias,
    proj_weight,
    proj_bias,
    fc_weight,
    fc_bias,
    out_weight,
    out_bias,
    attn_norm_gain,
    attn_norm_bias,
    mlp_norm_gain,
    mlp_norm_bias,
    cotangent,
):
    width = inputs.shape[1]
    rows = inputs.shape[0]
    share = proj_bias.shape[0]
    parts = width // share
    head_cols = qkv_weight.shape[2]
    pairs = head_cols // PAIR
    qkv_cols = 3 * head_cols
    hidden_cols = fc_weight.shape[1]
    place = lax.axis_index("tensor")
    core = place % 2
    is_low = place < 2
    is_first = core == 0

    def pick_x(low, high):
        return jnp.where(is_low, low, high)

    mlp_shard = jnp.concatenate([fc_weight, out_weight.T], axis=1)
    qv_row = jnp.pad(qv_bias.reshape(-1), (0, share - qv_bias.size))
    vectors = jnp.stack(
        [
            proj_bias,
            out_bias,
            attn_norm_gain,
            attn_norm_bias,
            mlp_norm_gain,
            mlp_norm_bias,
            fc_bias,
            qv_row,
        ]
    )
    qkv_shard = jnp.transpose(
        qkv_weight.reshape(3, share, pairs, PAIR), (1, 2, 0, 3)
    ).reshape(share, qkv_cols)
    attn_shard = jnp.concatenate([qkv_shard, proj_weight.T], axis=1)
    side_rows = 16
    vectors = jnp.pad(
        vectors.reshape(1, -1), ((0, side_rows - 1), (0, attn_shard.shape[1] - vectors.size))
    )
    attn_shard = jnp.concatenate([attn_shard, vectors], axis=0)

    input_x_sent = swap_x(inputs)
    input_core = swap_core(inputs)
    cot_x = swap_x(cotangent)
    blocks = []

    def assemble(late):
        input_x = tie(input_x_sent, *late)
        input_far = swap_core(input_x)
        low, high = pick_x(inputs, input_x), pick_x(input_x, inputs)
        far_low, far_high = pick_x(input_core, input_far), pick_x(input_far, input_core)
        sequence = jnp.concatenate(
            [
                jnp.where(is_first, low, far_low),
                jnp.where(is_first, far_low, low),
                jnp.where(is_first, high, far_high),
                jnp.where(is_first, far_high, high),
            ],
            axis=0,
        )
        blocks.extend([low, high, sequence])
        return (sequence, cot_x)

    if parts == 8:
        shares = {0: attn_shard, **gather_z(attn_shard)}
        behind = (shares[6], shares[4], shares[2])
        mlp_shares = {0: mlp_shard, 1: swap_dp(mlp_shard, 1)}
        mlp_shares.update(gather_z(tie(mlp_shard, *behind)))
        for k in (0, 2, 4, 6):
            shares[k + 1] = swap_dp(shares[k], 1)
        for k in (2, 4):
            mlp_shares[k + 1] = swap_dp(mlp_shares[k], 1)
        attn_all = place_shares(
            lax.axis_index("dp"),
            [shares[k] for k in range(parts)],
            side_rows,
            assemble(behind) + (mlp_shares[1], mlp_shares[2], mlp_shares[4]),
        )
        early = (mlp_shares[3], mlp_shares[5], mlp_shares[6])
    else:
        attn_all = gather_whole(attn_shard, side_rows)
        assemble((attn_all,))
        early = ()
    input_low, input_high, sequence = blocks
    attn_sib = swap_core(attn_all)
    vectors = attn_all[width:].reshape(parts, side_rows, -1)[:, 0, : 8 * share]
    vectors = vectors.reshape(parts, 8, share).transpose(1, 0, 2).reshape(8, width)
    columns = vectors.astype(F32)
    out_shift, gain_one = columns[1:2], columns[2:3]
    fc_shift_own = columns[6:7]
    fc_shift_sib = attn_sib[width:].reshape(parts, side_rows, -1)[:, 0, 6 * share : 7 * share]
    fc_shift_sib = fc_shift_sib.reshape(1, width).astype(F32)
    qv_shift = (
        columns[7]
        .reshape(parts, share)[:, : share // 2]
        .reshape(parts, 2, share // 4)
        .transpose(1, 0, 2)
        .reshape(2, head_cols)
    )
    qkv_shift = jnp.stack([qv_shift[0], jnp.zeros_like(qv_shift[0]), qv_shift[1]])
    qkv_shift = qkv_shift.reshape(3, pairs, PAIR).transpose(1, 0, 2).reshape(1, qkv_cols)
    proj_both = jnp.concatenate(
        [
            attn_all[:width, qkv_cols : qkv_cols + head_cols],
            attn_sib[:width, qkv_cols : qkv_cols + head_cols],
        ],
        axis=1,
    )

    normed_one, qkv = project(sequence, columns, qkv_shift, attn_all, rows)
    cots = [pick_x(cotangent, cot_x), pick_x(cot_x, cotangent)]

    inputs_two = [input_low, input_high]
    mixed, totals, mixed_own, mixed_sib, parts_two, received_two = [], [], [], [], [], []
    for half in range(2):
        half_mixed, half_totals = attend(
            qkv, half * 2 * rows, 2 * rows, rows, after=tuple(parts_two) + early * half
        )
        mixed.append(half_mixed)
        totals.append(half_totals)
        two = half_mixed.reshape(2, rows, head_cols)
        mine = jnp.where(is_first, two[0], two[1])
        received = swap_core(jnp.where(is_first, two[1], two[0]))
        both = jnp.concatenate([mine, received], axis=1)
        mixed_own.append(mine)
        mixed_sib.append(received)
        part = dot(both, proj_both, NT).astype(BF16)
        parts_two.append(part)
        received_two.append(swap_x(part))
    if parts == 8:
        mlp_shares[7] = swap_dp(mlp_shares[6], 1)
        mlp_all = place_shares(
            lax.axis_index("dp"),
            [mlp_shares[k] for k in range(parts)],
            0,
            (received_two[0], parts_two[1]),
        )
    else:
        mlp_all = gather_whole(mlp_shard, 0)
    mlp_sib = swap_core(mlp_all)
    residuals, normed_two, acts, grads_hidden, backs, out_parts = [], [], [], [], [], []
    fc_bias_sums = 0.0
    for half in range(2):
        residual, normed, act, grad_hidden, back, out_part, sums = feed(
            inputs_two[half],
            parts_two[half],
            received_two[half],
            cots[half],
            columns,
            fc_shift_own,
            fc_shift_sib,
            mlp_all,
            mlp_sib,
            after=(parts_two[1],),
        )
        residuals.append(residual)
        normed_two.append(normed)
        acts.append(act)
        grads_hidden.append(grad_hidden)
        backs.append(back)
        out_parts.append(out_part)
        fc_bias_sums = fc_bias_sums + sums[0]
    back_recv = [swap_x(back) for back in backs]

    sib_grads = feed_grads(
        normed_two, cots, grads_hidden, acts, hidden_cols, None, after=(back_recv[0],)
    )
    grad_mlp = feed_grads(normed_two, cots, grads_hidden, acts, 0, swap_core(sib_grads))
    mlp_sum = lax.psum_scatter(grad_mlp, "dp", scatter_dimension=0, tiled=True)

    grad_residuals, branches, grads_mixed = [], [], []
    for half in range(2):
        grad_residual, branch, grad_both, sums_two = norm_two(
            backs[half],
            back_recv[half],
            residuals[half],
            cots[half],
            columns,
            proj_both,
            after=(grad_mlp,) if half == 0 else (grad_mlp, low_grads),
        )
        grad_residuals.append(grad_residual)
        branches.append(branch)
        mine = grad_both[:, :head_cols]
        received = swap_core(grad_both[:, head_cols:])
        grads_mixed.append(
            jnp.concatenate(
                [jnp.where(is_first, mine, received), jnp.where(is_first, received, mine)], axis=0
            )
        )
        vec_two = sums_two if half == 0 else vec_two + sums_two
        if half == 0:
            low_grads, _ = attend_back(
                qkv, mixed[0], grads_mixed[0], totals[0], None, 0, rows, 0, pairs
            )
    proj_sib = dot(branches[0], mixed_sib[0], TN) + dot(branches[1], mixed_sib[1], TN)
    proj_received = swap_core(proj_sib.astype(BF16))

    out_sent = tie(pick_x(out_parts[1], out_parts[0]), low_grads)
    out_recv = swap_x(out_sent)

    y = lax.axis_index("dp") % 2 if parts == 8 else jnp.zeros((), jnp.int32)
    place_ids = jnp.stack([place // 2, core]).astype(jnp.int32)
    full_grads, grads_received, side_sums, exchanges = [], [], [], []
    after = ()
    for pair in range(pairs):
        grad_pair, pair_sums, grad_sent = attend_back(
            qkv,
            mixed[1],
            grads_mixed[1],
            totals[1],
            low_grads,
            2 * rows,
            rows,
            pair,
            1,
            after=after,
            core=core,
        )
        full_grads.append(grad_pair)
        side_sums.append(pair_sums)
        if pair > 0 and parts == 8:
            grad_sent = tie(grad_sent, exchanges[-1][2])
        grads_received.append(swap_core(grad_sent))
        proj = (branches, mixed_own, proj_received) if pair == 0 else None
        if pair == 0:
            out_recv = tie(out_recv, grad_pair)
        kept, sent = weight_grads(y, normed_one, grad_pair, proj)
        received = scatter_y(sent, parts) if pair < pairs - 1 else None
        exchanges.append((kept, sent, received))
        after = (sent, out_recv)

    z_own, z_sent, vec_one = norm_one(
        place_ids,
        input_low,
        input_high,
        full_grads,
        grads_received,
        attn_all,
        attn_sib,
        after=(exchanges[-1][1],),
    )
    z_recv = swap_x(z_sent)
    vec_two = vec_two + swap_core(vec_two)
    fc_bias_grad = fc_bias_sums[:hidden_cols] + swap_core(fc_bias_sums[hidden_cols:])

    vec_grads = jnp.concatenate(
        [
            vec_two[:2],
            vec_one[:2],
            vec_two[2:4],
            fc_bias_grad[None],
            jnp.zeros((1, width), F32),
        ],
        axis=0,
    )
    vec_blocks = vec_grads.reshape(8, parts, share).transpose(1, 0, 2)
    vec_blocks = jnp.pad(vec_blocks, ((0, 0), (0, 0), (0, 3 * PAIR - share)))
    pair_rows = jnp.pad(jnp.concatenate(side_sums, axis=0), ((0, 8 - pairs), (0, 0)))
    side = jnp.concatenate(
        [vec_blocks, jnp.broadcast_to(pair_rows[None], (parts, 8, 3 * PAIR))], axis=1
    )
    if parts == 8:
        views = side.reshape((parts // 2, 2) + side.shape[1:])
        side_kept = lax.dynamic_index_in_dim(views, y, 1, keepdims=False)
        side_sent = lax.dynamic_index_in_dim(views, 1 - y, 1, keepdims=False)
        side = side_kept + swap_dp(side_sent, 1)
    terms = []
    for pair in range(pairs):
        kept, sent, received = exchanges[pair]
        last = pair == pairs - 1
        if last:
            received = scatter_y(tie(sent, z_sent), parts)
        elif received is not None:
            received = tie(received, z_sent)
        terms.append(scatter_z(kept, sent, received, side if last else None, parts))

    out_recv = tie(out_recv, z_sent)
    out_mine = pick_x(out_parts[0], out_parts[1])
    outputs = (
        pick_x(residuals[0], residuals[1])
        + out_mine.astype(F32)
        + out_recv.astype(F32)
        + out_shift
    ).astype(BF16)

    qkv_out, proj_out, six, fc_out, out_out = finish(
        terms, mlp_sum, share, head_cols, side_rows, after=(outputs,)
    )
    unit, factor = normalize(inputs.astype(F32))
    z_own = z_own + tie(z_recv, six).astype(F32)
    grad_inputs = (
        pick_x(grad_residuals[0], grad_residuals[1]) + norm_back(unit, factor, gain_one, z_own)
    ).astype(BF16)
    one = six[2:4, :share]
    two = (
        one
        + swap_core(one)
        + swap_x(one)
        + lax.ppermute(one, "tensor", [(i, i ^ 3) for i in range(4)])
    )
    piece = share // 4
    start = lax.axis_index("dp") * piece
    mine = lax.dynamic_index_in_dim(six[8 : 8 + pairs], start // PAIR, 0, keepdims=False)
    qv_out = lax.dynamic_slice_in_dim(mine.reshape(3, PAIR), start % PAIR, piece, 1)[0::2]
    return (
        outputs,
        grad_inputs,
        qkv_out,
        qv_out,
        proj_out,
        six[0, :share],
        fc_out,
        six[6, :share],
        out_out,
        six[1, :share],
        two[0],
        two[1],
        six[4, :share],
        six[5, :share],
    )


def solution(mesh):
    rows = P(("dp", "tensor"), None)
    vector = P("dp")
    wide = P(("tensor", "dp"))
    weights = (
        P(None, "dp", "tensor"),
        P(None, ("tensor", "dp")),
        P("tensor", "dp"),
        vector,
        P("dp", "tensor"),
        wide,
        P("tensor", "dp"),
        vector,
        vector,
        vector,
        vector,
        vector,
    )
    return jax.shard_map(
        local,
        mesh=mesh,
        in_specs=(rows, *weights, rows),
        out_specs=(rows, rows, *weights),
        check_vma=False,
    )
```

```python
import functools

import jax
import jax.numpy as jnp
from jax import lax
from jax.experimental import pallas as pl
from jax.experimental.pallas import tpu as pltpu
from jax.sharding import PartitionSpec as P

HD = 64
PAIR = 2 * HD
EPSILON = 1e-05
NEGATIVE = -1e30
ROOT_TWO_PI = 0.7978845608028654
F32 = jnp.float32
BF16 = jnp.bfloat16
MIB = 1024 * 1024
SCALE = 0.25
ANY_SPACE = pl.BlockSpec(memory_space=pl.ANY)
SCALARS = pl.BlockSpec(memory_space=pltpu.SMEM)


def params(mib):
    return pltpu.CompilerParams(vmem_limit_bytes=mib * MIB)


def cost(micros):
    return pl.CostEstimate(
        flops=int(micros * SCALE * 1.1e9),
        bytes_accessed=int(micros * SCALE * 1e6),
        transcendentals=0,
    )


def swap_x(value):
    return lax.ppermute(value, "tensor", [(0, 2), (2, 0), (1, 3), (3, 1)])


def swap_core(value):
    return lax.ppermute(value, "tensor", [(0, 1), (1, 0), (2, 3), (3, 2)])


def dot(a, b, contract, kind=F32):
    return lax.dot_general(a, b, (contract, ((), ())), preferred_element_type=kind)


NN = ((1,), (0,))
NT = ((1,), (1,))
TN = ((0,), (0,))


def normalize(values):
    average = jnp.mean(values, axis=-1, keepdims=True)
    centered = values - average
    spread = jnp.mean(centered * centered, axis=-1, keepdims=True)
    factor = lax.rsqrt(spread + EPSILON)
    return centered * factor, factor


def norm_back(unit, factor, gain, grad):
    scaled = grad * gain
    return factor * (
        scaled
        - jnp.mean(scaled, axis=-1, keepdims=True)
        - unit * jnp.mean(scaled * unit, axis=-1, keepdims=True)
    )


def gelu_both(values):
    squared = values * values
    bent = jnp.tanh(ROOT_TWO_PI * values * (1.0 + 0.044715 * squared))
    half = 0.5 * (1.0 + bent)
    slope = half + 0.5 * values * (1.0 - bent * bent) * ROOT_TWO_PI * (
        1.0 + 3.0 * 0.044715 * squared
    )
    return values * half, slope


def split_heads(block):
    first = lax.broadcasted_iota(jnp.int32, block.shape, 1) < HD
    return [jnp.where(first, block, 0.0).astype(BF16), jnp.where(first, 0.0, block).astype(BF16)]


def attend_kernel(qkv_ref, *rest, row0, block):
    mixed_ref, total_ref, kept, acc = rest[-4:]
    count = mixed_ref.shape[0] // block
    first = lax.broadcasted_iota(jnp.int32, (PAIR, block), 0) < HD
    causal = lax.broadcasted_iota(jnp.int32, (block, block), 0) <= lax.broadcasted_iota(
        jnp.int32, (block, block), 1
    )
    for i in range(count):
        start = row0 + i * block
        heads = split_heads(qkv_ref[pl.ds(start, block), 0:PAIR].astype(F32) * (HD**-0.5))
        keys = qkv_ref[pl.ds(start, block), PAIR : 2 * PAIR]
        tops = []
        for h in range(2):
            scores = jnp.where(causal, dot(keys, heads[h], NT), NEGATIVE)
            kept[h, pl.ds(start, block), :] = scores
            tops.append(jnp.max(scores, axis=0, keepdims=True))

        def score_step(j, tops):
            at = pl.multiple_of(j * block, block)
            tile_keys = qkv_ref[pl.ds(at, block), PAIR : 2 * PAIR]
            found = []
            for h in range(2):
                scores = dot(tile_keys, heads[h], NT)
                kept[h, pl.ds(at, block), :] = scores
                found.append(jnp.maximum(tops[h], jnp.max(scores, axis=0, keepdims=True)))
            return tuple(found)

        tops = lax.fori_loop(0, start // block, score_step, tuple(tops))
        acc[...] = jnp.zeros(acc.shape, F32)

        def value_step(j, sums):
            at = pl.multiple_of(j * block, block)
            tile_values = qkv_ref[pl.ds(at, block), 2 * PAIR : 3 * PAIR]
            found = []
            for h in range(2):
                powers = jnp.exp(kept[h, pl.ds(at, block), :] - tops[h])
                found.append(sums[h] + jnp.sum(powers, axis=0, keepdims=True))
                acc[h] += dot(powers.astype(BF16), tile_values, TN)
            return tuple(found)

        zero = jnp.zeros((1, block), F32)
        sums = lax.fori_loop(0, start // block + 1, value_step, (zero, zero))
        inverse = jnp.transpose(jnp.where(first, 1.0 / sums[0], 1.0 / sums[1]))
        lane = lax.broadcasted_iota(jnp.int32, (block, PAIR), 1) < HD
        local = slice(i * block, (i + 1) * block)
        mixed_ref[local, :] = (jnp.where(lane, acc[0], acc[1]) * inverse).astype(BF16)
        for h in range(2):
            total_ref[0, h : h + 1, local] = tops[h] + jnp.log(sums[h])


def attend(qkv, row0, rows, block, after=()):
    pairs = qkv.shape[1] // (3 * PAIR)
    return pl.pallas_call(
        functools.partial(attend_kernel, row0=row0, block=block),
        grid=(pairs,),
        in_specs=[pl.BlockSpec((row0 + rows, 3 * PAIR), lambda j: (0, j))]
        + [ANY_SPACE] * len(after),
        out_specs=[
            pl.BlockSpec((rows, PAIR), lambda j: (0, j)),
            pl.BlockSpec((1, 2, rows), lambda j: (j, 0, 0)),
        ],
        out_shape=[
            jax.ShapeDtypeStruct((rows, pairs * PAIR), BF16),
            jax.ShapeDtypeStruct((pairs, 2, rows), F32),
        ],
        scratch_shapes=[
            pltpu.VMEM((2, row0 + rows, block), F32),
            pltpu.VMEM((2, block, PAIR), F32),
        ],
        compiler_params=params(16),
        cost_estimate=cost(16 if row0 else 6),
        name="attend_%d" % row0,
    )(qkv, *after)


def attend_back_kernel(
    core_ref, qkv_ref, mixed_ref, grad_ref, total_ref, *rest, row0, block, has_before
):
    before_ref = rest[0]
    sent_ref = None
    if has_before:
        out_ref, sums_ref, sent_ref, key_acc, value_acc, query_acc = rest[-6:]
    else:
        out_ref, sums_ref, key_acc, value_acc, query_acc = rest[-5:]
    rows = mixed_ref.shape[0]
    count = rows // block
    lane = lax.broadcasted_iota(jnp.int32, (block, PAIR), 1)
    first = lane < HD
    causal = lax.broadcasted_iota(jnp.int32, (block, block), 0) <= lax.broadcasted_iota(
        jnp.int32, (block, block), 1
    )
    if has_before:
        key_acc[0:row0, :] = before_ref[:, PAIR : 2 * PAIR]
        value_acc[0:row0, :] = before_ref[:, 2 * PAIR : 3 * PAIR]
        key_acc[row0:, :] = jnp.zeros((rows, PAIR), F32)
        value_acc[row0:, :] = jnp.zeros((rows, PAIR), F32)
    else:
        key_acc[...] = jnp.zeros(key_acc.shape, F32)
        value_acc[...] = jnp.zeros(value_acc.shape, F32)
    for i in range(count):
        start = row0 + i * block
        local = slice(i * block, (i + 1) * block)
        query_heads = split_heads(
            qkv_ref[pl.ds(start, block), 0:PAIR].astype(F32) * (HD**-0.5)
        )
        grads = grad_ref[local, :].astype(F32)
        grad_heads = split_heads(grads)
        inner = jnp.transpose(grads * mixed_ref[local, :].astype(F32))
        total_rows = [total_ref[0, h : h + 1, local] for h in range(2)]
        inner_rows = [
            jnp.sum(inner[h * HD : (h + 1) * HD, :], axis=0, keepdims=True) for h in range(2)
        ]

        def tile(at, masked):
            tile_keys = qkv_ref[pl.ds(at, block), PAIR : 2 * PAIR]
            tile_values = qkv_ref[pl.ds(at, block), 2 * PAIR : 3 * PAIR]
            key_sum, value_sum = None, None
            for h in range(2):
                scores = dot(tile_keys, query_heads[h], NT)
                weights = jnp.exp(scores - total_rows[h])
                if masked:
                    weights = jnp.where(causal, weights, 0.0)
                grad_weights = dot(tile_values, grad_heads[h], NT)
                grad_scores = (weights * (grad_weights - inner_rows[h])).astype(BF16)
                value_part = dot(weights.astype(BF16), grad_heads[h], NN)
                key_part = dot(grad_scores, query_heads[h], NN)
                query_part = dot(grad_scores, tile_keys, TN)
                key_sum = key_part if key_sum is None else key_sum + key_part
                value_sum = value_part if value_sum is None else value_sum + value_part
                if masked:
                    query_acc[h] = query_part
                else:
                    query_acc[h] += query_part
            key_acc[pl.ds(at, block), :] += key_sum
            value_acc[pl.ds(at, block), :] += value_sum

        tile(start, True)

        def step(j, carry):
            tile(pl.multiple_of(j * block, block), False)
            return carry

        if start:
            lax.fori_loop(0, start // block, step, 0)
        query_grad = jnp.where(first, query_acc[0], query_acc[1]) * (HD**-0.5)
        out_ref[start : start + block, 0:PAIR] = query_grad.astype(out_ref.dtype)
    if has_before:
        out_ref[0:row0, 0:PAIR] = before_ref[:, 0:PAIR].astype(out_ref.dtype)
    out_ref[:, PAIR : 2 * PAIR] = key_acc[...].astype(out_ref.dtype)
    out_ref[:, 2 * PAIR : 3 * PAIR] = value_acc[...].astype(out_ref.dtype)
    sums_ref[...] = jnp.sum(out_ref[...].astype(F32), axis=0, keepdims=True)
    if has_before:
        size = sent_ref.shape[0] // 2
        for half in range(2):
            at = pl.multiple_of((2 * half + 1 - core_ref[0]) * size, size)
            sent_ref[half * size : (half + 1) * size, :] = out_ref[pl.ds(at, size), :]


def attend_back(qkv, mixed, grads, totals, before, row0, block, pair, pairs, after=(), core=None):
    rows = mixed.shape[0]
    extent = row0 + rows
    narrow = pl.BlockSpec((rows, PAIR), lambda j: (0, pair + j))
    in_specs = [
        SCALARS,
        pl.BlockSpec((extent, 3 * PAIR), lambda j: (0, pair + j)),
        narrow,
        narrow,
        pl.BlockSpec((1, 2, rows), lambda j: (pair + j, 0, 0)),
    ]
    core = jnp.zeros((), jnp.int32) if core is None else core
    operands = [core.reshape(1).astype(jnp.int32), qkv, mixed, grads, totals]
    if before is not None:
        in_specs.append(pl.BlockSpec((row0, 3 * PAIR), lambda j: (0, pair + j)))
        operands.append(before)
    in_specs += [ANY_SPACE] * len(after)
    return pl.pallas_call(
        functools.partial(
            attend_back_kernel, row0=row0, block=block, has_before=before is not None
        ),
        grid=(pairs,),
        in_specs=in_specs,
        out_specs=[
            pl.BlockSpec((extent, 3 * PAIR), lambda j: (0, j)),
            pl.BlockSpec((1, 3 * PAIR), lambda j: (0, j)),
        ]
        + ([] if before is None else [pl.BlockSpec((extent // 2, 3 * PAIR), lambda j: (0, j))]),
        out_shape=[
            jax.ShapeDtypeStruct((extent, pairs * 3 * PAIR), F32 if before is None else BF16),
            jax.ShapeDtypeStruct((1, pairs * 3 * PAIR), F32),
        ]
        + (
            []
            if before is None
            else [jax.ShapeDtypeStruct((extent // 2, pairs * 3 * PAIR), BF16)]
        ),
        scratch_shapes=[
            pltpu.VMEM((extent, PAIR), F32),
            pltpu.VMEM((extent, PAIR), F32),
            pltpu.VMEM((2, block, PAIR), F32),
        ],
        compiler_params=params(20),
        cost_estimate=cost(5.5 * pairs if before is None else 13 * pairs),
        name="attend_back_%d_%d" % (row0, pair),
    )(*operands, *after)


def norm_two_kernel(
    back_ref, recv_ref, residual_ref, cot_ref, vec_ref, proj_ref, *rest, steps
):
    grad_ref, branch_ref, both_ref, sums_ref = rest[-4:]
    z = back_ref[...].astype(F32) + recv_ref[...].astype(F32)
    unit, factor = normalize(residual_ref[...])
    cot = cot_ref[...].astype(F32)
    grad = cot + norm_back(unit, factor, vec_ref[4:5, :], z)
    grad_ref[...] = grad
    branch = grad.astype(BF16)
    branch_ref[...] = branch
    both_ref[...] = dot(branch, proj_ref[...], NN).astype(BF16)

    @pl.when(pl.program_id(0) == 0)
    def _():
        sums_ref[...] = jnp.zeros(sums_ref.shape, F32)

    for at, part in enumerate((branch.astype(F32), cot, z * unit, z)):
        sums_ref[at : at + 1, :] += jnp.sum(part, axis=0, keepdims=True)


def norm_two(back, recv, residual, cot, vectors, proj, after=()):
    rows, width = back.shape
    steps = 2
    block = rows // steps
    strip = pl.BlockSpec((block, width), lambda i: (i, 0))
    return pl.pallas_call(
        functools.partial(norm_two_kernel, steps=steps),
        grid=(steps,),
        in_specs=[
            strip,
            strip,
            strip,
            strip,
            pl.BlockSpec(vectors.shape, lambda i: (0, 0)),
            pl.BlockSpec(proj.shape, lambda i: (0, 0)),
        ]
        + [ANY_SPACE] * len(after),
        out_specs=[
            strip,
            strip,
            pl.BlockSpec((block, proj.shape[1]), lambda i: (i, 0)),
            pl.BlockSpec((8, width), lambda i: (0, 0)),
        ],
        out_shape=[
            jax.ShapeDtypeStruct((rows, width), F32),
            jax.ShapeDtypeStruct((rows, width), BF16),
            jax.ShapeDtypeStruct((rows, proj.shape[1]), BF16),
            jax.ShapeDtypeStruct((8, width), F32),
        ],
        compiler_params=params(10),
        cost_estimate=cost(4),
        name="norm_two",
    )(back, recv, residual, cot, vectors, proj, *after)


def norm_one_kernel(place_ref, low_ref, high_ref, *refs, terms):
    grads, weights = refs[:terms], refs[terms : 2 * terms]
    own_ref, sent_ref, sums_ref = refs[-3:]
    i = pl.program_id(0)
    z = None
    for grad_ref, weight_ref in zip(grads, weights):
        part = dot(grad_ref[...], weight_ref[...], NT)
        z = part if z is None else z + part
    rows = jnp.where(i == 0, low_ref[...].astype(F32), high_ref[...].astype(F32))
    unit, _ = normalize(rows)

    @pl.when(i == 0)
    def _():
        sums_ref[...] = jnp.zeros(sums_ref.shape, F32)

    sums_ref[0:1, :] += jnp.sum(z * unit, axis=0, keepdims=True)
    sums_ref[1:2, :] += jnp.sum(z, axis=0, keepdims=True)

    @pl.when(i == place_ref[0])
    def _():
        own_ref[...] = z

    @pl.when(i != place_ref[0])
    def _():
        sent_ref[...] = z.astype(BF16)


def norm_one(places, low, high, full, received, own_weights, sib_weights, after=()):
    rows, width = low.shape
    pairs = len(full)
    cols = full[0].shape[1]
    whole = pl.BlockSpec((rows, width), lambda i, at: (0, 0))
    weight_specs = [
        pl.BlockSpec((width, cols), functools.partial(lambda pair, i, at: (0, pair), pair))
        for pair in range(pairs)
    ]
    return pl.pallas_call(
        functools.partial(norm_one_kernel, terms=2 * pairs),
        grid_spec=pltpu.PrefetchScalarGridSpec(
            num_scalar_prefetch=1,
            grid=(2,),
            in_specs=[whole, whole]
            + [pl.BlockSpec((rows, cols), lambda i, at: (2 * i + at[1], 0))] * pairs
            + [pl.BlockSpec((rows, cols), lambda i, at: (i, 0))] * pairs
            + weight_specs * 2
            + [ANY_SPACE] * len(after),
            out_specs=[whole, whole, pl.BlockSpec((8, width), lambda i, at: (0, 0))],
        ),
        out_shape=[
            jax.ShapeDtypeStruct((rows, width), F32),
            jax.ShapeDtypeStruct((rows, width), BF16),
            jax.ShapeDtypeStruct((8, width), F32),
        ],
        compiler_params=params(20),
        cost_estimate=cost(8),
        name="norm_one",
    )(
        places,
        low,
        high,
        *full,
        *received,
        *[own_weights] * pairs,
        *[sib_weights] * pairs,
        *after,
    )


def tie_kernel(value_ref, *rest):
    pass


def tie(value, *after):
    return pl.pallas_call(
        tie_kernel,
        in_specs=[ANY_SPACE] * (1 + len(after)),
        out_specs=ANY_SPACE,
        out_shape=jax.ShapeDtypeStruct(value.shape, value.dtype),
        input_output_aliases={0: 0},
        cost_estimate=cost(0.1),
        name="tie",
    )(value, *after)


def place_kernel(me_ref, *refs, parts, side_rows):
    full_ref = refs[-1]
    rows = refs[0].shape[0] - side_rows
    for k in range(parts):
        at = lax.bitwise_xor(me_ref[0], k)
        full_ref[pl.ds(pl.multiple_of(at * rows, rows), rows), :] = refs[k][0:rows, :]
        if side_rows:
            side = pl.multiple_of(parts * rows + at * side_rows, side_rows)
            full_ref[pl.ds(side, side_rows), :] = refs[k][rows:, :]


def place_shares(me, pieces, side_rows, after):
    total, cols = pieces[0].shape
    parts, kind = len(pieces), pieces[0].dtype
    return pl.pallas_call(
        functools.partial(place_kernel, parts=parts, side_rows=side_rows),
        grid=(1,),
        in_specs=[SCALARS]
        + [pl.BlockSpec((total, cols), lambda i: (0, 0))] * parts
        + [ANY_SPACE] * len(after),
        out_specs=pl.BlockSpec((parts * total, cols), lambda i: (0, 0)),
        out_shape=jax.ShapeDtypeStruct((parts * total, cols), kind),
        compiler_params=params(18),
        cost_estimate=cost(3),
        name="place_shares",
    )(me.reshape(1).astype(jnp.int32), *pieces, *after)


def feed_grads_kernel(*refs, tiles, received):
    normed, cots, grads, acts = refs[0:2], refs[2:4], refs[4:6], refs[6:8]
    out_ref = refs[-1]
    i = pl.program_id(0)

    def work(left, right):
        total = dot(left[0][...], right[0][...], TN) + dot(left[1][...], right[1][...], TN)
        if received:
            total = total + refs[8][...].astype(F32)
        out_ref[...] = total.astype(BF16)

    @pl.when(i < tiles)
    def _():
        work(normed, grads)

    @pl.when(i >= tiles)
    def _():
        work(cots, acts)


def feed_grads(normed, cots, grads, acts, first, received, after=()):
    rows, width = normed[0].shape
    hidden_cols = grads[0].shape[1] // 2
    tile = min(512, hidden_cols)
    tiles = hidden_cols // tile
    base = first // tile
    whole = pl.BlockSpec((rows, width), lambda i: (0, 0))
    grad_spec = pl.BlockSpec((rows, tile), lambda i: (0, base + jnp.minimum(i, tiles - 1)))
    act_spec = pl.BlockSpec((rows, tile), lambda i: (0, base + jnp.maximum(i - tiles, 0)))
    out_spec = pl.BlockSpec((width, tile), lambda i: (0, i))
    return pl.pallas_call(
        functools.partial(feed_grads_kernel, tiles=tiles, received=received is not None),
        grid=(2 * tiles,),
        in_specs=[whole] * 4
        + [grad_spec] * 2
        + [act_spec] * 2
        + ([] if received is None else [out_spec])
        + [ANY_SPACE] * len(after),
        out_specs=out_spec,
        out_shape=jax.ShapeDtypeStruct((width, 2 * hidden_cols), BF16),
        compiler_params=params(24),
        cost_estimate=cost(6),
        name="feed_grads",
    )(*normed, *cots, *grads, *acts, *([] if received is None else [received]), *after)


def weight_grads_kernel(y_ref, normed_ref, grad_ref, *refs, with_proj):
    kept_ref, sent_ref = refs[-2:]
    share = kept_ref.shape[1]
    total = dot(normed_ref[...], grad_ref[...], TN)
    if with_proj:
        low_ref, high_ref, low_mixed_ref, high_mixed_ref, recv_ref = refs[:5]
        proj = dot(low_ref[...], low_mixed_ref[...], TN) + dot(
            high_ref[...], high_mixed_ref[...], TN
        )
        proj = proj + recv_ref[...].astype(F32)
        total = jnp.concatenate([total, proj], axis=1)
    even, odd = total[:share], total[share:]
    stays = y_ref[0] == 0
    kept_ref[0] = jnp.where(stays, even, odd)
    sent_ref[0] = jnp.where(stays, odd, even).astype(BF16)


def weight_grads(y, normed, grads, proj, after=()):
    length, width = normed.shape
    cols = grads.shape[1]
    steps, share = 4, width // 8
    in_specs = [
        SCALARS,
        pl.BlockSpec((length, 2 * share), lambda i: (0, i)),
        pl.BlockSpec((length, cols), lambda i: (0, 0)),
    ]
    operands = [y.reshape(1).astype(jnp.int32), normed, grads]
    total = cols
    if proj is not None:
        branches, mixed, received = proj
        rows, head_cols = mixed[0].shape
        total += head_cols
        in_specs += [pl.BlockSpec((rows, 2 * share), lambda i: (0, i))] * 2
        in_specs += [pl.BlockSpec((rows, head_cols), lambda i: (0, 0))] * 2
        in_specs += [pl.BlockSpec((2 * share, head_cols), lambda i: (i, 0))]
        operands += [*branches, *mixed, received]
    return pl.pallas_call(
        functools.partial(weight_grads_kernel, with_proj=proj is not None),
        grid=(steps,),
        in_specs=in_specs + [ANY_SPACE] * len(after),
        out_specs=[pl.BlockSpec((1, share, total), lambda i: (i, 0, 0))] * 2,
        out_shape=[
            jax.ShapeDtypeStruct((steps, share, total), F32),
            jax.ShapeDtypeStruct((steps, share, total), BF16),
        ],
        compiler_params=params(16),
        cost_estimate=cost(4),
        name="weight_grads",
    )(*operands, *after)


def finish_kernel(*refs, pairs, counts):
    qkv_ref, proj_ref, side_ref, fc_ref, out_ref = refs[-5:]
    feed_ref = refs[sum(counts)]
    hidden_cols = fc_ref.shape[1]
    fc_ref[...] = feed_ref[:, :hidden_cols].astype(F32)
    out_ref[...] = jnp.transpose(feed_ref[:, hidden_cols:].astype(F32))
    at = 0
    for pair in range(pairs):
        total = refs[at][...].astype(F32)
        for part in range(1, counts[pair]):
            total = total + refs[at + part][...].astype(F32)
        at += counts[pair]
        share = qkv_ref.shape[1]
        for j in range(3):
            qkv_ref[j, :, pair * PAIR : (pair + 1) * PAIR] = total[:share, j * PAIR : (j + 1) * PAIR]
        if pair == 0:
            proj_ref[...] = jnp.transpose(total[:share, 3 * PAIR :])
        if pair == pairs - 1:
            side_ref[...] = total[share:, : 3 * PAIR]


def finish(terms, feed_sum, share, head_cols, side_rows, after=()):
    pairs = len(terms)
    flat = [term for pair in terms for term in pair]
    hidden_cols = feed_sum.shape[1] // 2
    return pl.pallas_call(
        functools.partial(
            finish_kernel, pairs=pairs, counts=[len(pair) for pair in terms]
        ),
        grid=(1,),
        in_specs=[pl.BlockSpec(term.shape, lambda i: (0, 0)) for term in flat + [feed_sum]]
        + [ANY_SPACE] * len(after),
        out_specs=[
            pl.BlockSpec((3, share, head_cols), lambda i: (0, 0, 0)),
            pl.BlockSpec((head_cols, share), lambda i: (0, 0)),
            pl.BlockSpec((side_rows, 3 * PAIR), lambda i: (0, 0)),
            pl.BlockSpec((share, hidden_cols), lambda i: (0, 0)),
            pl.BlockSpec((hidden_cols, share), lambda i: (0, 0)),
        ],
        out_shape=[
            jax.ShapeDtypeStruct((3, share, head_cols), F32),
            jax.ShapeDtypeStruct((head_cols, share), F32),
            jax.ShapeDtypeStruct((side_rows, 3 * PAIR), F32),
            jax.ShapeDtypeStruct((share, hidden_cols), F32),
            jax.ShapeDtypeStruct((hidden_cols, share), F32),
        ],
        compiler_params=params(12),
        cost_estimate=cost(3),
        name="finish",
    )(*flat, feed_sum, *after)


def project_kernel(rows_ref, vec_ref, shift_ref, weight_ref, *rest):
    normed_ref, out_ref = rest[-2:]
    unit, _ = normalize(rows_ref[...].astype(F32))
    normed_ref[...] = (unit * vec_ref[2:3, :] + vec_ref[3:4, :]).astype(BF16)
    out_ref[...] = (dot(normed_ref[...], weight_ref[...], NN) + shift_ref[...]).astype(BF16)


def project(sequence, vectors, shift, weights, block, after=()):
    length, width = sequence.shape
    cols = shift.shape[1]
    return pl.pallas_call(
        project_kernel,
        grid=(length // block,),
        in_specs=[
            pl.BlockSpec((block, width), lambda i: (i, 0)),
            pl.BlockSpec(vectors.shape, lambda i: (0, 0)),
            pl.BlockSpec(shift.shape, lambda i: (0, 0)),
            pl.BlockSpec((width, cols), lambda i: (0, 0)),
        ]
        + [ANY_SPACE] * len(after),
        out_specs=[
            pl.BlockSpec((block, width), lambda i: (i, 0)),
            pl.BlockSpec((block, cols), lambda i: (i, 0)),
        ],
        out_shape=[
            jax.ShapeDtypeStruct((length, width), BF16),
            jax.ShapeDtypeStruct((length, cols), BF16),
        ],
        compiler_params=params(16),
        cost_estimate=cost(6),
        name="project",
    )(sequence, vectors, shift, weights, *after)


def feed_kernel(
    base_ref,
    part_ref,
    recv_ref,
    cot_ref,
    vec_ref,
    shift_own_ref,
    shift_sib_ref,
    fc_own_ref,
    out_own_ref,
    fc_sib_ref,
    out_sib_ref,
    *rest,
    tiles,
):
    residual_ref, normed_ref, act_ref, grad_ref, back_ref, sent_ref, sums_ref = rest[-9:-2]
    back_acc, out_acc = rest[-2:]
    i = pl.program_id(0)
    rows = base_ref.shape[0]

    @pl.when(i == 0)
    def _():
        residual = (
            base_ref[...].astype(F32)
            + part_ref[...].astype(F32)
            + recv_ref[...].astype(F32)
            + vec_ref[0:1, :]
        )
        residual_ref[...] = residual
        unit, _ = normalize(residual)
        normed_ref[...] = (unit * vec_ref[4:5, :] + vec_ref[5:6, :]).astype(BF16)
        back_acc[...] = jnp.zeros(back_acc.shape, F32)
        out_acc[...] = jnp.zeros(out_acc.shape, F32)

    def work(shift_ref, fc_ref, out_ref):
        step = rows // 2
        total = None
        for r in range(2):
            at = slice(r * step, (r + 1) * step)
            hidden = dot(normed_ref[at, :], fc_ref[...], NN) + shift_ref[...]
            grad_act = dot(cot_ref[at, :], out_ref[...], NN)
            act, slope = gelu_both(hidden)
            act = act.astype(BF16)
            grad = (grad_act * slope).astype(BF16)
            act_ref[at, :] = act
            grad_ref[at, :] = grad
            part = jnp.sum(grad.astype(F32), axis=0, keepdims=True)
            total = part if total is None else total + part
            back_acc[at, :] += dot(grad, fc_ref[...], NT)
            out_acc[at, :] += dot(act, out_ref[...], NT)
        sums_ref[...] = total

    @pl.when(i < tiles)
    def _():
        work(shift_own_ref, fc_own_ref, out_own_ref)

    @pl.when(i >= tiles)
    def _():
        work(shift_sib_ref, fc_sib_ref, out_sib_ref)

    @pl.when(i == 2 * tiles - 1)
    def _():
        back_ref[...] = back_acc[...].astype(BF16)
        sent_ref[...] = out_acc[...].astype(BF16)


def feed(base, part, recv, cot, vectors, shift_own, shift_sib, own, sib, after=()):
    rows, width = base.shape
    hidden_cols = shift_own.shape[1]
    tile = min(512, hidden_cols)
    tiles = hidden_cols // tile
    whole = pl.BlockSpec((rows, width), lambda i: (0, 0))

    def low(i):
        return jnp.minimum(i, tiles - 1)

    def high(i):
        return jnp.maximum(i - tiles, 0)

    return pl.pallas_call(
        functools.partial(feed_kernel, tiles=tiles),
        grid=(2 * tiles,),
        in_specs=[
            whole,
            whole,
            whole,
            whole,
            pl.BlockSpec(vectors.shape, lambda i: (0, 0)),
            pl.BlockSpec((1, tile), lambda i: (0, low(i))),
            pl.BlockSpec((1, tile), lambda i: (0, high(i))),
            pl.BlockSpec((width, tile), lambda i: (0, low(i))),
            pl.BlockSpec((width, tile), lambda i: (0, tiles + low(i))),
            pl.BlockSpec((width, tile), lambda i: (0, high(i))),
            pl.BlockSpec((width, tile), lambda i: (0, tiles + high(i))),
        ]
        + [ANY_SPACE] * len(after),
        out_specs=[
            whole,
            whole,
            pl.BlockSpec((rows, tile), lambda i: (0, i)),
            pl.BlockSpec((rows, tile), lambda i: (0, i)),
            whole,
            whole,
            pl.BlockSpec((1, tile), lambda i: (0, i)),
        ],
        out_shape=[
            jax.ShapeDtypeStruct((rows, width), F32),
            jax.ShapeDtypeStruct((rows, width), BF16),
            jax.ShapeDtypeStruct((rows, 2 * hidden_cols), BF16),
            jax.ShapeDtypeStruct((rows, 2 * hidden_cols), BF16),
            jax.ShapeDtypeStruct((rows, width), BF16),
            jax.ShapeDtypeStruct((rows, width), BF16),
            jax.ShapeDtypeStruct((1, 2 * hidden_cols), F32),
        ],
        scratch_shapes=[pltpu.VMEM((rows, width), F32), pltpu.VMEM((rows, width), F32)],
        compiler_params=params(32),
        cost_estimate=cost(16),
        name="feed",
    )(
        base, part, recv, cot, vectors, shift_own, shift_sib, own, own, sib, sib, *after
    )


def swap_dp(value, mask):
    size = lax.axis_size("dp")
    return lax.ppermute(value, "dp", [(i, i ^ mask) for i in range(size)])


def gather_z(shard):
    return {k: swap_dp(shard, k) for k in (6, 4, 2)}


def gather_whole(shard, side_rows):
    rows, cols = shard.shape[0] - side_rows, shard.shape[1]
    full = lax.all_gather(shard, "dp", axis=0)
    return jnp.concatenate(
        [full[:, :rows].reshape(-1, cols), full[:, rows:].reshape(-1, cols)], axis=0
    )


def scatter_y(sent, parts):
    return swap_dp(sent, 1) if parts == 8 else None


def scatter_z(kept, sent, received, side, parts):
    if parts != 8:
        whole = jnp.concatenate([kept, sent.astype(F32)], axis=1)
        whole = whole.reshape(parts, -1, whole.shape[2])
        if side is not None:
            whole = jnp.concatenate([whole, side], axis=1)
        return [lax.psum_scatter(whole.astype(BF16), "dp", scatter_dimension=0)]
    sums = kept + received.astype(F32)
    if side is not None:
        sums = jnp.concatenate([sums, side], axis=1)
    z = lax.axis_index("dp") // 2
    terms = [lax.dynamic_index_in_dim(sums, z, 0, keepdims=False)]
    for k in (3, 2, 1):
        sent = lax.dynamic_index_in_dim(sums, z ^ k, 0, keepdims=False).astype(BF16)
        terms.append(swap_dp(sent, 2 * k))
    return terms


def local(
    inputs,
    qkv_weight,
    qv_bias,
    proj_weight,
    proj_bias,
    fc_weight,
    fc_bias,
    out_weight,
    out_bias,
    attn_norm_gain,
    attn_norm_bias,
    mlp_norm_gain,
    mlp_norm_bias,
    cotangent,
):
    width = inputs.shape[1]
    rows = inputs.shape[0]
    share = proj_bias.shape[0]
    parts = width // share
    head_cols = qkv_weight.shape[2]
    pairs = head_cols // PAIR
    qkv_cols = 3 * head_cols
    hidden_cols = fc_weight.shape[1]
    place = lax.axis_index("tensor")
    core = place % 2
    is_low = place < 2
    is_first = core == 0

    def pick_x(low, high):
        return jnp.where(is_low, low, high)

    mlp_shard = jnp.concatenate([fc_weight, out_weight.T], axis=1)
    qv_row = jnp.pad(qv_bias.reshape(-1), (0, share - qv_bias.size))
    vectors = jnp.stack(
        [
            proj_bias,
            out_bias,
            attn_norm_gain,
            attn_norm_bias,
            mlp_norm_gain,
            mlp_norm_bias,
            fc_bias,
            qv_row,
        ]
    )
    qkv_shard = jnp.transpose(
        qkv_weight.reshape(3, share, pairs, PAIR), (1, 2, 0, 3)
    ).reshape(share, qkv_cols)
    attn_shard = jnp.concatenate([qkv_shard, proj_weight.T], axis=1)
    side_rows = 16
    vectors = jnp.pad(
        vectors.reshape(1, -1), ((0, side_rows - 1), (0, attn_shard.shape[1] - vectors.size))
    )
    attn_shard = jnp.concatenate([attn_shard, vectors], axis=0)

    input_x_sent = swap_x(inputs)
    input_core = swap_core(inputs)
    cot_x = swap_x(cotangent)
    blocks = []

    def assemble(late):
        input_x = tie(input_x_sent, *late)
        input_far = swap_core(input_x)
        low, high = pick_x(inputs, input_x), pick_x(input_x, inputs)
        far_low, far_high = pick_x(input_core, input_far), pick_x(input_far, input_core)
        sequence = jnp.concatenate(
            [
                jnp.where(is_first, low, far_low),
                jnp.where(is_first, far_low, low),
                jnp.where(is_first, high, far_high),
                jnp.where(is_first, far_high, high),
            ],
            axis=0,
        )
        blocks.extend([low, high, sequence])
        return (sequence, cot_x)

    if parts == 8:
        shares = {0: attn_shard, **gather_z(attn_shard)}
        mlp_shares = {0: mlp_shard, 1: swap_dp(mlp_shard, 1)}
        for k in (0, 2, 4, 6):
            shares[k + 1] = swap_dp(shares[k], 1)
        behind = (shares[6], shares[5], shares[3], shares[1], mlp_shares[1])
        mlp_shares.update(gather_z(tie(mlp_shard, *(shares[k] for k in (2, 4, 6)))))
        for k in (2, 4):
            mlp_shares[k + 1] = swap_dp(mlp_shares[k], 1)
        attn_all = place_shares(
            lax.axis_index("dp"),
            [shares[k] for k in range(parts)],
            side_rows,
            assemble(behind) + (mlp_shares[2], mlp_shares[4]),
        )
        early = (mlp_shares[3], mlp_shares[5], mlp_shares[6])
    else:
        attn_all = gather_whole(attn_shard, side_rows)
        assemble((attn_all,))
        early = ()
    input_low, input_high, sequence = blocks
    attn_sib = swap_core(attn_all)
    vectors = attn_all[width:].reshape(parts, side_rows, -1)[:, 0, : 8 * share]
    vectors = vectors.reshape(parts, 8, share).transpose(1, 0, 2).reshape(8, width)
    columns = vectors.astype(F32)
    out_shift, gain_one = columns[1:2], columns[2:3]
    fc_shift_own = columns[6:7]
    fc_shift_sib = attn_sib[width:].reshape(parts, side_rows, -1)[:, 0, 6 * share : 7 * share]
    fc_shift_sib = fc_shift_sib.reshape(1, width).astype(F32)
    qv_shift = (
        columns[7]
        .reshape(parts, share)[:, : share // 2]
        .reshape(parts, 2, share // 4)
        .transpose(1, 0, 2)
        .reshape(2, head_cols)
    )
    qkv_shift = jnp.stack([qv_shift[0], jnp.zeros_like(qv_shift[0]), qv_shift[1]])
    qkv_shift = qkv_shift.reshape(3, pairs, PAIR).transpose(1, 0, 2).reshape(1, qkv_cols)
    proj_both = jnp.concatenate(
        [
            attn_all[:width, qkv_cols : qkv_cols + head_cols],
            attn_sib[:width, qkv_cols : qkv_cols + head_cols],
        ],
        axis=1,
    )

    normed_one, qkv = project(sequence, columns, qkv_shift, attn_all, rows)
    cots = [pick_x(cotangent, cot_x), pick_x(cot_x, cotangent)]

    inputs_two = [input_low, input_high]
    mixed, totals, mixed_own, mixed_sib, parts_two, received_two = [], [], [], [], [], []
    for half in range(2):
        half_mixed, half_totals = attend(
            qkv, half * 2 * rows, 2 * rows, rows, after=tuple(parts_two) + early * half
        )
        mixed.append(half_mixed)
        totals.append(half_totals)
        two = half_mixed.reshape(2, rows, head_cols)
        mine = jnp.where(is_first, two[0], two[1])
        received = swap_core(jnp.where(is_first, two[1], two[0]))
        both = jnp.concatenate([mine, received], axis=1)
        mixed_own.append(mine)
        mixed_sib.append(received)
        part = dot(both, proj_both, NT).astype(BF16)
        parts_two.append(part)
        received_two.append(swap_x(part))
    if parts == 8:
        mlp_shares[7] = swap_dp(mlp_shares[6], 1)
        mlp_all = place_shares(
            lax.axis_index("dp"),
            [mlp_shares[k] for k in range(parts)],
            0,
            (received_two[0], parts_two[1]),
        )
    else:
        mlp_all = gather_whole(mlp_shard, 0)
    mlp_sib = swap_core(mlp_all)
    residuals, normed_two, acts, grads_hidden, backs, out_parts = [], [], [], [], [], []
    fc_bias_sums = 0.0
    for half in range(2):
        residual, normed, act, grad_hidden, back, out_part, sums = feed(
            inputs_two[half],
            parts_two[half],
            received_two[half],
            cots[half],
            columns,
            fc_shift_own,
            fc_shift_sib,
            mlp_all,
            mlp_sib,
            after=(parts_two[1],),
        )
        residuals.append(residual)
        normed_two.append(normed)
        acts.append(act)
        grads_hidden.append(grad_hidden)
        backs.append(back)
        out_parts.append(out_part)
        fc_bias_sums = fc_bias_sums + sums[0]
    back_recv = [swap_x(back) for back in backs]

    sib_grads = feed_grads(
        normed_two, cots, grads_hidden, acts, hidden_cols, None, after=(back_recv[0],)
    )
    grad_mlp = feed_grads(normed_two, cots, grads_hidden, acts, 0, swap_core(sib_grads))
    mlp_sum = lax.psum_scatter(grad_mlp, "dp", scatter_dimension=0, tiled=True)

    grad_residuals, branches, grads_mixed = [], [], []
    for half in range(2):
        grad_residual, branch, grad_both, sums_two = norm_two(
            backs[half],
            back_recv[half],
            residuals[half],
            cots[half],
            columns,
            proj_both,
            after=(sib_grads,) if half == 0 else (grad_mlp, low_grads),
        )
        grad_residuals.append(grad_residual)
        branches.append(branch)
        mine = grad_both[:, :head_cols]
        received = swap_core(grad_both[:, head_cols:])
        grads_mixed.append(
            jnp.concatenate(
                [jnp.where(is_first, mine, received), jnp.where(is_first, received, mine)], axis=0
            )
        )
        vec_two = sums_two if half == 0 else vec_two + sums_two
        if half == 0:
            low_grads, _ = attend_back(
                qkv,
                mixed[0],
                grads_mixed[0],
                totals[0],
                None,
                0,
                rows,
                0,
                pairs,
                after=(grad_mlp,),
            )
    proj_sib = dot(branches[0], mixed_sib[0], TN) + dot(branches[1], mixed_sib[1], TN)
    proj_received = swap_core(proj_sib.astype(BF16))

    out_sent = tie(pick_x(out_parts[1], out_parts[0]), low_grads)
    out_recv = swap_x(out_sent)

    y = lax.axis_index("dp") % 2 if parts == 8 else jnp.zeros((), jnp.int32)
    place_ids = jnp.stack([place // 2, core]).astype(jnp.int32)
    full_grads, grads_received, side_sums, exchanges = [], [], [], []
    after = ()
    for pair in range(pairs):
        grad_pair, pair_sums, grad_sent = attend_back(
            qkv,
            mixed[1],
            grads_mixed[1],
            totals[1],
            low_grads,
            2 * rows,
            rows,
            pair,
            1,
            after=after,
            core=core,
        )
        full_grads.append(grad_pair)
        side_sums.append(pair_sums)
        if pair > 0 and parts == 8:
            grad_sent = tie(grad_sent, exchanges[-1][2])
        grads_received.append(swap_core(grad_sent))
        proj = (branches, mixed_own, proj_received) if pair == 0 else None
        if pair == 0:
            out_recv = tie(out_recv, grad_pair)
        kept, sent = weight_grads(y, normed_one, grad_pair, proj)
        received = scatter_y(sent, parts) if pair < pairs - 1 else None
        exchanges.append((kept, sent, received))
        after = (sent, out_recv)

    z_own, z_sent, vec_one = norm_one(
        place_ids,
        input_low,
        input_high,
        full_grads,
        grads_received,
        attn_all,
        attn_sib,
        after=(exchanges[-1][1],),
    )
    first_terms = scatter_z(*exchanges[0], side=None, parts=parts)
    z_recv = swap_x(z_sent)
    vec_two = vec_two + swap_core(vec_two)
    fc_bias_grad = fc_bias_sums[:hidden_cols] + swap_core(fc_bias_sums[hidden_cols:])

    vec_grads = jnp.concatenate(
        [
            vec_two[:2],
            vec_one[:2],
            vec_two[2:4],
            fc_bias_grad[None],
            jnp.zeros((1, width), F32),
        ],
        axis=0,
    )
    vec_blocks = vec_grads.reshape(8, parts, share).transpose(1, 0, 2)
    vec_blocks = jnp.pad(vec_blocks, ((0, 0), (0, 0), (0, 3 * PAIR - share)))
    pair_rows = jnp.pad(jnp.concatenate(side_sums, axis=0), ((0, 8 - pairs), (0, 0)))
    side = jnp.concatenate(
        [vec_blocks, jnp.broadcast_to(pair_rows[None], (parts, 8, 3 * PAIR))], axis=1
    )
    if parts == 8:
        views = side.reshape((parts // 2, 2) + side.shape[1:])
        side_kept = lax.dynamic_index_in_dim(views, y, 1, keepdims=False)
        side_sent = lax.dynamic_index_in_dim(views, 1 - y, 1, keepdims=False)
        side = side_kept + swap_dp(side_sent, 1)
    terms = [first_terms]
    for pair in range(1, pairs):
        kept, sent, received = exchanges[pair]
        last = pair == pairs - 1
        if last:
            received = scatter_y(tie(sent, z_sent), parts)
        terms.append(scatter_z(kept, sent, received, side if last else None, parts))

    qkv_out, proj_out, six, fc_out, out_out = finish(
        terms, mlp_sum, share, head_cols, side_rows, after=(z_sent,)
    )
    out_recv = tie(out_recv, six)
    out_mine = pick_x(out_parts[0], out_parts[1])
    outputs = (
        pick_x(residuals[0], residuals[1])
        + out_mine.astype(F32)
        + out_recv.astype(F32)
        + out_shift
    ).astype(BF16)

    unit, factor = normalize(inputs.astype(F32))
    z_own = z_own + tie(z_recv, six).astype(F32)
    grad_inputs = (
        pick_x(grad_residuals[0], grad_residuals[1]) + norm_back(unit, factor, gain_one, z_own)
    ).astype(BF16)
    one = six[2:4, :share]
    far = lax.ppermute(one, "tensor", [(i, i ^ 3) for i in range(4)])
    two = one + swap_core(one) + swap_x(one) + far
    piece = share // 4
    start = lax.axis_index("dp") * piece
    mine = lax.dynamic_index_in_dim(six[8 : 8 + pairs], start // PAIR, 0, keepdims=False)
    qv_out = lax.dynamic_slice_in_dim(mine.reshape(3, PAIR), start % PAIR, piece, 1)[0::2]
    return (
        outputs,
        grad_inputs,
        qkv_out,
        qv_out,
        proj_out,
        six[0, :share],
        fc_out,
        six[6, :share],
        out_out,
        six[1, :share],
        two[0],
        two[1],
        six[4, :share],
        six[5, :share],
    )


def solution(mesh):
    rows = P(("dp", "tensor"), None)
    vector = P("dp")
    wide = P(("tensor", "dp"))
    weights = (
        P(None, "dp", "tensor"),
        P(None, ("tensor", "dp")),
        P("tensor", "dp"),
        vector,
        P("dp", "tensor"),
        wide,
        P("tensor", "dp"),
        vector,
        vector,
        vector,
        vector,
        vector,
    )
    return jax.shard_map(
        local,
        mesh=mesh,
        in_specs=(rows, *weights, rows),
        out_specs=(rows, rows, *weights),
        check_vma=False,
    )
```

```python
import functools

import jax
import jax.numpy as jnp
from jax import lax
from jax.experimental import pallas as pl
from jax.experimental.pallas import tpu as pltpu
from jax.sharding import PartitionSpec as P

HD = 64
PAIR = 2 * HD
EPSILON = 1e-05
NEGATIVE = -1e30
ROOT_TWO_PI = 0.7978845608028654
F32 = jnp.float32
BF16 = jnp.bfloat16
MIB = 1024 * 1024
SCALE = 0.25
ANY_SPACE = pl.BlockSpec(memory_space=pl.ANY)
SCALARS = pl.BlockSpec(memory_space=pltpu.SMEM)


def params(mib):
    return pltpu.CompilerParams(vmem_limit_bytes=mib * MIB)


def cost(micros):
    return pl.CostEstimate(
        flops=int(micros * SCALE * 1.1e9),
        bytes_accessed=int(micros * SCALE * 1e6),
        transcendentals=0,
    )


def swap_x(value):
    return lax.ppermute(value, "tensor", [(0, 2), (2, 0), (1, 3), (3, 1)])


def swap_core(value):
    return lax.ppermute(value, "tensor", [(0, 1), (1, 0), (2, 3), (3, 2)])


def dot(a, b, contract, kind=F32):
    return lax.dot_general(a, b, (contract, ((), ())), preferred_element_type=kind)


NN = ((1,), (0,))
NT = ((1,), (1,))
TN = ((0,), (0,))


def normalize(values):
    average = jnp.mean(values, axis=-1, keepdims=True)
    centered = values - average
    spread = jnp.mean(centered * centered, axis=-1, keepdims=True)
    factor = lax.rsqrt(spread + EPSILON)
    return centered * factor, factor


def norm_back(unit, factor, gain, grad):
    scaled = grad * gain
    return factor * (
        scaled
        - jnp.mean(scaled, axis=-1, keepdims=True)
        - unit * jnp.mean(scaled * unit, axis=-1, keepdims=True)
    )


def gelu_both(values):
    squared = values * values
    bent = jnp.tanh(ROOT_TWO_PI * values * (1.0 + 0.044715 * squared))
    half = 0.5 * (1.0 + bent)
    slope = half + 0.5 * values * (1.0 - bent * bent) * ROOT_TWO_PI * (
        1.0 + 3.0 * 0.044715 * squared
    )
    return values * half, slope


def split_heads(block):
    first = lax.broadcasted_iota(jnp.int32, block.shape, 1) < HD
    return [jnp.where(first, block, 0.0).astype(BF16), jnp.where(first, 0.0, block).astype(BF16)]


def attend_kernel(qkv_ref, *rest, row0, block):
    mixed_ref, total_ref, kept, acc = rest[-4:]
    count = mixed_ref.shape[0] // block
    first = lax.broadcasted_iota(jnp.int32, (PAIR, block), 0) < HD
    causal = lax.broadcasted_iota(jnp.int32, (block, block), 0) <= lax.broadcasted_iota(
        jnp.int32, (block, block), 1
    )
    for i in range(count):
        start = row0 + i * block
        heads = split_heads(qkv_ref[pl.ds(start, block), 0:PAIR].astype(F32) * (HD**-0.5))
        keys = qkv_ref[pl.ds(start, block), PAIR : 2 * PAIR]
        tops = []
        for h in range(2):
            scores = jnp.where(causal, dot(keys, heads[h], NT), NEGATIVE)
            kept[h, pl.ds(start, block), :] = scores
            tops.append(jnp.max(scores, axis=0, keepdims=True))

        def score_step(j, tops):
            at = pl.multiple_of(j * block, block)
            tile_keys = qkv_ref[pl.ds(at, block), PAIR : 2 * PAIR]
            found = []
            for h in range(2):
                scores = dot(tile_keys, heads[h], NT)
                kept[h, pl.ds(at, block), :] = scores
                found.append(jnp.maximum(tops[h], jnp.max(scores, axis=0, keepdims=True)))
            return tuple(found)

        tops = lax.fori_loop(0, start // block, score_step, tuple(tops))
        acc[...] = jnp.zeros(acc.shape, F32)

        def value_step(j, sums):
            at = pl.multiple_of(j * block, block)
            tile_values = qkv_ref[pl.ds(at, block), 2 * PAIR : 3 * PAIR]
            found = []
            for h in range(2):
                powers = jnp.exp(kept[h, pl.ds(at, block), :] - tops[h])
                found.append(sums[h] + jnp.sum(powers, axis=0, keepdims=True))
                acc[h] += dot(powers.astype(BF16), tile_values, TN)
            return tuple(found)

        zero = jnp.zeros((1, block), F32)
        sums = lax.fori_loop(0, start // block + 1, value_step, (zero, zero))
        inverse = jnp.transpose(jnp.where(first, 1.0 / sums[0], 1.0 / sums[1]))
        lane = lax.broadcasted_iota(jnp.int32, (block, PAIR), 1) < HD
        local = slice(i * block, (i + 1) * block)
        mixed_ref[local, :] = (jnp.where(lane, acc[0], acc[1]) * inverse).astype(BF16)
        for h in range(2):
            total_ref[0, h : h + 1, local] = tops[h] + jnp.log(sums[h])


def attend(qkv, row0, rows, block, after=()):
    pairs = qkv.shape[1] // (3 * PAIR)
    return pl.pallas_call(
        functools.partial(attend_kernel, row0=row0, block=block),
        grid=(pairs,),
        in_specs=[pl.BlockSpec((row0 + rows, 3 * PAIR), lambda j: (0, j))]
        + [ANY_SPACE] * len(after),
        out_specs=[
            pl.BlockSpec((rows, PAIR), lambda j: (0, j)),
            pl.BlockSpec((1, 2, rows), lambda j: (j, 0, 0)),
        ],
        out_shape=[
            jax.ShapeDtypeStruct((rows, pairs * PAIR), BF16),
            jax.ShapeDtypeStruct((pairs, 2, rows), F32),
        ],
        scratch_shapes=[
            pltpu.VMEM((2, row0 + rows, block), F32),
            pltpu.VMEM((2, block, PAIR), F32),
        ],
        compiler_params=params(16),
        cost_estimate=cost(16 if row0 else 6),
        name="attend_%d" % row0,
    )(qkv, *after)


def attend_back_kernel(
    core_ref, qkv_ref, mixed_ref, grad_ref, total_ref, *rest, row0, block, has_before
):
    before_ref = rest[0]
    sent_ref = None
    if has_before:
        out_ref, sums_ref, sent_ref, key_acc, value_acc, query_acc = rest[-6:]
    else:
        out_ref, sums_ref, key_acc, value_acc, query_acc = rest[-5:]
    rows = mixed_ref.shape[0]
    count = rows // block
    lane = lax.broadcasted_iota(jnp.int32, (block, PAIR), 1)
    first = lane < HD
    causal = lax.broadcasted_iota(jnp.int32, (block, block), 0) <= lax.broadcasted_iota(
        jnp.int32, (block, block), 1
    )
    if has_before:
        key_acc[0:row0, :] = before_ref[:, PAIR : 2 * PAIR]
        value_acc[0:row0, :] = before_ref[:, 2 * PAIR : 3 * PAIR]
        key_acc[row0:, :] = jnp.zeros((rows, PAIR), F32)
        value_acc[row0:, :] = jnp.zeros((rows, PAIR), F32)
    else:
        key_acc[...] = jnp.zeros(key_acc.shape, F32)
        value_acc[...] = jnp.zeros(value_acc.shape, F32)
    for i in range(count):
        start = row0 + i * block
        local = slice(i * block, (i + 1) * block)
        query_heads = split_heads(
            qkv_ref[pl.ds(start, block), 0:PAIR].astype(F32) * (HD**-0.5)
        )
        grads = grad_ref[local, :].astype(F32)
        grad_heads = split_heads(grads)
        inner = jnp.transpose(grads * mixed_ref[local, :].astype(F32))
        total_rows = [total_ref[0, h : h + 1, local] for h in range(2)]
        inner_rows = [
            jnp.sum(inner[h * HD : (h + 1) * HD, :], axis=0, keepdims=True) for h in range(2)
        ]

        def tile(at, masked):
            tile_keys = qkv_ref[pl.ds(at, block), PAIR : 2 * PAIR]
            tile_values = qkv_ref[pl.ds(at, block), 2 * PAIR : 3 * PAIR]
            key_sum, value_sum = None, None
            for h in range(2):
                scores = dot(tile_keys, query_heads[h], NT)
                weights = jnp.exp(scores - total_rows[h])
                if masked:
                    weights = jnp.where(causal, weights, 0.0)
                grad_weights = dot(tile_values, grad_heads[h], NT)
                grad_scores = (weights * (grad_weights - inner_rows[h])).astype(BF16)
                value_part = dot(weights.astype(BF16), grad_heads[h], NN)
                key_part = dot(grad_scores, query_heads[h], NN)
                query_part = dot(grad_scores, tile_keys, TN)
                key_sum = key_part if key_sum is None else key_sum + key_part
                value_sum = value_part if value_sum is None else value_sum + value_part
                if masked:
                    query_acc[h] = query_part
                else:
                    query_acc[h] += query_part
            key_acc[pl.ds(at, block), :] += key_sum
            value_acc[pl.ds(at, block), :] += value_sum

        tile(start, True)

        def step(j, carry):
            tile(pl.multiple_of(j * block, block), False)
            return carry

        if start:
            lax.fori_loop(0, start // block, step, 0)
        query_grad = jnp.where(first, query_acc[0], query_acc[1]) * (HD**-0.5)
        out_ref[start : start + block, 0:PAIR] = query_grad.astype(out_ref.dtype)
    if has_before:
        out_ref[0:row0, 0:PAIR] = before_ref[:, 0:PAIR].astype(out_ref.dtype)
    out_ref[:, PAIR : 2 * PAIR] = key_acc[...].astype(out_ref.dtype)
    out_ref[:, 2 * PAIR : 3 * PAIR] = value_acc[...].astype(out_ref.dtype)
    sums_ref[...] = jnp.sum(out_ref[...].astype(F32), axis=0, keepdims=True)
    if has_before:
        size = sent_ref.shape[0] // 2
        for half in range(2):
            at = pl.multiple_of((2 * half + 1 - core_ref[0]) * size, size)
            sent_ref[half * size : (half + 1) * size, :] = out_ref[pl.ds(at, size), :]


def attend_back(qkv, mixed, grads, totals, before, row0, block, pair, pairs, after=(), core=None):
    rows = mixed.shape[0]
    extent = row0 + rows
    narrow = pl.BlockSpec((rows, PAIR), lambda j: (0, pair + j))
    in_specs = [
        SCALARS,
        pl.BlockSpec((extent, 3 * PAIR), lambda j: (0, pair + j)),
        narrow,
        narrow,
        pl.BlockSpec((1, 2, rows), lambda j: (pair + j, 0, 0)),
    ]
    core = jnp.zeros((), jnp.int32) if core is None else core
    operands = [core.reshape(1).astype(jnp.int32), qkv, mixed, grads, totals]
    if before is not None:
        in_specs.append(pl.BlockSpec((row0, 3 * PAIR), lambda j: (0, pair + j)))
        operands.append(before)
    in_specs += [ANY_SPACE] * len(after)
    return pl.pallas_call(
        functools.partial(
            attend_back_kernel, row0=row0, block=block, has_before=before is not None
        ),
        grid=(pairs,),
        in_specs=in_specs,
        out_specs=[
            pl.BlockSpec((extent, 3 * PAIR), lambda j: (0, j)),
            pl.BlockSpec((1, 3 * PAIR), lambda j: (0, j)),
        ]
        + ([] if before is None else [pl.BlockSpec((extent // 2, 3 * PAIR), lambda j: (0, j))]),
        out_shape=[
            jax.ShapeDtypeStruct((extent, pairs * 3 * PAIR), F32 if before is None else BF16),
            jax.ShapeDtypeStruct((1, pairs * 3 * PAIR), F32),
        ]
        + (
            []
            if before is None
            else [jax.ShapeDtypeStruct((extent // 2, pairs * 3 * PAIR), BF16)]
        ),
        scratch_shapes=[
            pltpu.VMEM((extent, PAIR), F32),
            pltpu.VMEM((extent, PAIR), F32),
            pltpu.VMEM((2, block, PAIR), F32),
        ],
        compiler_params=params(20),
        cost_estimate=cost(5.5 * pairs if before is None else 13 * pairs),
        name="attend_back_%d_%d" % (row0, pair),
    )(*operands, *after)


def norm_two_kernel(
    back_ref, recv_ref, residual_ref, cot_ref, vec_ref, proj_ref, *rest, steps
):
    grad_ref, branch_ref, both_ref, sums_ref = rest[-4:]
    z = back_ref[...].astype(F32) + recv_ref[...].astype(F32)
    unit, factor = normalize(residual_ref[...])
    cot = cot_ref[...].astype(F32)
    grad = cot + norm_back(unit, factor, vec_ref[4:5, :], z)
    grad_ref[...] = grad
    branch = grad.astype(BF16)
    branch_ref[...] = branch
    both_ref[...] = dot(branch, proj_ref[...], NN).astype(BF16)

    @pl.when(pl.program_id(0) == 0)
    def _():
        sums_ref[...] = jnp.zeros(sums_ref.shape, F32)

    for at, part in enumerate((branch.astype(F32), cot, z * unit, z)):
        sums_ref[at : at + 1, :] += jnp.sum(part, axis=0, keepdims=True)


def norm_two(back, recv, residual, cot, vectors, proj, after=()):
    rows, width = back.shape
    steps = 2
    block = rows // steps
    strip = pl.BlockSpec((block, width), lambda i: (i, 0))
    return pl.pallas_call(
        functools.partial(norm_two_kernel, steps=steps),
        grid=(steps,),
        in_specs=[
            strip,
            strip,
            strip,
            strip,
            pl.BlockSpec(vectors.shape, lambda i: (0, 0)),
            pl.BlockSpec(proj.shape, lambda i: (0, 0)),
        ]
        + [ANY_SPACE] * len(after),
        out_specs=[
            strip,
            strip,
            pl.BlockSpec((block, proj.shape[1]), lambda i: (i, 0)),
            pl.BlockSpec((8, width), lambda i: (0, 0)),
        ],
        out_shape=[
            jax.ShapeDtypeStruct((rows, width), F32),
            jax.ShapeDtypeStruct((rows, width), BF16),
            jax.ShapeDtypeStruct((rows, proj.shape[1]), BF16),
            jax.ShapeDtypeStruct((8, width), F32),
        ],
        compiler_params=params(10),
        cost_estimate=cost(4),
        name="norm_two",
    )(back, recv, residual, cot, vectors, proj, *after)


def norm_one_kernel(place_ref, low_ref, high_ref, *refs, terms):
    grads, weights = refs[:terms], refs[terms : 2 * terms]
    own_ref, sent_ref, sums_ref = refs[-3:]
    i = pl.program_id(0)
    z = None
    for grad_ref, weight_ref in zip(grads, weights):
        part = dot(grad_ref[...], weight_ref[...], NT)
        z = part if z is None else z + part
    rows = jnp.where(i == 0, low_ref[...].astype(F32), high_ref[...].astype(F32))
    unit, _ = normalize(rows)

    @pl.when(i == 0)
    def _():
        sums_ref[...] = jnp.zeros(sums_ref.shape, F32)

    sums_ref[0:1, :] += jnp.sum(z * unit, axis=0, keepdims=True)
    sums_ref[1:2, :] += jnp.sum(z, axis=0, keepdims=True)

    @pl.when(i == place_ref[0])
    def _():
        own_ref[...] = z

    @pl.when(i != place_ref[0])
    def _():
        sent_ref[...] = z.astype(BF16)


def norm_one(places, low, high, full, received, own_weights, sib_weights, after=()):
    rows, width = low.shape
    pairs = len(full)
    cols = full[0].shape[1]
    whole = pl.BlockSpec((rows, width), lambda i, at: (0, 0))
    weight_specs = [
        pl.BlockSpec((width, cols), functools.partial(lambda pair, i, at: (0, pair), pair))
        for pair in range(pairs)
    ]
    return pl.pallas_call(
        functools.partial(norm_one_kernel, terms=2 * pairs),
        grid_spec=pltpu.PrefetchScalarGridSpec(
            num_scalar_prefetch=1,
            grid=(2,),
            in_specs=[whole, whole]
            + [pl.BlockSpec((rows, cols), lambda i, at: (2 * i + at[1], 0))] * pairs
            + [pl.BlockSpec((rows, cols), lambda i, at: (i, 0))] * pairs
            + weight_specs * 2
            + [ANY_SPACE] * len(after),
            out_specs=[whole, whole, pl.BlockSpec((8, width), lambda i, at: (0, 0))],
        ),
        out_shape=[
            jax.ShapeDtypeStruct((rows, width), F32),
            jax.ShapeDtypeStruct((rows, width), BF16),
            jax.ShapeDtypeStruct((8, width), F32),
        ],
        compiler_params=params(20),
        cost_estimate=cost(8),
        name="norm_one",
    )(
        places,
        low,
        high,
        *full,
        *received,
        *[own_weights] * pairs,
        *[sib_weights] * pairs,
        *after,
    )


def norm_one_back_kernel(
    place_ref, input_ref, own_ref, recv_ref, low_ref, high_ref, vec_ref, out_ref
):
    unit, factor = normalize(input_ref[...].astype(F32))
    z = own_ref[...] + recv_ref[...].astype(F32)
    residual = jnp.where(place_ref[0] == 0, low_ref[...], high_ref[...])
    out_ref[...] = (residual + norm_back(unit, factor, vec_ref[2:3, :], z)).astype(BF16)


def norm_one_back(places, inputs, z_own, z_recv, residual_grads, vectors):
    rows, width = inputs.shape
    steps = 4
    strip = pl.BlockSpec((rows // steps, width), lambda i: (i, 0))
    return pl.pallas_call(
        norm_one_back_kernel,
        grid=(steps,),
        in_specs=[SCALARS]
        + [strip] * 5
        + [pl.BlockSpec(vectors.shape, lambda i: (0, 0))],
        out_specs=strip,
        out_shape=jax.ShapeDtypeStruct((rows, width), BF16),
        compiler_params=params(12),
        cost_estimate=cost(4),
        name="norm_one_back",
    )(places, inputs, z_own, z_recv, *residual_grads, vectors)


def tie_kernel(value_ref, *rest):
    pass


def tie(value, *after):
    return pl.pallas_call(
        tie_kernel,
        in_specs=[ANY_SPACE] * (1 + len(after)),
        out_specs=ANY_SPACE,
        out_shape=jax.ShapeDtypeStruct(value.shape, value.dtype),
        input_output_aliases={0: 0},
        cost_estimate=cost(0.1),
        name="tie",
    )(value, *after)


def place_kernel(me_ref, *refs, parts, side_rows):
    full_ref = refs[-1]
    rows = refs[0].shape[0] - side_rows
    for k in range(parts):
        at = lax.bitwise_xor(me_ref[0], k)
        full_ref[pl.ds(pl.multiple_of(at * rows, rows), rows), :] = refs[k][0:rows, :]
        if side_rows:
            side = pl.multiple_of(parts * rows + at * side_rows, side_rows)
            full_ref[pl.ds(side, side_rows), :] = refs[k][rows:, :]


def place_shares(me, pieces, side_rows, after):
    total, cols = pieces[0].shape
    parts, kind = len(pieces), pieces[0].dtype
    return pl.pallas_call(
        functools.partial(place_kernel, parts=parts, side_rows=side_rows),
        grid=(1,),
        in_specs=[SCALARS]
        + [pl.BlockSpec((total, cols), lambda i: (0, 0))] * parts
        + [ANY_SPACE] * len(after),
        out_specs=pl.BlockSpec((parts * total, cols), lambda i: (0, 0)),
        out_shape=jax.ShapeDtypeStruct((parts * total, cols), kind),
        compiler_params=params(18),
        cost_estimate=cost(3),
        name="place_shares",
    )(me.reshape(1).astype(jnp.int32), *pieces, *after)


def feed_grads_kernel(*refs, tiles, received):
    normed, cots, grads, acts = refs[0:2], refs[2:4], refs[4:6], refs[6:8]
    out_ref = refs[-1]
    i = pl.program_id(0)

    def work(left, right):
        total = dot(left[0][...], right[0][...], TN) + dot(left[1][...], right[1][...], TN)
        if received:
            total = total + refs[8][...].astype(F32)
        out_ref[...] = total.astype(BF16)

    @pl.when(i < tiles)
    def _():
        work(normed, grads)

    @pl.when(i >= tiles)
    def _():
        work(cots, acts)


def feed_grads(normed, cots, grads, acts, first, received, after=()):
    rows, width = normed[0].shape
    hidden_cols = grads[0].shape[1] // 2
    tile = min(512, hidden_cols)
    tiles = hidden_cols // tile
    base = first // tile
    whole = pl.BlockSpec((rows, width), lambda i: (0, 0))
    grad_spec = pl.BlockSpec((rows, tile), lambda i: (0, base + jnp.minimum(i, tiles - 1)))
    act_spec = pl.BlockSpec((rows, tile), lambda i: (0, base + jnp.maximum(i - tiles, 0)))
    out_spec = pl.BlockSpec((width, tile), lambda i: (0, i))
    return pl.pallas_call(
        functools.partial(feed_grads_kernel, tiles=tiles, received=received is not None),
        grid=(2 * tiles,),
        in_specs=[whole] * 4
        + [grad_spec] * 2
        + [act_spec] * 2
        + ([] if received is None else [out_spec])
        + [ANY_SPACE] * len(after),
        out_specs=out_spec,
        out_shape=jax.ShapeDtypeStruct((width, 2 * hidden_cols), BF16),
        compiler_params=params(24),
        cost_estimate=cost(6),
        name="feed_grads",
    )(*normed, *cots, *grads, *acts, *([] if received is None else [received]), *after)


def weight_grads_kernel(y_ref, normed_ref, grad_ref, *refs, with_proj):
    kept_ref, sent_ref = refs[-2:]
    share = kept_ref.shape[1]
    total = dot(normed_ref[...], grad_ref[...], TN)
    if with_proj:
        low_ref, high_ref, low_mixed_ref, high_mixed_ref, recv_ref = refs[:5]
        proj = dot(low_ref[...], low_mixed_ref[...], TN) + dot(
            high_ref[...], high_mixed_ref[...], TN
        )
        proj = proj + recv_ref[...].astype(F32)
        total = jnp.concatenate([total, proj], axis=1)
    even, odd = total[:share], total[share:]
    stays = y_ref[0] == 0
    kept_ref[0] = jnp.where(stays, even, odd)
    sent_ref[0] = jnp.where(stays, odd, even).astype(BF16)


def weight_grads(y, normed, grads, proj, after=()):
    length, width = normed.shape
    cols = grads.shape[1]
    steps, share = 4, width // 8
    in_specs = [
        SCALARS,
        pl.BlockSpec((length, 2 * share), lambda i: (0, i)),
        pl.BlockSpec((length, cols), lambda i: (0, 0)),
    ]
    operands = [y.reshape(1).astype(jnp.int32), normed, grads]
    total = cols
    if proj is not None:
        branches, mixed, received = proj
        rows, head_cols = mixed[0].shape
        total += head_cols
        in_specs += [pl.BlockSpec((rows, 2 * share), lambda i: (0, i))] * 2
        in_specs += [pl.BlockSpec((rows, head_cols), lambda i: (0, 0))] * 2
        in_specs += [pl.BlockSpec((2 * share, head_cols), lambda i: (i, 0))]
        operands += [*branches, *mixed, received]
    return pl.pallas_call(
        functools.partial(weight_grads_kernel, with_proj=proj is not None),
        grid=(steps,),
        in_specs=in_specs + [ANY_SPACE] * len(after),
        out_specs=[pl.BlockSpec((1, share, total), lambda i: (i, 0, 0))] * 2,
        out_shape=[
            jax.ShapeDtypeStruct((steps, share, total), F32),
            jax.ShapeDtypeStruct((steps, share, total), BF16),
        ],
        compiler_params=params(16),
        cost_estimate=cost(4),
        name="weight_grads",
    )(*operands, *after)


def finish_kernel(*refs, pairs, counts):
    qkv_ref, proj_ref, side_ref, fc_ref, out_ref = refs[-5:]
    feed_ref = refs[sum(counts)]
    hidden_cols = fc_ref.shape[1]
    fc_ref[...] = feed_ref[:, :hidden_cols].astype(F32)
    out_ref[...] = jnp.transpose(feed_ref[:, hidden_cols:].astype(F32))
    at = 0
    for pair in range(pairs):
        total = refs[at][...].astype(F32)
        for part in range(1, counts[pair]):
            total = total + refs[at + part][...].astype(F32)
        at += counts[pair]
        share = qkv_ref.shape[1]
        for j in range(3):
            qkv_ref[j, :, pair * PAIR : (pair + 1) * PAIR] = total[:share, j * PAIR : (j + 1) * PAIR]
        if pair == 0:
            proj_ref[...] = jnp.transpose(total[:share, 3 * PAIR :])
        if pair == pairs - 1:
            side_ref[...] = total[share:, : 3 * PAIR]


def finish(terms, feed_sum, share, head_cols, side_rows, after=()):
    pairs = len(terms)
    flat = [term for pair in terms for term in pair]
    hidden_cols = feed_sum.shape[1] // 2
    return pl.pallas_call(
        functools.partial(
            finish_kernel, pairs=pairs, counts=[len(pair) for pair in terms]
        ),
        grid=(1,),
        in_specs=[pl.BlockSpec(term.shape, lambda i: (0, 0)) for term in flat + [feed_sum]]
        + [ANY_SPACE] * len(after),
        out_specs=[
            pl.BlockSpec((3, share, head_cols), lambda i: (0, 0, 0)),
            pl.BlockSpec((head_cols, share), lambda i: (0, 0)),
            pl.BlockSpec((side_rows, 3 * PAIR), lambda i: (0, 0)),
            pl.BlockSpec((share, hidden_cols), lambda i: (0, 0)),
            pl.BlockSpec((hidden_cols, share), lambda i: (0, 0)),
        ],
        out_shape=[
            jax.ShapeDtypeStruct((3, share, head_cols), F32),
            jax.ShapeDtypeStruct((head_cols, share), F32),
            jax.ShapeDtypeStruct((side_rows, 3 * PAIR), F32),
            jax.ShapeDtypeStruct((share, hidden_cols), F32),
            jax.ShapeDtypeStruct((hidden_cols, share), F32),
        ],
        compiler_params=params(60),
        cost_estimate=cost(3),
        name="finish",
    )(*flat, feed_sum, *after)


def project_kernel(rows_ref, vec_ref, shift_ref, weight_ref, *rest):
    normed_ref, out_ref = rest[-2:]
    unit, _ = normalize(rows_ref[...].astype(F32))
    normed_ref[...] = (unit * vec_ref[2:3, :] + vec_ref[3:4, :]).astype(BF16)
    out_ref[...] = (dot(normed_ref[...], weight_ref[...], NN) + shift_ref[...]).astype(BF16)


def project(sequence, vectors, shift, weights, block, after=()):
    length, width = sequence.shape
    cols = shift.shape[1]
    return pl.pallas_call(
        project_kernel,
        grid=(length // block,),
        in_specs=[
            pl.BlockSpec((block, width), lambda i: (i, 0)),
            pl.BlockSpec(vectors.shape, lambda i: (0, 0)),
            pl.BlockSpec(shift.shape, lambda i: (0, 0)),
            pl.BlockSpec((width, cols), lambda i: (0, 0)),
        ]
        + [ANY_SPACE] * len(after),
        out_specs=[
            pl.BlockSpec((block, width), lambda i: (i, 0)),
            pl.BlockSpec((block, cols), lambda i: (i, 0)),
        ],
        out_shape=[
            jax.ShapeDtypeStruct((length, width), BF16),
            jax.ShapeDtypeStruct((length, cols), BF16),
        ],
        compiler_params=params(16),
        cost_estimate=cost(6),
        name="project",
    )(sequence, vectors, shift, weights, *after)


def feed_kernel(
    base_ref,
    part_ref,
    recv_ref,
    cot_ref,
    vec_ref,
    shift_own_ref,
    shift_sib_ref,
    fc_own_ref,
    out_own_ref,
    fc_sib_ref,
    out_sib_ref,
    *rest,
    tiles,
):
    residual_ref, normed_ref, act_ref, grad_ref, back_ref, sent_ref, sums_ref = rest[-9:-2]
    back_acc, out_acc = rest[-2:]
    i = pl.program_id(0)
    rows = base_ref.shape[0]

    @pl.when(i == 0)
    def _():
        residual = (
            base_ref[...].astype(F32)
            + part_ref[...].astype(F32)
            + recv_ref[...].astype(F32)
            + vec_ref[0:1, :]
        )
        residual_ref[...] = residual
        unit, _ = normalize(residual)
        normed_ref[...] = (unit * vec_ref[4:5, :] + vec_ref[5:6, :]).astype(BF16)
        back_acc[...] = jnp.zeros(back_acc.shape, F32)
        out_acc[...] = jnp.zeros(out_acc.shape, F32)

    def work(shift_ref, fc_ref, out_ref):
        step = rows // 2
        total = None
        for r in range(2):
            at = slice(r * step, (r + 1) * step)
            hidden = dot(normed_ref[at, :], fc_ref[...], NN) + shift_ref[...]
            grad_act = dot(cot_ref[at, :], out_ref[...], NN)
            act, slope = gelu_both(hidden)
            act = act.astype(BF16)
            grad = (grad_act * slope).astype(BF16)
            act_ref[at, :] = act
            grad_ref[at, :] = grad
            part = jnp.sum(grad.astype(F32), axis=0, keepdims=True)
            total = part if total is None else total + part
            back_acc[at, :] += dot(grad, fc_ref[...], NT)
            out_acc[at, :] += dot(act, out_ref[...], NT)
        sums_ref[...] = total

    @pl.when(i < tiles)
    def _():
        work(shift_own_ref, fc_own_ref, out_own_ref)

    @pl.when(i >= tiles)
    def _():
        work(shift_sib_ref, fc_sib_ref, out_sib_ref)

    @pl.when(i == 2 * tiles - 1)
    def _():
        back_ref[...] = back_acc[...].astype(BF16)
        sent_ref[...] = out_acc[...].astype(BF16)


def feed(base, part, recv, cot, vectors, shift_own, shift_sib, own, sib, after=()):
    rows, width = base.shape
    hidden_cols = shift_own.shape[1]
    tile = min(512, hidden_cols)
    tiles = hidden_cols // tile
    whole = pl.BlockSpec((rows, width), lambda i: (0, 0))

    def low(i):
        return jnp.minimum(i, tiles - 1)

    def high(i):
        return jnp.maximum(i - tiles, 0)

    return pl.pallas_call(
        functools.partial(feed_kernel, tiles=tiles),
        grid=(2 * tiles,),
        in_specs=[
            whole,
            whole,
            whole,
            whole,
            pl.BlockSpec(vectors.shape, lambda i: (0, 0)),
            pl.BlockSpec((1, tile), lambda i: (0, low(i))),
            pl.BlockSpec((1, tile), lambda i: (0, high(i))),
            pl.BlockSpec((width, tile), lambda i: (0, low(i))),
            pl.BlockSpec((width, tile), lambda i: (0, tiles + low(i))),
            pl.BlockSpec((width, tile), lambda i: (0, high(i))),
            pl.BlockSpec((width, tile), lambda i: (0, tiles + high(i))),
        ]
        + [ANY_SPACE] * len(after),
        out_specs=[
            whole,
            whole,
            pl.BlockSpec((rows, tile), lambda i: (0, i)),
            pl.BlockSpec((rows, tile), lambda i: (0, i)),
            whole,
            whole,
            pl.BlockSpec((1, tile), lambda i: (0, i)),
        ],
        out_shape=[
            jax.ShapeDtypeStruct((rows, width), F32),
            jax.ShapeDtypeStruct((rows, width), BF16),
            jax.ShapeDtypeStruct((rows, 2 * hidden_cols), BF16),
            jax.ShapeDtypeStruct((rows, 2 * hidden_cols), BF16),
            jax.ShapeDtypeStruct((rows, width), BF16),
            jax.ShapeDtypeStruct((rows, width), BF16),
            jax.ShapeDtypeStruct((1, 2 * hidden_cols), F32),
        ],
        scratch_shapes=[pltpu.VMEM((rows, width), F32), pltpu.VMEM((rows, width), F32)],
        compiler_params=params(32),
        cost_estimate=cost(16),
        name="feed",
    )(
        base, part, recv, cot, vectors, shift_own, shift_sib, own, own, sib, sib, *after
    )


def swap_dp(value, mask):
    size = lax.axis_size("dp")
    return lax.ppermute(value, "dp", [(i, i ^ mask) for i in range(size)])


def gather_z(shard):
    return {k: swap_dp(shard, k) for k in (6, 4, 2)}


def gather_whole(shard, side_rows):
    rows, cols = shard.shape[0] - side_rows, shard.shape[1]
    full = lax.all_gather(shard, "dp", axis=0)
    return jnp.concatenate(
        [full[:, :rows].reshape(-1, cols), full[:, rows:].reshape(-1, cols)], axis=0
    )


def scatter_y(sent, parts):
    return swap_dp(sent, 1) if parts == 8 else None


def scatter_z(kept, sent, received, side, parts):
    if parts != 8:
        whole = jnp.concatenate([kept, sent.astype(F32)], axis=1)
        whole = whole.reshape(parts, -1, whole.shape[2])
        if side is not None:
            whole = jnp.concatenate([whole, side], axis=1)
        return [lax.psum_scatter(whole.astype(BF16), "dp", scatter_dimension=0)]
    sums = kept + received.astype(F32)
    z = lax.axis_index("dp") // 2
    terms = [lax.dynamic_index_in_dim(sums, z, 0, keepdims=False)]
    for k in (3, 2, 1):
        sent = lax.dynamic_index_in_dim(sums, z ^ k, 0, keepdims=False).astype(BF16)
        terms.append(swap_dp(sent, 2 * k))
    return terms


def local(
    inputs,
    qkv_weight,
    qv_bias,
    proj_weight,
    proj_bias,
    fc_weight,
    fc_bias,
    out_weight,
    out_bias,
    attn_norm_gain,
    attn_norm_bias,
    mlp_norm_gain,
    mlp_norm_bias,
    cotangent,
):
    width = inputs.shape[1]
    rows = inputs.shape[0]
    share = proj_bias.shape[0]
    parts = width // share
    head_cols = qkv_weight.shape[2]
    pairs = head_cols // PAIR
    qkv_cols = 3 * head_cols
    hidden_cols = fc_weight.shape[1]
    place = lax.axis_index("tensor")
    core = place % 2
    is_low = place < 2
    is_first = core == 0

    def pick_x(low, high):
        return jnp.where(is_low, low, high)

    mlp_shard = jnp.concatenate([fc_weight, out_weight.T], axis=1)
    qv_row = jnp.pad(qv_bias.reshape(-1), (0, share - qv_bias.size))
    vectors = jnp.stack(
        [
            proj_bias,
            out_bias,
            attn_norm_gain,
            attn_norm_bias,
            mlp_norm_gain,
            mlp_norm_bias,
            fc_bias,
            qv_row,
        ]
    )
    qkv_shard = jnp.transpose(
        qkv_weight.reshape(3, share, pairs, PAIR), (1, 2, 0, 3)
    ).reshape(share, qkv_cols)
    attn_shard = jnp.concatenate([qkv_shard, proj_weight.T], axis=1)
    side_rows = 16
    vectors = jnp.pad(
        vectors.reshape(1, -1), ((0, side_rows - 1), (0, attn_shard.shape[1] - vectors.size))
    )
    attn_shard = jnp.concatenate([attn_shard, vectors], axis=0)

    input_x_sent = swap_x(inputs)
    input_core = swap_core(inputs)
    cot_x = swap_x(cotangent)
    blocks = []

    def assemble(late):
        input_x = tie(input_x_sent, *late)
        input_far = swap_core(input_x)
        low, high = pick_x(inputs, input_x), pick_x(input_x, inputs)
        far_low, far_high = pick_x(input_core, input_far), pick_x(input_far, input_core)
        sequence = jnp.concatenate(
            [
                jnp.where(is_first, low, far_low),
                jnp.where(is_first, far_low, low),
                jnp.where(is_first, high, far_high),
                jnp.where(is_first, far_high, high),
            ],
            axis=0,
        )
        blocks.extend([low, high, sequence])
        return (sequence, cot_x)

    if parts == 8:
        shares = {0: attn_shard, **gather_z(attn_shard)}
        mlp_shares = {0: mlp_shard, 1: swap_dp(mlp_shard, 1)}
        for k in (0, 2, 4, 6):
            shares[k + 1] = swap_dp(shares[k], 1)
        mlp_shares.update(gather_z(tie(mlp_shard, *(shares[k] for k in (2, 4, 6)))))
        behind = tuple(shares[k] for k in (6, 5, 3, 1)) + (mlp_shares[1], mlp_shares[4])
        for k in (2, 4):
            mlp_shares[k + 1] = swap_dp(mlp_shares[k], 1)
        attn_all = place_shares(
            lax.axis_index("dp"),
            [shares[k] for k in range(parts)],
            side_rows,
            assemble(behind),
        )
        early = (mlp_shares[3], mlp_shares[5], mlp_shares[6])
    else:
        attn_all = gather_whole(attn_shard, side_rows)
        assemble((attn_all,))
        early = ()
    input_low, input_high, sequence = blocks
    attn_sib = swap_core(attn_all)
    vectors = attn_all[width:].reshape(parts, side_rows, -1)[:, 0, : 8 * share]
    vectors = vectors.reshape(parts, 8, share).transpose(1, 0, 2).reshape(8, width)
    columns = vectors.astype(F32)
    out_shift, gain_one = columns[1:2], columns[2:3]
    fc_shift_own = columns[6:7]
    fc_shift_sib = attn_sib[width:].reshape(parts, side_rows, -1)[:, 0, 6 * share : 7 * share]
    fc_shift_sib = fc_shift_sib.reshape(1, width).astype(F32)
    qv_shift = (
        columns[7]
        .reshape(parts, share)[:, : share // 2]
        .reshape(parts, 2, share // 4)
        .transpose(1, 0, 2)
        .reshape(2, head_cols)
    )
    qkv_shift = jnp.stack([qv_shift[0], jnp.zeros_like(qv_shift[0]), qv_shift[1]])
    qkv_shift = qkv_shift.reshape(3, pairs, PAIR).transpose(1, 0, 2).reshape(1, qkv_cols)
    proj_both = jnp.concatenate(
        [
            attn_all[:width, qkv_cols : qkv_cols + head_cols],
            attn_sib[:width, qkv_cols : qkv_cols + head_cols],
        ],
        axis=1,
    )

    normed_one, qkv = project(sequence, columns, qkv_shift, attn_all, rows)
    cots = [pick_x(cotangent, cot_x), pick_x(cot_x, cotangent)]

    inputs_two = [input_low, input_high]
    mixed, totals, mixed_own, mixed_sib, parts_two, received_two = [], [], [], [], [], []
    for half in range(2):
        half_mixed, half_totals = attend(
            qkv, half * 2 * rows, 2 * rows, rows, after=tuple(parts_two) + early * half
        )
        mixed.append(half_mixed)
        totals.append(half_totals)
        two = half_mixed.reshape(2, rows, head_cols)
        mine = jnp.where(is_first, two[0], two[1])
        received = swap_core(jnp.where(is_first, two[1], two[0]))
        both = jnp.concatenate([mine, received], axis=1)
        mixed_own.append(mine)
        mixed_sib.append(received)
        part = dot(both, proj_both, NT).astype(BF16)
        parts_two.append(part)
        received_two.append(swap_x(part))
    if parts == 8:
        mlp_shares[7] = swap_dp(mlp_shares[6], 1)
        mlp_all = place_shares(
            lax.axis_index("dp"),
            [mlp_shares[k] for k in range(parts)],
            0,
            (received_two[0], parts_two[1]),
        )
    else:
        mlp_all = gather_whole(mlp_shard, 0)
    mlp_sib = swap_core(mlp_all)
    residuals, normed_two, acts, grads_hidden, backs, out_parts = [], [], [], [], [], []
    fc_bias_sums = 0.0
    for half in range(2):
        residual, normed, act, grad_hidden, back, out_part, sums = feed(
            inputs_two[half],
            parts_two[half],
            received_two[half],
            cots[half],
            columns,
            fc_shift_own,
            fc_shift_sib,
            mlp_all,
            mlp_sib,
            after=(parts_two[1],),
        )
        residuals.append(residual)
        normed_two.append(normed)
        acts.append(act)
        grads_hidden.append(grad_hidden)
        backs.append(back)
        out_parts.append(out_part)
        fc_bias_sums = fc_bias_sums + sums[0]
    back_recv = [swap_x(back) for back in backs]

    sib_grads = feed_grads(
        normed_two, cots, grads_hidden, acts, hidden_cols, None, after=(back_recv[0],)
    )
    sib_received = swap_core(sib_grads)

    grad_residuals, branches, grads_mixed = [], [], []
    for half in range(2):
        grad_residual, branch, grad_both, sums_two = norm_two(
            backs[half],
            back_recv[half],
            residuals[half],
            cots[half],
            columns,
            proj_both,
            after=(sib_grads,) if half == 0 else (low_grads,),
        )
        grad_residuals.append(grad_residual)
        branches.append(branch)
        mine = grad_both[:, :head_cols]
        received = swap_core(grad_both[:, head_cols:])
        grads_mixed.append(
            jnp.concatenate(
                [jnp.where(is_first, mine, received), jnp.where(is_first, received, mine)], axis=0
            )
        )
        vec_two = sums_two if half == 0 else vec_two + sums_two
        if half == 0:
            grad_mlp = feed_grads(
                normed_two, cots, grads_hidden, acts, 0, sib_received, after=(branch,)
            )
            mlp_sum = lax.psum_scatter(grad_mlp, "dp", scatter_dimension=0, tiled=True)
            low_grads, _ = attend_back(
                qkv,
                mixed[0],
                grads_mixed[0],
                totals[0],
                None,
                0,
                rows,
                0,
                pairs,
                after=(grad_mlp,),
            )
    proj_sib = dot(branches[0], mixed_sib[0], TN) + dot(branches[1], mixed_sib[1], TN)
    proj_received = swap_core(proj_sib.astype(BF16))

    out_sent = tie(pick_x(out_parts[1], out_parts[0]), low_grads)
    out_recv = swap_x(out_sent)

    y = lax.axis_index("dp") % 2 if parts == 8 else jnp.zeros((), jnp.int32)
    place_ids = jnp.stack([place // 2, core]).astype(jnp.int32)
    full_grads, grads_received, side_sums, exchanges = [], [], [], []
    after = ()
    for pair in range(pairs):
        grad_pair, pair_sums, grad_sent = attend_back(
            qkv,
            mixed[1],
            grads_mixed[1],
            totals[1],
            low_grads,
            2 * rows,
            rows,
            pair,
            1,
            after=after,
            core=core,
        )
        full_grads.append(grad_pair)
        side_sums.append(pair_sums)
        if pair > 0 and parts == 8:
            grad_sent = tie(grad_sent, exchanges[-1][2])
        grads_received.append(swap_core(grad_sent))
        proj = (branches, mixed_own, proj_received) if pair == 0 else None
        if pair == 0:
            out_recv = tie(out_recv, grad_pair)
        kept, sent = weight_grads(y, normed_one, grad_pair, proj)
        received = scatter_y(sent, parts) if pair < pairs - 1 else None
        exchanges.append((kept, sent, received))
        after = (sent, out_recv)

    z_own, z_sent, vec_one = norm_one(
        place_ids,
        input_low,
        input_high,
        full_grads,
        grads_received,
        attn_all,
        attn_sib,
        after=(exchanges[-1][1],),
    )
    first_terms = scatter_z(*exchanges[0], side=None, parts=parts)
    z_recv = swap_x(z_sent)
    vec_two = vec_two + swap_core(vec_two)
    fc_bias_grad = fc_bias_sums[:hidden_cols] + swap_core(fc_bias_sums[hidden_cols:])

    vec_grads = jnp.concatenate(
        [
            vec_two[:2],
            vec_one[:2],
            vec_two[2:4],
            fc_bias_grad[None],
            jnp.zeros((1, width), F32),
        ],
        axis=0,
    )
    vec_blocks = vec_grads.reshape(8, parts, share).transpose(1, 0, 2)
    vec_blocks = jnp.pad(vec_blocks, ((0, 0), (0, 0), (0, 3 * PAIR - share)))
    pair_rows = jnp.pad(jnp.concatenate(side_sums, axis=0), ((0, 8 - pairs), (0, 0)))
    side = jnp.concatenate(
        [vec_blocks, jnp.broadcast_to(pair_rows[None], (parts, 8, 3 * PAIR))], axis=1
    )
    views = side.reshape((-1, 2) + side.shape[1:])
    side_kept = lax.dynamic_index_in_dim(views, y, 1, keepdims=False)
    side_sent = lax.dynamic_index_in_dim(views, 1 - y, 1, keepdims=False)
    terms = [first_terms]
    for pair in range(1, pairs):
        kept, sent, received = exchanges[pair]
        last = pair == pairs - 1
        if last and parts == 8:
            kept = jnp.concatenate([kept, side_kept], axis=1)
            sent = jnp.concatenate([sent, side_sent.astype(BF16)], axis=1)
            received = tie(scatter_y(sent, parts), *first_terms[1:])
        terms.append(scatter_z(kept, sent, received, side if last else None, parts))

    out_recv = tie(out_recv, *terms[-1][1:])
    out_mine = pick_x(out_parts[0], out_parts[1])
    outputs = (
        pick_x(residuals[0], residuals[1])
        + out_mine.astype(F32)
        + out_recv.astype(F32)
        + out_shift
    ).astype(BF16)

    qkv_out, proj_out, six, fc_out, out_out = finish(
        terms, mlp_sum, share, head_cols, side_rows, after=(outputs, z_recv)
    )
    grad_inputs = norm_one_back(
        place_ids, inputs, z_own, tie(z_recv, six), grad_residuals, columns
    )
    one = six[2:4, :share]
    far = lax.ppermute(one, "tensor", [(i, i ^ 3) for i in range(4)])
    two = one + swap_core(one) + swap_x(one) + far
    piece = share // 4
    start = lax.axis_index("dp") * piece
    mine = lax.dynamic_index_in_dim(six[8 : 8 + pairs], start // PAIR, 0, keepdims=False)
    qv_out = lax.dynamic_slice_in_dim(mine.reshape(3, PAIR), start % PAIR, piece, 1)[0::2]
    return (
        outputs,
        grad_inputs,
        qkv_out,
        qv_out,
        proj_out,
        six[0, :share],
        fc_out,
        six[6, :share],
        out_out,
        six[1, :share],
        two[0],
        two[1],
        six[4, :share],
        six[5, :share],
    )


def solution(mesh):
    rows = P(("dp", "tensor"), None)
    vector = P("dp")
    wide = P(("tensor", "dp"))
    weights = (
        P(None, "dp", "tensor"),
        P(None, ("tensor", "dp")),
        P("tensor", "dp"),
        vector,
        P("dp", "tensor"),
        wide,
        P("tensor", "dp"),
        vector,
        vector,
        vector,
        vector,
        vector,
    )
    return jax.shard_map(
        local,
        mesh=mesh,
        in_specs=(rows, *weights, rows),
        out_specs=(rows, rows, *weights),
        check_vma=False,
    )
```

```python
import functools

import jax
import jax.numpy as jnp
from jax import lax
from jax.experimental import pallas as pl
from jax.experimental.pallas import tpu as pltpu
from jax.sharding import PartitionSpec as P

HD = 64
PAIR = 2 * HD
EPSILON = 1e-05
NEGATIVE = -1e30
ROOT_TWO_PI = 0.7978845608028654
F32 = jnp.float32
BF16 = jnp.bfloat16
MIB = 1024 * 1024
SCALE = 0.25
ANY_SPACE = pl.BlockSpec(memory_space=pl.ANY)
SCALARS = pl.BlockSpec(memory_space=pltpu.SMEM)


def params(mib):
    return pltpu.CompilerParams(vmem_limit_bytes=mib * MIB)


def cost(micros):
    return pl.CostEstimate(
        flops=int(micros * SCALE * 1.1e9),
        bytes_accessed=int(micros * SCALE * 1e6),
        transcendentals=0,
    )


def swap_x(value):
    return lax.ppermute(value, "tensor", [(0, 2), (2, 0), (1, 3), (3, 1)])


def swap_core(value):
    return lax.ppermute(value, "tensor", [(0, 1), (1, 0), (2, 3), (3, 2)])


def dot(a, b, contract, kind=F32):
    return lax.dot_general(a, b, (contract, ((), ())), preferred_element_type=kind)


NN = ((1,), (0,))
NT = ((1,), (1,))
TN = ((0,), (0,))


def normalize(values):
    average = jnp.mean(values, axis=-1, keepdims=True)
    centered = values - average
    spread = jnp.mean(centered * centered, axis=-1, keepdims=True)
    factor = lax.rsqrt(spread + EPSILON)
    return centered * factor, factor


def norm_back(unit, factor, gain, grad):
    scaled = grad * gain
    return factor * (
        scaled
        - jnp.mean(scaled, axis=-1, keepdims=True)
        - unit * jnp.mean(scaled * unit, axis=-1, keepdims=True)
    )


def gelu_both(values):
    squared = values * values
    bent = jnp.tanh(ROOT_TWO_PI * values * (1.0 + 0.044715 * squared))
    half = 0.5 * (1.0 + bent)
    slope = half + 0.5 * values * (1.0 - bent * bent) * ROOT_TWO_PI * (
        1.0 + 3.0 * 0.044715 * squared
    )
    return values * half, slope


def split_heads(block):
    first = lax.broadcasted_iota(jnp.int32, block.shape, 1) < HD
    return [jnp.where(first, block, 0.0).astype(BF16), jnp.where(first, 0.0, block).astype(BF16)]


def attend_kernel(qkv_ref, *rest, row0, block):
    mixed_ref, total_ref, kept, acc = rest[-4:]
    count = mixed_ref.shape[0] // block
    first = lax.broadcasted_iota(jnp.int32, (PAIR, block), 0) < HD
    causal = lax.broadcasted_iota(jnp.int32, (block, block), 0) <= lax.broadcasted_iota(
        jnp.int32, (block, block), 1
    )
    for i in range(count):
        start = row0 + i * block
        heads = split_heads(qkv_ref[pl.ds(start, block), 0:PAIR].astype(F32) * (HD**-0.5))
        keys = qkv_ref[pl.ds(start, block), PAIR : 2 * PAIR]
        tops = []
        for h in range(2):
            scores = jnp.where(causal, dot(keys, heads[h], NT), NEGATIVE)
            kept[h, pl.ds(start, block), :] = scores
            tops.append(jnp.max(scores, axis=0, keepdims=True))

        def score_step(j, tops):
            at = pl.multiple_of(j * block, block)
            tile_keys = qkv_ref[pl.ds(at, block), PAIR : 2 * PAIR]
            found = []
            for h in range(2):
                scores = dot(tile_keys, heads[h], NT)
                kept[h, pl.ds(at, block), :] = scores
                found.append(jnp.maximum(tops[h], jnp.max(scores, axis=0, keepdims=True)))
            return tuple(found)

        tops = lax.fori_loop(0, start // block, score_step, tuple(tops))
        acc[...] = jnp.zeros(acc.shape, F32)

        def value_step(j, sums):
            at = pl.multiple_of(j * block, block)
            tile_values = qkv_ref[pl.ds(at, block), 2 * PAIR : 3 * PAIR]
            found = []
            for h in range(2):
                powers = jnp.exp(kept[h, pl.ds(at, block), :] - tops[h])
                found.append(sums[h] + jnp.sum(powers, axis=0, keepdims=True))
                acc[h] += dot(powers.astype(BF16), tile_values, TN)
            return tuple(found)

        zero = jnp.zeros((1, block), F32)
        sums = lax.fori_loop(0, start // block + 1, value_step, (zero, zero))
        inverse = jnp.transpose(jnp.where(first, 1.0 / sums[0], 1.0 / sums[1]))
        lane = lax.broadcasted_iota(jnp.int32, (block, PAIR), 1) < HD
        local = slice(i * block, (i + 1) * block)
        mixed_ref[local, :] = (jnp.where(lane, acc[0], acc[1]) * inverse).astype(BF16)
        for h in range(2):
            total_ref[0, h : h + 1, local] = tops[h] + jnp.log(sums[h])


def attend(qkv, row0, rows, block, after=()):
    pairs = qkv.shape[1] // (3 * PAIR)
    return pl.pallas_call(
        functools.partial(attend_kernel, row0=row0, block=block),
        grid=(pairs,),
        in_specs=[pl.BlockSpec((row0 + rows, 3 * PAIR), lambda j: (0, j))]
        + [ANY_SPACE] * len(after),
        out_specs=[
            pl.BlockSpec((rows, PAIR), lambda j: (0, j)),
            pl.BlockSpec((1, 2, rows), lambda j: (j, 0, 0)),
        ],
        out_shape=[
            jax.ShapeDtypeStruct((rows, pairs * PAIR), BF16),
            jax.ShapeDtypeStruct((pairs, 2, rows), F32),
        ],
        scratch_shapes=[
            pltpu.VMEM((2, row0 + rows, block), F32),
            pltpu.VMEM((2, block, PAIR), F32),
        ],
        compiler_params=params(16),
        cost_estimate=cost(16 if row0 else 6),
        name="attend_%d" % row0,
    )(qkv, *after)


def attend_back_kernel(
    core_ref, qkv_ref, mixed_ref, grad_ref, total_ref, *rest, row0, block, has_before
):
    before_ref = rest[0]
    sent_ref = None
    if has_before:
        out_ref, sums_ref, sent_ref, key_acc, value_acc, query_acc = rest[-6:]
    else:
        out_ref, sums_ref, key_acc, value_acc, query_acc = rest[-5:]
    rows = mixed_ref.shape[0]
    count = rows // block
    lane = lax.broadcasted_iota(jnp.int32, (block, PAIR), 1)
    first = lane < HD
    causal = lax.broadcasted_iota(jnp.int32, (block, block), 0) <= lax.broadcasted_iota(
        jnp.int32, (block, block), 1
    )
    if has_before:
        key_acc[0:row0, :] = before_ref[:, PAIR : 2 * PAIR]
        value_acc[0:row0, :] = before_ref[:, 2 * PAIR : 3 * PAIR]
        key_acc[row0:, :] = jnp.zeros((rows, PAIR), F32)
        value_acc[row0:, :] = jnp.zeros((rows, PAIR), F32)
    else:
        key_acc[...] = jnp.zeros(key_acc.shape, F32)
        value_acc[...] = jnp.zeros(value_acc.shape, F32)
    for i in range(count):
        start = row0 + i * block
        local = slice(i * block, (i + 1) * block)
        query_heads = split_heads(
            qkv_ref[pl.ds(start, block), 0:PAIR].astype(F32) * (HD**-0.5)
        )
        grads = grad_ref[local, :].astype(F32)
        grad_heads = split_heads(grads)
        inner = jnp.transpose(grads * mixed_ref[local, :].astype(F32))
        total_rows = [total_ref[0, h : h + 1, local] for h in range(2)]
        inner_rows = [
            jnp.sum(inner[h * HD : (h + 1) * HD, :], axis=0, keepdims=True) for h in range(2)
        ]

        def tile(at, masked):
            tile_keys = qkv_ref[pl.ds(at, block), PAIR : 2 * PAIR]
            tile_values = qkv_ref[pl.ds(at, block), 2 * PAIR : 3 * PAIR]
            key_sum, value_sum = None, None
            for h in range(2):
                scores = dot(tile_keys, query_heads[h], NT)
                weights = jnp.exp(scores - total_rows[h])
                if masked:
                    weights = jnp.where(causal, weights, 0.0)
                grad_weights = dot(tile_values, grad_heads[h], NT)
                grad_scores = (weights * (grad_weights - inner_rows[h])).astype(BF16)
                value_part = dot(weights.astype(BF16), grad_heads[h], NN)
                key_part = dot(grad_scores, query_heads[h], NN)
                query_part = dot(grad_scores, tile_keys, TN)
                key_sum = key_part if key_sum is None else key_sum + key_part
                value_sum = value_part if value_sum is None else value_sum + value_part
                if masked:
                    query_acc[h] = query_part
                else:
                    query_acc[h] += query_part
            key_acc[pl.ds(at, block), :] += key_sum
            value_acc[pl.ds(at, block), :] += value_sum

        tile(start, True)

        def step(j, carry):
            tile(pl.multiple_of(j * block, block), False)
            return carry

        if start:
            lax.fori_loop(0, start // block, step, 0)
        query_grad = jnp.where(first, query_acc[0], query_acc[1]) * (HD**-0.5)
        out_ref[start : start + block, 0:PAIR] = query_grad.astype(out_ref.dtype)
    if has_before:
        out_ref[0:row0, 0:PAIR] = before_ref[:, 0:PAIR].astype(out_ref.dtype)
    out_ref[:, PAIR : 2 * PAIR] = key_acc[...].astype(out_ref.dtype)
    out_ref[:, 2 * PAIR : 3 * PAIR] = value_acc[...].astype(out_ref.dtype)
    sums_ref[...] = jnp.sum(out_ref[...].astype(F32), axis=0, keepdims=True)
    if has_before:
        size = sent_ref.shape[0] // 2
        for half in range(2):
            at = pl.multiple_of((2 * half + 1 - core_ref[0]) * size, size)
            sent_ref[half * size : (half + 1) * size, :] = out_ref[pl.ds(at, size), :]


def attend_back(qkv, mixed, grads, totals, before, row0, block, pair, pairs, after=(), core=None):
    rows = mixed.shape[0]
    extent = row0 + rows
    narrow = pl.BlockSpec((rows, PAIR), lambda j: (0, pair + j))
    in_specs = [
        SCALARS,
        pl.BlockSpec((extent, 3 * PAIR), lambda j: (0, pair + j)),
        narrow,
        narrow,
        pl.BlockSpec((1, 2, rows), lambda j: (pair + j, 0, 0)),
    ]
    core = jnp.zeros((), jnp.int32) if core is None else core
    operands = [core.reshape(1).astype(jnp.int32), qkv, mixed, grads, totals]
    if before is not None:
        in_specs.append(pl.BlockSpec((row0, 3 * PAIR), lambda j: (0, pair + j)))
        operands.append(before)
    in_specs += [ANY_SPACE] * len(after)
    return pl.pallas_call(
        functools.partial(
            attend_back_kernel, row0=row0, block=block, has_before=before is not None
        ),
        grid=(pairs,),
        in_specs=in_specs,
        out_specs=[
            pl.BlockSpec((extent, 3 * PAIR), lambda j: (0, j)),
            pl.BlockSpec((1, 3 * PAIR), lambda j: (0, j)),
        ]
        + ([] if before is None else [pl.BlockSpec((extent // 2, 3 * PAIR), lambda j: (0, j))]),
        out_shape=[
            jax.ShapeDtypeStruct((extent, pairs * 3 * PAIR), F32 if before is None else BF16),
            jax.ShapeDtypeStruct((1, pairs * 3 * PAIR), F32),
        ]
        + (
            []
            if before is None
            else [jax.ShapeDtypeStruct((extent // 2, pairs * 3 * PAIR), BF16)]
        ),
        scratch_shapes=[
            pltpu.VMEM((extent, PAIR), F32),
            pltpu.VMEM((extent, PAIR), F32),
            pltpu.VMEM((2, block, PAIR), F32),
        ],
        compiler_params=params(20),
        cost_estimate=cost(5.5 * pairs if before is None else 13 * pairs),
        name="attend_back_%d_%d" % (row0, pair),
    )(*operands, *after)


def norm_two_kernel(
    back_ref, recv_ref, residual_ref, cot_ref, vec_ref, proj_ref, *rest, steps
):
    grad_ref, branch_ref, both_ref, sums_ref = rest[-4:]
    z = back_ref[...].astype(F32) + recv_ref[...].astype(F32)
    unit, factor = normalize(residual_ref[...])
    cot = cot_ref[...].astype(F32)
    grad = cot + norm_back(unit, factor, vec_ref[4:5, :], z)
    grad_ref[...] = grad
    branch = grad.astype(BF16)
    branch_ref[...] = branch
    both_ref[...] = dot(branch, proj_ref[...], NN).astype(BF16)

    @pl.when(pl.program_id(0) == 0)
    def _():
        sums_ref[...] = jnp.zeros(sums_ref.shape, F32)

    for at, part in enumerate((branch.astype(F32), cot, z * unit, z)):
        sums_ref[at : at + 1, :] += jnp.sum(part, axis=0, keepdims=True)


def norm_two(back, recv, residual, cot, vectors, proj, after=()):
    rows, width = back.shape
    steps = 2
    block = rows // steps
    strip = pl.BlockSpec((block, width), lambda i: (i, 0))
    return pl.pallas_call(
        functools.partial(norm_two_kernel, steps=steps),
        grid=(steps,),
        in_specs=[
            strip,
            strip,
            strip,
            strip,
            pl.BlockSpec(vectors.shape, lambda i: (0, 0)),
            pl.BlockSpec(proj.shape, lambda i: (0, 0)),
        ]
        + [ANY_SPACE] * len(after),
        out_specs=[
            strip,
            strip,
            pl.BlockSpec((block, proj.shape[1]), lambda i: (i, 0)),
            pl.BlockSpec((8, width), lambda i: (0, 0)),
        ],
        out_shape=[
            jax.ShapeDtypeStruct((rows, width), F32),
            jax.ShapeDtypeStruct((rows, width), BF16),
            jax.ShapeDtypeStruct((rows, proj.shape[1]), BF16),
            jax.ShapeDtypeStruct((8, width), F32),
        ],
        compiler_params=params(10),
        cost_estimate=cost(4),
        name="norm_two",
    )(back, recv, residual, cot, vectors, proj, *after)


def norm_one_kernel(place_ref, low_ref, high_ref, *refs, terms):
    grads, weights = refs[:terms], refs[terms : 2 * terms]
    own_ref, sent_ref, sums_ref = refs[-3:]
    i = pl.program_id(0)
    z = None
    for grad_ref, weight_ref in zip(grads, weights):
        part = dot(grad_ref[...], weight_ref[...], NT)
        z = part if z is None else z + part
    rows = jnp.where(i == 0, low_ref[...].astype(F32), high_ref[...].astype(F32))
    unit, _ = normalize(rows)

    @pl.when(i == 0)
    def _():
        sums_ref[...] = jnp.zeros(sums_ref.shape, F32)

    sums_ref[0:1, :] += jnp.sum(z * unit, axis=0, keepdims=True)
    sums_ref[1:2, :] += jnp.sum(z, axis=0, keepdims=True)

    @pl.when(i == place_ref[0])
    def _():
        own_ref[...] = z

    @pl.when(i != place_ref[0])
    def _():
        sent_ref[...] = z.astype(BF16)


def norm_one(places, low, high, full, received, own_weights, sib_weights, after=()):
    rows, width = low.shape
    pairs = len(full)
    cols = full[0].shape[1]
    whole = pl.BlockSpec((rows, width), lambda i, at: (0, 0))
    weight_specs = [
        pl.BlockSpec((width, cols), functools.partial(lambda pair, i, at: (0, pair), pair))
        for pair in range(pairs)
    ]
    return pl.pallas_call(
        functools.partial(norm_one_kernel, terms=2 * pairs),
        grid_spec=pltpu.PrefetchScalarGridSpec(
            num_scalar_prefetch=1,
            grid=(2,),
            in_specs=[whole, whole]
            + [pl.BlockSpec((rows, cols), lambda i, at: (2 * i + at[1], 0))] * pairs
            + [pl.BlockSpec((rows, cols), lambda i, at: (i, 0))] * pairs
            + weight_specs * 2
            + [ANY_SPACE] * len(after),
            out_specs=[whole, whole, pl.BlockSpec((8, width), lambda i, at: (0, 0))],
        ),
        out_shape=[
            jax.ShapeDtypeStruct((rows, width), F32),
            jax.ShapeDtypeStruct((rows, width), BF16),
            jax.ShapeDtypeStruct((8, width), F32),
        ],
        compiler_params=params(20),
        cost_estimate=cost(8),
        name="norm_one",
    )(
        places,
        low,
        high,
        *full,
        *received,
        *[own_weights] * pairs,
        *[sib_weights] * pairs,
        *after,
    )


def norm_one_back_kernel(
    place_ref, input_ref, own_ref, recv_ref, low_ref, high_ref, vec_ref, out_ref
):
    unit, factor = normalize(input_ref[...].astype(F32))
    z = own_ref[...] + recv_ref[...].astype(F32)
    residual = jnp.where(place_ref[0] == 0, low_ref[...], high_ref[...])
    out_ref[...] = (residual + norm_back(unit, factor, vec_ref[2:3, :], z)).astype(BF16)


def norm_one_back(places, inputs, z_own, z_recv, residual_grads, vectors):
    rows, width = inputs.shape
    steps = 4
    strip = pl.BlockSpec((rows // steps, width), lambda i: (i, 0))
    return pl.pallas_call(
        norm_one_back_kernel,
        grid=(steps,),
        in_specs=[SCALARS]
        + [strip] * 5
        + [pl.BlockSpec(vectors.shape, lambda i: (0, 0))],
        out_specs=strip,
        out_shape=jax.ShapeDtypeStruct((rows, width), BF16),
        compiler_params=params(60),
        cost_estimate=cost(4),
        name="norm_one_back",
    )(places, inputs, z_own, z_recv, *residual_grads, vectors)


def tie_kernel(value_ref, *rest):
    pass


def tie(value, *after):
    return pl.pallas_call(
        tie_kernel,
        in_specs=[ANY_SPACE] * (1 + len(after)),
        out_specs=ANY_SPACE,
        out_shape=jax.ShapeDtypeStruct(value.shape, value.dtype),
        input_output_aliases={0: 0},
        cost_estimate=cost(0.1),
        name="tie",
    )(value, *after)


def place_kernel(me_ref, *refs, parts, side_rows):
    full_ref = refs[-1]
    rows = refs[0].shape[0] - side_rows
    for k in range(parts):
        at = lax.bitwise_xor(me_ref[0], k)
        full_ref[pl.ds(pl.multiple_of(at * rows, rows), rows), :] = refs[k][0:rows, :]
        if side_rows:
            side = pl.multiple_of(parts * rows + at * side_rows, side_rows)
            full_ref[pl.ds(side, side_rows), :] = refs[k][rows:, :]


def place_shares(me, pieces, side_rows, after):
    total, cols = pieces[0].shape
    parts, kind = len(pieces), pieces[0].dtype
    return pl.pallas_call(
        functools.partial(place_kernel, parts=parts, side_rows=side_rows),
        grid=(1,),
        in_specs=[SCALARS]
        + [pl.BlockSpec((total, cols), lambda i: (0, 0))] * parts
        + [ANY_SPACE] * len(after),
        out_specs=pl.BlockSpec((parts * total, cols), lambda i: (0, 0)),
        out_shape=jax.ShapeDtypeStruct((parts * total, cols), kind),
        compiler_params=params(18),
        cost_estimate=cost(3),
        name="place_shares",
    )(me.reshape(1).astype(jnp.int32), *pieces, *after)


def feed_grads_kernel(*refs, tiles, received):
    normed, cots, grads, acts = refs[0:2], refs[2:4], refs[4:6], refs[6:8]
    out_ref = refs[-1]
    i = pl.program_id(0)

    def work(left, right):
        total = dot(left[0][...], right[0][...], TN) + dot(left[1][...], right[1][...], TN)
        if received:
            total = total + refs[8][...].astype(F32)
        out_ref[...] = total.astype(BF16)

    @pl.when(i < tiles)
    def _():
        work(normed, grads)

    @pl.when(i >= tiles)
    def _():
        work(cots, acts)


def feed_grads(normed, cots, grads, acts, first, received, after=()):
    rows, width = normed[0].shape
    hidden_cols = grads[0].shape[1] // 2
    tile = min(512, hidden_cols)
    tiles = hidden_cols // tile
    base = first // tile
    whole = pl.BlockSpec((rows, width), lambda i: (0, 0))
    grad_spec = pl.BlockSpec((rows, tile), lambda i: (0, base + jnp.minimum(i, tiles - 1)))
    act_spec = pl.BlockSpec((rows, tile), lambda i: (0, base + jnp.maximum(i - tiles, 0)))
    out_spec = pl.BlockSpec((width, tile), lambda i: (0, i))
    return pl.pallas_call(
        functools.partial(feed_grads_kernel, tiles=tiles, received=received is not None),
        grid=(2 * tiles,),
        in_specs=[whole] * 4
        + [grad_spec] * 2
        + [act_spec] * 2
        + ([] if received is None else [out_spec])
        + [ANY_SPACE] * len(after),
        out_specs=out_spec,
        out_shape=jax.ShapeDtypeStruct((width, 2 * hidden_cols), BF16),
        compiler_params=params(24),
        cost_estimate=cost(6),
        name="feed_grads",
    )(*normed, *cots, *grads, *acts, *([] if received is None else [received]), *after)


def weight_grads_kernel(y_ref, normed_ref, grad_ref, *refs, with_proj):
    kept_ref, sent_ref = refs[-2:]
    share = kept_ref.shape[1]
    total = dot(normed_ref[...], grad_ref[...], TN)
    if with_proj:
        low_ref, high_ref, low_mixed_ref, high_mixed_ref, recv_ref = refs[:5]
        proj = dot(low_ref[...], low_mixed_ref[...], TN) + dot(
            high_ref[...], high_mixed_ref[...], TN
        )
        proj = proj + recv_ref[...].astype(F32)
        total = jnp.concatenate([total, proj], axis=1)
    even, odd = total[:share], total[share:]
    stays = y_ref[0] == 0
    kept_ref[0] = jnp.where(stays, even, odd)
    sent_ref[0] = jnp.where(stays, odd, even).astype(BF16)


def weight_grads(y, normed, grads, proj, after=()):
    length, width = normed.shape
    cols = grads.shape[1]
    steps, share = 4, width // 8
    in_specs = [
        SCALARS,
        pl.BlockSpec((length, 2 * share), lambda i: (0, i)),
        pl.BlockSpec((length, cols), lambda i: (0, 0)),
    ]
    operands = [y.reshape(1).astype(jnp.int32), normed, grads]
    total = cols
    if proj is not None:
        branches, mixed, received = proj
        rows, head_cols = mixed[0].shape
        total += head_cols
        in_specs += [pl.BlockSpec((rows, 2 * share), lambda i: (0, i))] * 2
        in_specs += [pl.BlockSpec((rows, head_cols), lambda i: (0, 0))] * 2
        in_specs += [pl.BlockSpec((2 * share, head_cols), lambda i: (i, 0))]
        operands += [*branches, *mixed, received]
    return pl.pallas_call(
        functools.partial(weight_grads_kernel, with_proj=proj is not None),
        grid=(steps,),
        in_specs=in_specs + [ANY_SPACE] * len(after),
        out_specs=[pl.BlockSpec((1, share, total), lambda i: (i, 0, 0))] * 2,
        out_shape=[
            jax.ShapeDtypeStruct((steps, share, total), F32),
            jax.ShapeDtypeStruct((steps, share, total), BF16),
        ],
        compiler_params=params(16),
        cost_estimate=cost(4),
        name="weight_grads",
    )(*operands, *after)


def finish_kernel(*refs, pairs, counts):
    qkv_ref, proj_ref, side_ref, fc_ref, out_ref = refs[-5:]
    feed_ref = refs[sum(counts)]
    hidden_cols = fc_ref.shape[1]
    fc_ref[...] = feed_ref[:, :hidden_cols].astype(F32)
    out_ref[...] = jnp.transpose(feed_ref[:, hidden_cols:].astype(F32))
    at = 0
    for pair in range(pairs):
        total = refs[at][...].astype(F32)
        for part in range(1, counts[pair]):
            total = total + refs[at + part][...].astype(F32)
        at += counts[pair]
        share = qkv_ref.shape[1]
        for j in range(3):
            qkv_ref[j, :, pair * PAIR : (pair + 1) * PAIR] = total[:share, j * PAIR : (j + 1) * PAIR]
        if pair == 0:
            proj_ref[...] = jnp.transpose(total[:share, 3 * PAIR :])
        if pair == pairs - 1:
            side_ref[...] = total[share:, : 3 * PAIR]


def finish(terms, feed_sum, share, head_cols, side_rows, after=()):
    pairs = len(terms)
    flat = [term for pair in terms for term in pair]
    hidden_cols = feed_sum.shape[1] // 2
    return pl.pallas_call(
        functools.partial(
            finish_kernel, pairs=pairs, counts=[len(pair) for pair in terms]
        ),
        grid=(1,),
        in_specs=[pl.BlockSpec(term.shape, lambda i: (0, 0)) for term in flat + [feed_sum]]
        + [ANY_SPACE] * len(after),
        out_specs=[
            pl.BlockSpec((3, share, head_cols), lambda i: (0, 0, 0)),
            pl.BlockSpec((head_cols, share), lambda i: (0, 0)),
            pl.BlockSpec((side_rows, 3 * PAIR), lambda i: (0, 0)),
            pl.BlockSpec((share, hidden_cols), lambda i: (0, 0)),
            pl.BlockSpec((hidden_cols, share), lambda i: (0, 0)),
        ],
        out_shape=[
            jax.ShapeDtypeStruct((3, share, head_cols), F32),
            jax.ShapeDtypeStruct((head_cols, share), F32),
            jax.ShapeDtypeStruct((side_rows, 3 * PAIR), F32),
            jax.ShapeDtypeStruct((share, hidden_cols), F32),
            jax.ShapeDtypeStruct((hidden_cols, share), F32),
        ],
        compiler_params=params(60),
        cost_estimate=cost(3),
        name="finish",
    )(*flat, feed_sum, *after)


def project_kernel(rows_ref, vec_ref, shift_ref, weight_ref, *rest):
    normed_ref, out_ref = rest[-2:]
    unit, _ = normalize(rows_ref[...].astype(F32))
    normed_ref[...] = (unit * vec_ref[2:3, :] + vec_ref[3:4, :]).astype(BF16)
    out_ref[...] = (dot(normed_ref[...], weight_ref[...], NN) + shift_ref[...]).astype(BF16)


def project(sequence, vectors, shift, weights, block, after=()):
    length, width = sequence.shape
    cols = shift.shape[1]
    return pl.pallas_call(
        project_kernel,
        grid=(length // block,),
        in_specs=[
            pl.BlockSpec((block, width), lambda i: (i, 0)),
            pl.BlockSpec(vectors.shape, lambda i: (0, 0)),
            pl.BlockSpec(shift.shape, lambda i: (0, 0)),
            pl.BlockSpec((width, cols), lambda i: (0, 0)),
        ]
        + [ANY_SPACE] * len(after),
        out_specs=[
            pl.BlockSpec((block, width), lambda i: (i, 0)),
            pl.BlockSpec((block, cols), lambda i: (i, 0)),
        ],
        out_shape=[
            jax.ShapeDtypeStruct((length, width), BF16),
            jax.ShapeDtypeStruct((length, cols), BF16),
        ],
        compiler_params=params(16),
        cost_estimate=cost(6),
        name="project",
    )(sequence, vectors, shift, weights, *after)


def feed_kernel(
    base_ref,
    part_ref,
    recv_ref,
    cot_ref,
    vec_ref,
    shift_own_ref,
    shift_sib_ref,
    fc_own_ref,
    out_own_ref,
    fc_sib_ref,
    out_sib_ref,
    *rest,
    tiles,
):
    residual_ref, normed_ref, act_ref, grad_ref, back_ref, sent_ref, sums_ref = rest[-9:-2]
    back_acc, out_acc = rest[-2:]
    i = pl.program_id(0)
    rows = base_ref.shape[0]

    @pl.when(i == 0)
    def _():
        residual = (
            base_ref[...].astype(F32)
            + part_ref[...].astype(F32)
            + recv_ref[...].astype(F32)
            + vec_ref[0:1, :]
        )
        residual_ref[...] = residual
        unit, _ = normalize(residual)
        normed_ref[...] = (unit * vec_ref[4:5, :] + vec_ref[5:6, :]).astype(BF16)
        back_acc[...] = jnp.zeros(back_acc.shape, F32)
        out_acc[...] = jnp.zeros(out_acc.shape, F32)

    def work(shift_ref, fc_ref, out_ref):
        step = rows // 2
        total = None
        for r in range(2):
            at = slice(r * step, (r + 1) * step)
            hidden = dot(normed_ref[at, :], fc_ref[...], NN) + shift_ref[...]
            grad_act = dot(cot_ref[at, :], out_ref[...], NN)
            act, slope = gelu_both(hidden)
            act = act.astype(BF16)
            grad = (grad_act * slope).astype(BF16)
            act_ref[at, :] = act
            grad_ref[at, :] = grad
            part = jnp.sum(grad.astype(F32), axis=0, keepdims=True)
            total = part if total is None else total + part
            back_acc[at, :] += dot(grad, fc_ref[...], NT)
            out_acc[at, :] += dot(act, out_ref[...], NT)
        sums_ref[...] = total

    @pl.when(i < tiles)
    def _():
        work(shift_own_ref, fc_own_ref, out_own_ref)

    @pl.when(i >= tiles)
    def _():
        work(shift_sib_ref, fc_sib_ref, out_sib_ref)

    @pl.when(i == 2 * tiles - 1)
    def _():
        back_ref[...] = back_acc[...].astype(BF16)
        sent_ref[...] = out_acc[...].astype(BF16)


def feed(base, part, recv, cot, vectors, shift_own, shift_sib, own, sib, after=()):
    rows, width = base.shape
    hidden_cols = shift_own.shape[1]
    tile = min(512, hidden_cols)
    tiles = hidden_cols // tile
    whole = pl.BlockSpec((rows, width), lambda i: (0, 0))

    def low(i):
        return jnp.minimum(i, tiles - 1)

    def high(i):
        return jnp.maximum(i - tiles, 0)

    return pl.pallas_call(
        functools.partial(feed_kernel, tiles=tiles),
        grid=(2 * tiles,),
        in_specs=[
            whole,
            whole,
            whole,
            whole,
            pl.BlockSpec(vectors.shape, lambda i: (0, 0)),
            pl.BlockSpec((1, tile), lambda i: (0, low(i))),
            pl.BlockSpec((1, tile), lambda i: (0, high(i))),
            pl.BlockSpec((width, tile), lambda i: (0, low(i))),
            pl.BlockSpec((width, tile), lambda i: (0, tiles + low(i))),
            pl.BlockSpec((width, tile), lambda i: (0, high(i))),
            pl.BlockSpec((width, tile), lambda i: (0, tiles + high(i))),
        ]
        + [ANY_SPACE] * len(after),
        out_specs=[
            whole,
            whole,
            pl.BlockSpec((rows, tile), lambda i: (0, i)),
            pl.BlockSpec((rows, tile), lambda i: (0, i)),
            whole,
            whole,
            pl.BlockSpec((1, tile), lambda i: (0, i)),
        ],
        out_shape=[
            jax.ShapeDtypeStruct((rows, width), F32),
            jax.ShapeDtypeStruct((rows, width), BF16),
            jax.ShapeDtypeStruct((rows, 2 * hidden_cols), BF16),
            jax.ShapeDtypeStruct((rows, 2 * hidden_cols), BF16),
            jax.ShapeDtypeStruct((rows, width), BF16),
            jax.ShapeDtypeStruct((rows, width), BF16),
            jax.ShapeDtypeStruct((1, 2 * hidden_cols), F32),
        ],
        scratch_shapes=[pltpu.VMEM((rows, width), F32), pltpu.VMEM((rows, width), F32)],
        compiler_params=params(32),
        cost_estimate=cost(16),
        name="feed",
    )(
        base, part, recv, cot, vectors, shift_own, shift_sib, own, own, sib, sib, *after
    )


def swap_dp(value, mask):
    size = lax.axis_size("dp")
    return lax.ppermute(value, "dp", [(i, i ^ mask) for i in range(size)])


def gather_z(shard):
    return {k: swap_dp(shard, k) for k in (6, 4, 2)}


def gather_whole(shard, side_rows):
    rows, cols = shard.shape[0] - side_rows, shard.shape[1]
    full = lax.all_gather(shard, "dp", axis=0)
    return jnp.concatenate(
        [full[:, :rows].reshape(-1, cols), full[:, rows:].reshape(-1, cols)], axis=0
    )


def scatter_y(sent, parts):
    return swap_dp(sent, 1) if parts == 8 else None


def scatter_z(kept, sent, received, side, parts):
    if parts != 8:
        whole = jnp.concatenate([kept, sent.astype(F32)], axis=1)
        whole = whole.reshape(parts, -1, whole.shape[2])
        if side is not None:
            whole = jnp.concatenate([whole, side], axis=1)
        return [lax.psum_scatter(whole.astype(BF16), "dp", scatter_dimension=0)]
    sums = kept + received.astype(F32)
    z = lax.axis_index("dp") // 2
    terms = [lax.dynamic_index_in_dim(sums, z, 0, keepdims=False)]
    for k in (3, 2, 1):
        sent = lax.dynamic_index_in_dim(sums, z ^ k, 0, keepdims=False).astype(BF16)
        terms.append(swap_dp(sent, 2 * k))
    return terms


def local(
    inputs,
    qkv_weight,
    qv_bias,
    proj_weight,
    proj_bias,
    fc_weight,
    fc_bias,
    out_weight,
    out_bias,
    attn_norm_gain,
    attn_norm_bias,
    mlp_norm_gain,
    mlp_norm_bias,
    cotangent,
):
    width = inputs.shape[1]
    rows = inputs.shape[0]
    share = proj_bias.shape[0]
    parts = width // share
    head_cols = qkv_weight.shape[2]
    pairs = head_cols // PAIR
    qkv_cols = 3 * head_cols
    hidden_cols = fc_weight.shape[1]
    place = lax.axis_index("tensor")
    core = place % 2
    is_low = place < 2
    is_first = core == 0

    def pick_x(low, high):
        return jnp.where(is_low, low, high)

    mlp_shard = jnp.concatenate([fc_weight, out_weight.T], axis=1)
    qv_row = jnp.pad(qv_bias.reshape(-1), (0, share - qv_bias.size))
    vectors = jnp.stack(
        [
            proj_bias,
            out_bias,
            attn_norm_gain,
            attn_norm_bias,
            mlp_norm_gain,
            mlp_norm_bias,
            fc_bias,
            qv_row,
        ]
    )
    qkv_shard = jnp.transpose(
        qkv_weight.reshape(3, share, pairs, PAIR), (1, 2, 0, 3)
    ).reshape(share, qkv_cols)
    attn_shard = jnp.concatenate([qkv_shard, proj_weight.T], axis=1)
    side_rows = 16
    vectors = jnp.pad(
        vectors.reshape(1, -1), ((0, side_rows - 1), (0, attn_shard.shape[1] - vectors.size))
    )
    attn_shard = jnp.concatenate([attn_shard, vectors], axis=0)

    input_x_sent = swap_x(inputs)
    input_core = swap_core(inputs)
    cot_x = swap_x(cotangent)
    blocks = []

    def assemble(late):
        input_x = tie(input_x_sent, *late)
        input_far = swap_core(input_x)
        low, high = pick_x(inputs, input_x), pick_x(input_x, inputs)
        far_low, far_high = pick_x(input_core, input_far), pick_x(input_far, input_core)
        sequence = jnp.concatenate(
            [
                jnp.where(is_first, low, far_low),
                jnp.where(is_first, far_low, low),
                jnp.where(is_first, high, far_high),
                jnp.where(is_first, far_high, high),
            ],
            axis=0,
        )
        blocks.extend([low, high, sequence])
        return (sequence,)

    if parts == 8:
        shares = {0: attn_shard, **gather_z(attn_shard)}
        mlp_shares = {0: mlp_shard, 1: swap_dp(mlp_shard, 1)}
        for k in (0, 2, 4, 6):
            shares[k + 1] = swap_dp(shares[k], 1)
        mlp_shares.update(gather_z(tie(mlp_shard, *(shares[k] for k in (2, 4, 6)))))
        behind = tuple(shares[k] for k in (6, 5, 3, 1))
        behind += (mlp_shares[1], mlp_shares[2], cot_x)
        for k in (2, 4):
            mlp_shares[k + 1] = swap_dp(mlp_shares[k], 1)
        attn_all = place_shares(
            lax.axis_index("dp"),
            [shares[k] for k in range(parts)],
            side_rows,
            assemble(behind),
        )
        early = (mlp_shares[3], mlp_shares[4], mlp_shares[6])
    else:
        attn_all = gather_whole(attn_shard, side_rows)
        assemble((attn_all,))
        early = ()
    input_low, input_high, sequence = blocks
    attn_sib = swap_core(attn_all)
    vectors = attn_all[width:].reshape(parts, side_rows, -1)[:, 0, : 8 * share]
    vectors = vectors.reshape(parts, 8, share).transpose(1, 0, 2).reshape(8, width)
    columns = vectors.astype(F32)
    out_shift, gain_one = columns[1:2], columns[2:3]
    fc_shift_own = columns[6:7]
    fc_shift_sib = attn_sib[width:].reshape(parts, side_rows, -1)[:, 0, 6 * share : 7 * share]
    fc_shift_sib = fc_shift_sib.reshape(1, width).astype(F32)
    qv_shift = (
        columns[7]
        .reshape(parts, share)[:, : share // 2]
        .reshape(parts, 2, share // 4)
        .transpose(1, 0, 2)
        .reshape(2, head_cols)
    )
    qkv_shift = jnp.stack([qv_shift[0], jnp.zeros_like(qv_shift[0]), qv_shift[1]])
    qkv_shift = qkv_shift.reshape(3, pairs, PAIR).transpose(1, 0, 2).reshape(1, qkv_cols)
    proj_both = jnp.concatenate(
        [
            attn_all[:width, qkv_cols : qkv_cols + head_cols],
            attn_sib[:width, qkv_cols : qkv_cols + head_cols],
        ],
        axis=1,
    )

    normed_one, qkv = project(sequence, columns, qkv_shift, attn_all, rows)
    cots = [pick_x(cotangent, cot_x), pick_x(cot_x, cotangent)]

    inputs_two = [input_low, input_high]
    mixed, totals, mixed_own, mixed_sib, parts_two, received_two = [], [], [], [], [], []
    for half in range(2):
        half_mixed, half_totals = attend(
            qkv, half * 2 * rows, 2 * rows, rows, after=tuple(parts_two) + early * half
        )
        mixed.append(half_mixed)
        totals.append(half_totals)
        two = half_mixed.reshape(2, rows, head_cols)
        mine = jnp.where(is_first, two[0], two[1])
        received = swap_core(jnp.where(is_first, two[1], two[0]))
        both = jnp.concatenate([mine, received], axis=1)
        mixed_own.append(mine)
        mixed_sib.append(received)
        part = dot(both, proj_both, NT).astype(BF16)
        parts_two.append(part)
        received_two.append(swap_x(part))
    if parts == 8:
        mlp_shares[7] = swap_dp(mlp_shares[6], 1)
        mlp_all = place_shares(
            lax.axis_index("dp"),
            [mlp_shares[k] for k in range(parts)],
            0,
            (received_two[0], parts_two[1]),
        )
    else:
        mlp_all = gather_whole(mlp_shard, 0)
    mlp_sib = swap_core(mlp_all)
    residuals, normed_two, acts, grads_hidden, backs, out_parts = [], [], [], [], [], []
    fc_bias_sums = 0.0
    for half in range(2):
        residual, normed, act, grad_hidden, back, out_part, sums = feed(
            inputs_two[half],
            parts_two[half],
            received_two[half],
            cots[half],
            columns,
            fc_shift_own,
            fc_shift_sib,
            mlp_all,
            mlp_sib,
            after=(parts_two[1],),
        )
        residuals.append(residual)
        normed_two.append(normed)
        acts.append(act)
        grads_hidden.append(grad_hidden)
        backs.append(back)
        out_parts.append(out_part)
        fc_bias_sums = fc_bias_sums + sums[0]
    back_recv = [swap_x(back) for back in backs]

    sib_grads = feed_grads(
        normed_two, cots, grads_hidden, acts, hidden_cols, None, after=(back_recv[0],)
    )
    sib_received = swap_core(sib_grads)

    grad_residuals, branches, grads_mixed = [], [], []
    for half in range(2):
        grad_residual, branch, grad_both, sums_two = norm_two(
            backs[half],
            back_recv[half],
            residuals[half],
            cots[half],
            columns,
            proj_both,
            after=(sib_grads,) if half == 0 else (low_grads,),
        )
        grad_residuals.append(grad_residual)
        branches.append(branch)
        mine = grad_both[:, :head_cols]
        received = swap_core(grad_both[:, head_cols:])
        grads_mixed.append(
            jnp.concatenate(
                [jnp.where(is_first, mine, received), jnp.where(is_first, received, mine)], axis=0
            )
        )
        vec_two = sums_two if half == 0 else vec_two + sums_two
        if half == 0:
            grad_mlp = feed_grads(
                normed_two, cots, grads_hidden, acts, 0, sib_received, after=(branch,)
            )
            mlp_sum = lax.psum_scatter(grad_mlp, "dp", scatter_dimension=0, tiled=True)
            low_grads, _ = attend_back(
                qkv,
                mixed[0],
                grads_mixed[0],
                totals[0],
                None,
                0,
                rows,
                0,
                pairs,
                after=(grad_mlp,),
            )
    proj_sib = dot(branches[0], mixed_sib[0], TN) + dot(branches[1], mixed_sib[1], TN)
    proj_received = swap_core(proj_sib.astype(BF16))

    out_sent = tie(pick_x(out_parts[1], out_parts[0]), low_grads)
    out_recv = swap_x(out_sent)

    y = lax.axis_index("dp") % 2 if parts == 8 else jnp.zeros((), jnp.int32)
    place_ids = jnp.stack([place // 2, core]).astype(jnp.int32)
    full_grads, grads_received, side_sums, exchanges = [], [], [], []
    after = ()
    for pair in range(pairs):
        grad_pair, pair_sums, grad_sent = attend_back(
            qkv,
            mixed[1],
            grads_mixed[1],
            totals[1],
            low_grads,
            2 * rows,
            rows,
            pair,
            1,
            after=after,
            core=core,
        )
        full_grads.append(grad_pair)
        side_sums.append(pair_sums)
        if pair > 0 and parts == 8:
            grad_sent = tie(grad_sent, exchanges[-1][2])
        grads_received.append(swap_core(grad_sent))
        proj = (branches, mixed_own, proj_received) if pair == 0 else None
        if pair == 0:
            out_recv = tie(out_recv, grad_pair)
        kept, sent = weight_grads(y, normed_one, grad_pair, proj)
        received = scatter_y(sent, parts) if pair < pairs - 1 else None
        exchanges.append((kept, sent, received))
        after = (sent, out_recv)

    z_own, z_sent, vec_one = norm_one(
        place_ids,
        input_low,
        input_high,
        full_grads,
        grads_received,
        attn_all,
        attn_sib,
        after=(exchanges[-1][1],),
    )
    first_terms = scatter_z(*exchanges[0], side=None, parts=parts)
    z_recv = swap_x(z_sent)
    vec_two = vec_two + swap_core(vec_two)
    fc_bias_grad = fc_bias_sums[:hidden_cols] + swap_core(fc_bias_sums[hidden_cols:])

    vec_grads = jnp.concatenate(
        [
            vec_two[:2],
            vec_one[:2],
            vec_two[2:4],
            fc_bias_grad[None],
            jnp.zeros((1, width), F32),
        ],
        axis=0,
    )
    vec_blocks = vec_grads.reshape(8, parts, share).transpose(1, 0, 2)
    vec_blocks = jnp.pad(vec_blocks, ((0, 0), (0, 0), (0, 3 * PAIR - share)))
    pair_rows = jnp.pad(jnp.concatenate(side_sums, axis=0), ((0, 8 - pairs), (0, 0)))
    side = jnp.concatenate(
        [vec_blocks, jnp.broadcast_to(pair_rows[None], (parts, 8, 3 * PAIR))], axis=1
    )
    views = side.reshape((-1, 2) + side.shape[1:])
    side_kept = lax.dynamic_index_in_dim(views, y, 1, keepdims=False)
    side_sent = lax.dynamic_index_in_dim(views, 1 - y, 1, keepdims=False)
    terms = [first_terms]
    for pair in range(1, pairs):
        kept, sent, received = exchanges[pair]
        last = pair == pairs - 1
        if last and parts == 8:
            kept = jnp.concatenate([kept, side_kept], axis=1)
            sent = jnp.concatenate([sent, side_sent.astype(BF16)], axis=1)
            received = tie(scatter_y(sent, parts), *first_terms[1:])
        terms.append(scatter_z(kept, sent, received, side if last else None, parts))

    out_recv = tie(out_recv, z_sent)
    out_mine = pick_x(out_parts[0], out_parts[1])
    outputs = (
        pick_x(residuals[0], residuals[1])
        + out_mine.astype(F32)
        + out_recv.astype(F32)
        + out_shift
    ).astype(BF16)

    qkv_out, proj_out, six, fc_out, out_out = finish(
        terms, mlp_sum, share, head_cols, side_rows, after=(outputs, z_recv)
    )
    grad_inputs = norm_one_back(
        place_ids, inputs, z_own, tie(z_recv, six), grad_residuals, columns
    )
    one = six[2:4, :share]
    far = lax.ppermute(one, "tensor", [(i, i ^ 3) for i in range(4)])
    two = one + swap_core(one) + swap_x(one) + far
    piece = share // 4
    start = lax.axis_index("dp") * piece
    mine = lax.dynamic_index_in_dim(six[8 : 8 + pairs], start // PAIR, 0, keepdims=False)
    qv_out = lax.dynamic_slice_in_dim(mine.reshape(3, PAIR), start % PAIR, piece, 1)[0::2]
    return (
        outputs,
        grad_inputs,
        qkv_out,
        qv_out,
        proj_out,
        six[0, :share],
        fc_out,
        six[6, :share],
        out_out,
        six[1, :share],
        two[0],
        two[1],
        six[4, :share],
        six[5, :share],
    )


def solution(mesh):
    rows = P(("dp", "tensor"), None)
    vector = P("dp")
    wide = P(("tensor", "dp"))
    weights = (
        P(None, "dp", "tensor"),
        P(None, ("tensor", "dp")),
        P("tensor", "dp"),
        vector,
        P("dp", "tensor"),
        wide,
        P("tensor", "dp"),
        vector,
        vector,
        vector,
        vector,
        vector,
    )
    return jax.shard_map(
        local,
        mesh=mesh,
        in_specs=(rows, *weights, rows),
        out_specs=(rows, rows, *weights),
        check_vma=False,
    )
```

```python
import functools

import jax
import jax.numpy as jnp
from jax import lax
from jax.experimental import pallas as pl
from jax.experimental.pallas import tpu as pltpu
from jax.sharding import PartitionSpec as P

HD = 64
PAIR = 2 * HD
EPSILON = 1e-05
NEGATIVE = -1e30
ROOT_TWO_PI = 0.7978845608028654
F32 = jnp.float32
BF16 = jnp.bfloat16
MIB = 1024 * 1024
SCALE = 0.25
ANY_SPACE = pl.BlockSpec(memory_space=pl.ANY)
SCALARS = pl.BlockSpec(memory_space=pltpu.SMEM)


def params(mib):
    return pltpu.CompilerParams(vmem_limit_bytes=mib * MIB)


def cost(micros):
    return pl.CostEstimate(
        flops=int(micros * SCALE * 1.1e9),
        bytes_accessed=int(micros * SCALE * 1e6),
        transcendentals=0,
    )


def swap_x(value):
    return lax.ppermute(value, "tensor", [(0, 2), (2, 0), (1, 3), (3, 1)])


def swap_core(value):
    return lax.ppermute(value, "tensor", [(0, 1), (1, 0), (2, 3), (3, 2)])


def dot(a, b, contract, kind=F32):
    return lax.dot_general(a, b, (contract, ((), ())), preferred_element_type=kind)


NN = ((1,), (0,))
NT = ((1,), (1,))
TN = ((0,), (0,))


def normalize(values):
    average = jnp.mean(values, axis=-1, keepdims=True)
    centered = values - average
    spread = jnp.mean(centered * centered, axis=-1, keepdims=True)
    factor = lax.rsqrt(spread + EPSILON)
    return centered * factor, factor


def norm_back(unit, factor, gain, grad):
    scaled = grad * gain
    return factor * (
        scaled
        - jnp.mean(scaled, axis=-1, keepdims=True)
        - unit * jnp.mean(scaled * unit, axis=-1, keepdims=True)
    )


def gelu_both(values):
    squared = values * values
    bent = jnp.tanh(ROOT_TWO_PI * values * (1.0 + 0.044715 * squared))
    half = 0.5 * (1.0 + bent)
    slope = half + 0.5 * values * (1.0 - bent * bent) * ROOT_TWO_PI * (
        1.0 + 3.0 * 0.044715 * squared
    )
    return values * half, slope


def split_heads(block):
    first = lax.broadcasted_iota(jnp.int32, block.shape, 1) < HD
    return [jnp.where(first, block, 0.0).astype(BF16), jnp.where(first, 0.0, block).astype(BF16)]


def attend_kernel(qkv_ref, *rest, row0, block):
    mixed_ref, total_ref, kept, acc = rest[-4:]
    count = mixed_ref.shape[0] // block
    first = lax.broadcasted_iota(jnp.int32, (PAIR, block), 0) < HD
    causal = lax.broadcasted_iota(jnp.int32, (block, block), 0) <= lax.broadcasted_iota(
        jnp.int32, (block, block), 1
    )
    for i in range(count):
        start = row0 + i * block
        heads = split_heads(qkv_ref[pl.ds(start, block), 0:PAIR].astype(F32) * (HD**-0.5))
        keys = qkv_ref[pl.ds(start, block), PAIR : 2 * PAIR]
        tops = []
        for h in range(2):
            scores = jnp.where(causal, dot(keys, heads[h], NT), NEGATIVE)
            kept[h, pl.ds(start, block), :] = scores
            tops.append(jnp.max(scores, axis=0, keepdims=True))

        def score_step(j, tops):
            at = pl.multiple_of(j * block, block)
            tile_keys = qkv_ref[pl.ds(at, block), PAIR : 2 * PAIR]
            found = []
            for h in range(2):
                scores = dot(tile_keys, heads[h], NT)
                kept[h, pl.ds(at, block), :] = scores
                found.append(jnp.maximum(tops[h], jnp.max(scores, axis=0, keepdims=True)))
            return tuple(found)

        tops = lax.fori_loop(0, start // block, score_step, tuple(tops))
        acc[...] = jnp.zeros(acc.shape, F32)

        def value_step(j, sums):
            at = pl.multiple_of(j * block, block)
            tile_values = qkv_ref[pl.ds(at, block), 2 * PAIR : 3 * PAIR]
            found = []
            for h in range(2):
                powers = jnp.exp(kept[h, pl.ds(at, block), :] - tops[h])
                found.append(sums[h] + jnp.sum(powers, axis=0, keepdims=True))
                acc[h] += dot(powers.astype(BF16), tile_values, TN)
            return tuple(found)

        zero = jnp.zeros((1, block), F32)
        sums = lax.fori_loop(0, start // block + 1, value_step, (zero, zero))
        inverse = jnp.transpose(jnp.where(first, 1.0 / sums[0], 1.0 / sums[1]))
        lane = lax.broadcasted_iota(jnp.int32, (block, PAIR), 1) < HD
        local = slice(i * block, (i + 1) * block)
        mixed_ref[local, :] = (jnp.where(lane, acc[0], acc[1]) * inverse).astype(BF16)
        for h in range(2):
            total_ref[0, h : h + 1, local] = tops[h] + jnp.log(sums[h])


def attend(qkv, row0, rows, block, after=()):
    pairs = qkv.shape[1] // (3 * PAIR)
    return pl.pallas_call(
        functools.partial(attend_kernel, row0=row0, block=block),
        grid=(pairs,),
        in_specs=[pl.BlockSpec((row0 + rows, 3 * PAIR), lambda j: (0, j))]
        + [ANY_SPACE] * len(after),
        out_specs=[
            pl.BlockSpec((rows, PAIR), lambda j: (0, j)),
            pl.BlockSpec((1, 2, rows), lambda j: (j, 0, 0)),
        ],
        out_shape=[
            jax.ShapeDtypeStruct((rows, pairs * PAIR), BF16),
            jax.ShapeDtypeStruct((pairs, 2, rows), F32),
        ],
        scratch_shapes=[
            pltpu.VMEM((2, row0 + rows, block), F32),
            pltpu.VMEM((2, block, PAIR), F32),
        ],
        compiler_params=params(16),
        cost_estimate=cost(0.01),
        name="attend_%d" % row0,
    )(qkv, *after)


def attend_back_kernel(
    core_ref, qkv_ref, mixed_ref, grad_ref, total_ref, *rest, row0, block, has_before
):
    before_ref = rest[0]
    sent_ref = None
    if has_before:
        out_ref, sums_ref, sent_ref, key_acc, value_acc, query_acc = rest[-6:]
    else:
        out_ref, sums_ref, key_acc, value_acc, query_acc = rest[-5:]
    rows = mixed_ref.shape[0]
    count = rows // block
    lane = lax.broadcasted_iota(jnp.int32, (block, PAIR), 1)
    first = lane < HD
    causal = lax.broadcasted_iota(jnp.int32, (block, block), 0) <= lax.broadcasted_iota(
        jnp.int32, (block, block), 1
    )
    if has_before:
        key_acc[0:row0, :] = before_ref[:, PAIR : 2 * PAIR]
        value_acc[0:row0, :] = before_ref[:, 2 * PAIR : 3 * PAIR]
        key_acc[row0:, :] = jnp.zeros((rows, PAIR), F32)
        value_acc[row0:, :] = jnp.zeros((rows, PAIR), F32)
    else:
        key_acc[...] = jnp.zeros(key_acc.shape, F32)
        value_acc[...] = jnp.zeros(value_acc.shape, F32)
    for i in range(count):
        start = row0 + i * block
        local = slice(i * block, (i + 1) * block)
        query_heads = split_heads(
            qkv_ref[pl.ds(start, block), 0:PAIR].astype(F32) * (HD**-0.5)
        )
        grads = grad_ref[local, :].astype(F32)
        grad_heads = split_heads(grads)
        inner = jnp.transpose(grads * mixed_ref[local, :].astype(F32))
        total_rows = [total_ref[0, h : h + 1, local] for h in range(2)]
        inner_rows = [
            jnp.sum(inner[h * HD : (h + 1) * HD, :], axis=0, keepdims=True) for h in range(2)
        ]

        def tile(at, masked):
            tile_keys = qkv_ref[pl.ds(at, block), PAIR : 2 * PAIR]
            tile_values = qkv_ref[pl.ds(at, block), 2 * PAIR : 3 * PAIR]
            key_sum, value_sum = None, None
            for h in range(2):
                scores = dot(tile_keys, query_heads[h], NT)
                weights = jnp.exp(scores - total_rows[h])
                if masked:
                    weights = jnp.where(causal, weights, 0.0)
                grad_weights = dot(tile_values, grad_heads[h], NT)
                grad_scores = (weights * (grad_weights - inner_rows[h])).astype(BF16)
                value_part = dot(weights.astype(BF16), grad_heads[h], NN)
                key_part = dot(grad_scores, query_heads[h], NN)
                query_part = dot(grad_scores, tile_keys, TN)
                key_sum = key_part if key_sum is None else key_sum + key_part
                value_sum = value_part if value_sum is None else value_sum + value_part
                if masked:
                    query_acc[h] = query_part
                else:
                    query_acc[h] += query_part
            key_acc[pl.ds(at, block), :] += key_sum
            value_acc[pl.ds(at, block), :] += value_sum

        tile(start, True)

        def step(j, carry):
            tile(pl.multiple_of(j * block, block), False)
            return carry

        if start:
            lax.fori_loop(0, start // block, step, 0)
        query_grad = jnp.where(first, query_acc[0], query_acc[1]) * (HD**-0.5)
        out_ref[start : start + block, 0:PAIR] = query_grad.astype(out_ref.dtype)
    if has_before:
        out_ref[0:row0, 0:PAIR] = before_ref[:, 0:PAIR].astype(out_ref.dtype)
    out_ref[:, PAIR : 2 * PAIR] = key_acc[...].astype(out_ref.dtype)
    out_ref[:, 2 * PAIR : 3 * PAIR] = value_acc[...].astype(out_ref.dtype)
    sums_ref[...] = jnp.sum(out_ref[...].astype(F32), axis=0, keepdims=True)
    if has_before:
        size = sent_ref.shape[0] // 2
        for half in range(2):
            at = pl.multiple_of((2 * half + 1 - core_ref[0]) * size, size)
            sent_ref[half * size : (half + 1) * size, :] = out_ref[pl.ds(at, size), :]


def attend_back(qkv, mixed, grads, totals, before, row0, block, pair, pairs, after=(), core=None):
    rows = mixed.shape[0]
    extent = row0 + rows
    narrow = pl.BlockSpec((rows, PAIR), lambda j: (0, pair + j))
    in_specs = [
        SCALARS,
        pl.BlockSpec((extent, 3 * PAIR), lambda j: (0, pair + j)),
        narrow,
        narrow,
        pl.BlockSpec((1, 2, rows), lambda j: (pair + j, 0, 0)),
    ]
    core = jnp.zeros((), jnp.int32) if core is None else core
    operands = [core.reshape(1).astype(jnp.int32), qkv, mixed, grads, totals]
    if before is not None:
        in_specs.append(pl.BlockSpec((row0, 3 * PAIR), lambda j: (0, pair + j)))
        operands.append(before)
    in_specs += [ANY_SPACE] * len(after)
    return pl.pallas_call(
        functools.partial(
            attend_back_kernel, row0=row0, block=block, has_before=before is not None
        ),
        grid=(pairs,),
        in_specs=in_specs,
        out_specs=[
            pl.BlockSpec((extent, 3 * PAIR), lambda j: (0, j)),
            pl.BlockSpec((1, 3 * PAIR), lambda j: (0, j)),
        ]
        + ([] if before is None else [pl.BlockSpec((extent // 2, 3 * PAIR), lambda j: (0, j))]),
        out_shape=[
            jax.ShapeDtypeStruct((extent, pairs * 3 * PAIR), F32 if before is None else BF16),
            jax.ShapeDtypeStruct((1, pairs * 3 * PAIR), F32),
        ]
        + (
            []
            if before is None
            else [jax.ShapeDtypeStruct((extent // 2, pairs * 3 * PAIR), BF16)]
        ),
        scratch_shapes=[
            pltpu.VMEM((extent, PAIR), F32),
            pltpu.VMEM((extent, PAIR), F32),
            pltpu.VMEM((2, block, PAIR), F32),
        ],
        compiler_params=params(20),
        cost_estimate=cost(5.5 * pairs if before is None else 13 * pairs),
        name="attend_back_%d_%d" % (row0, pair),
    )(*operands, *after)


def norm_two_kernel(
    back_ref, recv_ref, residual_ref, cot_ref, vec_ref, proj_ref, *rest, steps
):
    grad_ref, branch_ref, both_ref, sums_ref = rest[-4:]
    z = back_ref[...].astype(F32) + recv_ref[...].astype(F32)
    unit, factor = normalize(residual_ref[...])
    cot = cot_ref[...].astype(F32)
    grad = cot + norm_back(unit, factor, vec_ref[4:5, :], z)
    grad_ref[...] = grad
    branch = grad.astype(BF16)
    branch_ref[...] = branch
    both_ref[...] = dot(branch, proj_ref[...], NN).astype(BF16)

    @pl.when(pl.program_id(0) == 0)
    def _():
        sums_ref[...] = jnp.zeros(sums_ref.shape, F32)

    for at, part in enumerate((branch.astype(F32), cot, z * unit, z)):
        sums_ref[at : at + 1, :] += jnp.sum(part, axis=0, keepdims=True)


def norm_two(back, recv, residual, cot, vectors, proj, after=()):
    rows, width = back.shape
    steps = 2
    block = rows // steps
    strip = pl.BlockSpec((block, width), lambda i: (i, 0))
    return pl.pallas_call(
        functools.partial(norm_two_kernel, steps=steps),
        grid=(steps,),
        in_specs=[
            strip,
            strip,
            strip,
            strip,
            pl.BlockSpec(vectors.shape, lambda i: (0, 0)),
            pl.BlockSpec(proj.shape, lambda i: (0, 0)),
        ]
        + [ANY_SPACE] * len(after),
        out_specs=[
            strip,
            strip,
            pl.BlockSpec((block, proj.shape[1]), lambda i: (i, 0)),
            pl.BlockSpec((8, width), lambda i: (0, 0)),
        ],
        out_shape=[
            jax.ShapeDtypeStruct((rows, width), F32),
            jax.ShapeDtypeStruct((rows, width), BF16),
            jax.ShapeDtypeStruct((rows, proj.shape[1]), BF16),
            jax.ShapeDtypeStruct((8, width), F32),
        ],
        compiler_params=params(10),
        cost_estimate=cost(4),
        name="norm_two",
    )(back, recv, residual, cot, vectors, proj, *after)


def norm_one_kernel(place_ref, low_ref, high_ref, *refs, terms):
    grads, weights = refs[:terms], refs[terms : 2 * terms]
    own_ref, sent_ref, sums_ref = refs[-3:]
    i = pl.program_id(0)
    z = None
    for grad_ref, weight_ref in zip(grads, weights):
        part = dot(grad_ref[...], weight_ref[...], NT)
        z = part if z is None else z + part
    rows = jnp.where(i == 0, low_ref[...].astype(F32), high_ref[...].astype(F32))
    unit, _ = normalize(rows)

    @pl.when(i == 0)
    def _():
        sums_ref[...] = jnp.zeros(sums_ref.shape, F32)

    sums_ref[0:1, :] += jnp.sum(z * unit, axis=0, keepdims=True)
    sums_ref[1:2, :] += jnp.sum(z, axis=0, keepdims=True)

    @pl.when(i == place_ref[0])
    def _():
        own_ref[...] = z

    @pl.when(i != place_ref[0])
    def _():
        sent_ref[...] = z.astype(BF16)


def norm_one(places, low, high, full, received, own_weights, sib_weights, after=()):
    rows, width = low.shape
    pairs = len(full)
    cols = full[0].shape[1]
    whole = pl.BlockSpec((rows, width), lambda i, at: (0, 0))
    weight_specs = [
        pl.BlockSpec((width, cols), functools.partial(lambda pair, i, at: (0, pair), pair))
        for pair in range(pairs)
    ]
    return pl.pallas_call(
        functools.partial(norm_one_kernel, terms=2 * pairs),
        grid_spec=pltpu.PrefetchScalarGridSpec(
            num_scalar_prefetch=1,
            grid=(2,),
            in_specs=[whole, whole]
            + [pl.BlockSpec((rows, cols), lambda i, at: (2 * i + at[1], 0))] * pairs
            + [pl.BlockSpec((rows, cols), lambda i, at: (i, 0))] * pairs
            + weight_specs * 2
            + [ANY_SPACE] * len(after),
            out_specs=[whole, whole, pl.BlockSpec((8, width), lambda i, at: (0, 0))],
        ),
        out_shape=[
            jax.ShapeDtypeStruct((rows, width), F32),
            jax.ShapeDtypeStruct((rows, width), BF16),
            jax.ShapeDtypeStruct((8, width), F32),
        ],
        compiler_params=params(20),
        cost_estimate=cost(8),
        name="norm_one",
    )(
        places,
        low,
        high,
        *full,
        *received,
        *[own_weights] * pairs,
        *[sib_weights] * pairs,
        *after,
    )


def norm_one_back_kernel(
    place_ref, input_ref, own_ref, recv_ref, low_ref, high_ref, vec_ref, out_ref
):
    unit, factor = normalize(input_ref[...].astype(F32))
    z = own_ref[...] + recv_ref[...].astype(F32)
    residual = jnp.where(place_ref[0] == 0, low_ref[...], high_ref[...])
    out_ref[...] = (residual + norm_back(unit, factor, vec_ref[2:3, :], z)).astype(BF16)


def norm_one_back(places, inputs, z_own, z_recv, residual_grads, vectors):
    rows, width = inputs.shape
    steps = 4
    strip = pl.BlockSpec((rows // steps, width), lambda i: (i, 0))
    return pl.pallas_call(
        norm_one_back_kernel,
        grid=(steps,),
        in_specs=[SCALARS]
        + [strip] * 5
        + [pl.BlockSpec(vectors.shape, lambda i: (0, 0))],
        out_specs=strip,
        out_shape=jax.ShapeDtypeStruct((rows, width), BF16),
        compiler_params=params(60),
        cost_estimate=cost(4),
        name="norm_one_back",
    )(places, inputs, z_own, z_recv, *residual_grads, vectors)


def tie_kernel(value_ref, *rest):
    pass


def tie(value, *after):
    return pl.pallas_call(
        tie_kernel,
        in_specs=[ANY_SPACE] * (1 + len(after)),
        out_specs=ANY_SPACE,
        out_shape=jax.ShapeDtypeStruct(value.shape, value.dtype),
        input_output_aliases={0: 0},
        cost_estimate=cost(0.1),
        name="tie",
    )(value, *after)


def place_kernel(me_ref, *refs, parts, side_rows):
    full_ref = refs[-1]
    rows = refs[0].shape[0] - side_rows
    for k in range(parts):
        at = lax.bitwise_xor(me_ref[0], k)
        full_ref[pl.ds(pl.multiple_of(at * rows, rows), rows), :] = refs[k][0:rows, :]
        if side_rows:
            side = pl.multiple_of(parts * rows + at * side_rows, side_rows)
            full_ref[pl.ds(side, side_rows), :] = refs[k][rows:, :]


def place_shares(me, pieces, side_rows, after):
    total, cols = pieces[0].shape
    parts, kind = len(pieces), pieces[0].dtype
    return pl.pallas_call(
        functools.partial(place_kernel, parts=parts, side_rows=side_rows),
        grid=(1,),
        in_specs=[SCALARS]
        + [pl.BlockSpec((total, cols), lambda i: (0, 0))] * parts
        + [ANY_SPACE] * len(after),
        out_specs=pl.BlockSpec((parts * total, cols), lambda i: (0, 0)),
        out_shape=jax.ShapeDtypeStruct((parts * total, cols), kind),
        compiler_params=params(18),
        cost_estimate=cost(3),
        name="place_shares",
    )(me.reshape(1).astype(jnp.int32), *pieces, *after)


def feed_grads_kernel(*refs, tiles, received):
    normed, cots, grads, acts = refs[0:2], refs[2:4], refs[4:6], refs[6:8]
    out_ref = refs[-1]
    i = pl.program_id(0)

    def work(left, right):
        total = dot(left[0][...], right[0][...], TN) + dot(left[1][...], right[1][...], TN)
        if received:
            total = total + refs[8][...].astype(F32)
        out_ref[...] = total.astype(BF16)

    @pl.when(i < tiles)
    def _():
        work(normed, grads)

    @pl.when(i >= tiles)
    def _():
        work(cots, acts)


def feed_grads(normed, cots, grads, acts, first, received, after=()):
    rows, width = normed[0].shape
    hidden_cols = grads[0].shape[1] // 2
    tile = min(512, hidden_cols)
    tiles = hidden_cols // tile
    base = first // tile
    whole = pl.BlockSpec((rows, width), lambda i: (0, 0))
    grad_spec = pl.BlockSpec((rows, tile), lambda i: (0, base + jnp.minimum(i, tiles - 1)))
    act_spec = pl.BlockSpec((rows, tile), lambda i: (0, base + jnp.maximum(i - tiles, 0)))
    out_spec = pl.BlockSpec((width, tile), lambda i: (0, i))
    return pl.pallas_call(
        functools.partial(feed_grads_kernel, tiles=tiles, received=received is not None),
        grid=(2 * tiles,),
        in_specs=[whole] * 4
        + [grad_spec] * 2
        + [act_spec] * 2
        + ([] if received is None else [out_spec])
        + [ANY_SPACE] * len(after),
        out_specs=out_spec,
        out_shape=jax.ShapeDtypeStruct((width, 2 * hidden_cols), BF16),
        compiler_params=params(24),
        cost_estimate=cost(6),
        name="feed_grads",
    )(*normed, *cots, *grads, *acts, *([] if received is None else [received]), *after)


def weight_grads_kernel(y_ref, normed_ref, grad_ref, *refs, with_proj):
    kept_ref, sent_ref = refs[-2:]
    share = kept_ref.shape[1]
    total = dot(normed_ref[...], grad_ref[...], TN)
    if with_proj:
        low_ref, high_ref, low_mixed_ref, high_mixed_ref, recv_ref = refs[:5]
        proj = dot(low_ref[...], low_mixed_ref[...], TN) + dot(
            high_ref[...], high_mixed_ref[...], TN
        )
        proj = proj + recv_ref[...].astype(F32)
        total = jnp.concatenate([total, proj], axis=1)
    even, odd = total[:share], total[share:]
    stays = y_ref[0] == 0
    kept_ref[0] = jnp.where(stays, even, odd)
    sent_ref[0] = jnp.where(stays, odd, even).astype(BF16)


def weight_grads(y, normed, grads, proj, after=()):
    length, width = normed.shape
    cols = grads.shape[1]
    steps, share = 4, width // 8
    in_specs = [
        SCALARS,
        pl.BlockSpec((length, 2 * share), lambda i: (0, i)),
        pl.BlockSpec((length, cols), lambda i: (0, 0)),
    ]
    operands = [y.reshape(1).astype(jnp.int32), normed, grads]
    total = cols
    if proj is not None:
        branches, mixed, received = proj
        rows, head_cols = mixed[0].shape
        total += head_cols
        in_specs += [pl.BlockSpec((rows, 2 * share), lambda i: (0, i))] * 2
        in_specs += [pl.BlockSpec((rows, head_cols), lambda i: (0, 0))] * 2
        in_specs += [pl.BlockSpec((2 * share, head_cols), lambda i: (i, 0))]
        operands += [*branches, *mixed, received]
    return pl.pallas_call(
        functools.partial(weight_grads_kernel, with_proj=proj is not None),
        grid=(steps,),
        in_specs=in_specs + [ANY_SPACE] * len(after),
        out_specs=[pl.BlockSpec((1, share, total), lambda i: (i, 0, 0))] * 2,
        out_shape=[
            jax.ShapeDtypeStruct((steps, share, total), F32),
            jax.ShapeDtypeStruct((steps, share, total), BF16),
        ],
        compiler_params=params(16),
        cost_estimate=cost(4),
        name="weight_grads",
    )(*operands, *after)


def finish_kernel(*refs, pairs, counts):
    qkv_ref, proj_ref, side_ref, fc_ref, out_ref = refs[-5:]
    feed_ref = refs[sum(counts)]
    hidden_cols = fc_ref.shape[1]
    fc_ref[...] = feed_ref[:, :hidden_cols].astype(F32)
    out_ref[...] = jnp.transpose(feed_ref[:, hidden_cols:].astype(F32))
    at = 0
    for pair in range(pairs):
        total = refs[at][...].astype(F32)
        for part in range(1, counts[pair]):
            total = total + refs[at + part][...].astype(F32)
        at += counts[pair]
        share = qkv_ref.shape[1]
        for j in range(3):
            qkv_ref[j, :, pair * PAIR : (pair + 1) * PAIR] = total[:share, j * PAIR : (j + 1) * PAIR]
        if pair == 0:
            proj_ref[...] = jnp.transpose(total[:share, 3 * PAIR :])
        if pair == pairs - 1:
            side_ref[...] = total[share:, : 3 * PAIR]


def finish(terms, feed_sum, share, head_cols, side_rows, after=()):
    pairs = len(terms)
    flat = [term for pair in terms for term in pair]
    hidden_cols = feed_sum.shape[1] // 2
    return pl.pallas_call(
        functools.partial(
            finish_kernel, pairs=pairs, counts=[len(pair) for pair in terms]
        ),
        grid=(1,),
        in_specs=[pl.BlockSpec(term.shape, lambda i: (0, 0)) for term in flat + [feed_sum]]
        + [ANY_SPACE] * len(after),
        out_specs=[
            pl.BlockSpec((3, share, head_cols), lambda i: (0, 0, 0)),
            pl.BlockSpec((head_cols, share), lambda i: (0, 0)),
            pl.BlockSpec((side_rows, 3 * PAIR), lambda i: (0, 0)),
            pl.BlockSpec((share, hidden_cols), lambda i: (0, 0)),
            pl.BlockSpec((hidden_cols, share), lambda i: (0, 0)),
        ],
        out_shape=[
            jax.ShapeDtypeStruct((3, share, head_cols), F32),
            jax.ShapeDtypeStruct((head_cols, share), F32),
            jax.ShapeDtypeStruct((side_rows, 3 * PAIR), F32),
            jax.ShapeDtypeStruct((share, hidden_cols), F32),
            jax.ShapeDtypeStruct((hidden_cols, share), F32),
        ],
        compiler_params=params(60),
        cost_estimate=cost(3),
        name="finish",
    )(*flat, feed_sum, *after)


def project_kernel(rows_ref, vec_ref, shift_ref, weight_ref, *rest):
    normed_ref, out_ref = rest[-2:]
    unit, _ = normalize(rows_ref[...].astype(F32))
    normed_ref[...] = (unit * vec_ref[2:3, :] + vec_ref[3:4, :]).astype(BF16)
    out_ref[...] = (dot(normed_ref[...], weight_ref[...], NN) + shift_ref[...]).astype(BF16)


def project(sequence, vectors, shift, weights, block, after=()):
    length, width = sequence.shape
    cols = shift.shape[1]
    return pl.pallas_call(
        project_kernel,
        grid=(length // block,),
        in_specs=[
            pl.BlockSpec((block, width), lambda i: (i, 0)),
            pl.BlockSpec(vectors.shape, lambda i: (0, 0)),
            pl.BlockSpec(shift.shape, lambda i: (0, 0)),
            pl.BlockSpec((width, cols), lambda i: (0, 0)),
        ]
        + [ANY_SPACE] * len(after),
        out_specs=[
            pl.BlockSpec((block, width), lambda i: (i, 0)),
            pl.BlockSpec((block, cols), lambda i: (i, 0)),
        ],
        out_shape=[
            jax.ShapeDtypeStruct((length, width), BF16),
            jax.ShapeDtypeStruct((length, cols), BF16),
        ],
        compiler_params=params(16),
        cost_estimate=cost(0.01),
        name="project",
    )(sequence, vectors, shift, weights, *after)


def feed_kernel(
    base_ref,
    part_ref,
    recv_ref,
    cot_ref,
    vec_ref,
    shift_own_ref,
    shift_sib_ref,
    fc_own_ref,
    out_own_ref,
    fc_sib_ref,
    out_sib_ref,
    *rest,
    tiles,
):
    residual_ref, normed_ref, act_ref, grad_ref, back_ref, sent_ref, sums_ref = rest[-9:-2]
    back_acc, out_acc = rest[-2:]
    i = pl.program_id(0)
    rows = base_ref.shape[0]

    @pl.when(i == 0)
    def _():
        residual = (
            base_ref[...].astype(F32)
            + part_ref[...].astype(F32)
            + recv_ref[...].astype(F32)
            + vec_ref[0:1, :]
        )
        residual_ref[...] = residual
        unit, _ = normalize(residual)
        normed_ref[...] = (unit * vec_ref[4:5, :] + vec_ref[5:6, :]).astype(BF16)
        back_acc[...] = jnp.zeros(back_acc.shape, F32)
        out_acc[...] = jnp.zeros(out_acc.shape, F32)

    def work(shift_ref, fc_ref, out_ref):
        step = rows // 2
        total = None
        for r in range(2):
            at = slice(r * step, (r + 1) * step)
            hidden = dot(normed_ref[at, :], fc_ref[...], NN) + shift_ref[...]
            grad_act = dot(cot_ref[at, :], out_ref[...], NN)
            act, slope = gelu_both(hidden)
            act = act.astype(BF16)
            grad = (grad_act * slope).astype(BF16)
            act_ref[at, :] = act
            grad_ref[at, :] = grad
            part = jnp.sum(grad.astype(F32), axis=0, keepdims=True)
            total = part if total is None else total + part
            back_acc[at, :] += dot(grad, fc_ref[...], NT)
            out_acc[at, :] += dot(act, out_ref[...], NT)
        sums_ref[...] = total

    @pl.when(i < tiles)
    def _():
        work(shift_own_ref, fc_own_ref, out_own_ref)

    @pl.when(i >= tiles)
    def _():
        work(shift_sib_ref, fc_sib_ref, out_sib_ref)

    @pl.when(i == 2 * tiles - 1)
    def _():
        back_ref[...] = back_acc[...].astype(BF16)
        sent_ref[...] = out_acc[...].astype(BF16)


def feed(base, part, recv, cot, vectors, shift_own, shift_sib, own, sib, after=()):
    rows, width = base.shape
    hidden_cols = shift_own.shape[1]
    tile = min(512, hidden_cols)
    tiles = hidden_cols // tile
    whole = pl.BlockSpec((rows, width), lambda i: (0, 0))

    def low(i):
        return jnp.minimum(i, tiles - 1)

    def high(i):
        return jnp.maximum(i - tiles, 0)

    return pl.pallas_call(
        functools.partial(feed_kernel, tiles=tiles),
        grid=(2 * tiles,),
        in_specs=[
            whole,
            whole,
            whole,
            whole,
            pl.BlockSpec(vectors.shape, lambda i: (0, 0)),
            pl.BlockSpec((1, tile), lambda i: (0, low(i))),
            pl.BlockSpec((1, tile), lambda i: (0, high(i))),
            pl.BlockSpec((width, tile), lambda i: (0, low(i))),
            pl.BlockSpec((width, tile), lambda i: (0, tiles + low(i))),
            pl.BlockSpec((width, tile), lambda i: (0, high(i))),
            pl.BlockSpec((width, tile), lambda i: (0, tiles + high(i))),
        ]
        + [ANY_SPACE] * len(after),
        out_specs=[
            whole,
            whole,
            pl.BlockSpec((rows, tile), lambda i: (0, i)),
            pl.BlockSpec((rows, tile), lambda i: (0, i)),
            whole,
            whole,
            pl.BlockSpec((1, tile), lambda i: (0, i)),
        ],
        out_shape=[
            jax.ShapeDtypeStruct((rows, width), F32),
            jax.ShapeDtypeStruct((rows, width), BF16),
            jax.ShapeDtypeStruct((rows, 2 * hidden_cols), BF16),
            jax.ShapeDtypeStruct((rows, 2 * hidden_cols), BF16),
            jax.ShapeDtypeStruct((rows, width), BF16),
            jax.ShapeDtypeStruct((rows, width), BF16),
            jax.ShapeDtypeStruct((1, 2 * hidden_cols), F32),
        ],
        scratch_shapes=[pltpu.VMEM((rows, width), F32), pltpu.VMEM((rows, width), F32)],
        compiler_params=params(32),
        cost_estimate=cost(16),
        name="feed",
    )(
        base, part, recv, cot, vectors, shift_own, shift_sib, own, own, sib, sib, *after
    )


def swap_dp(value, mask):
    size = lax.axis_size("dp")
    return lax.ppermute(value, "dp", [(i, i ^ mask) for i in range(size)])


def gather_z(shard):
    return {k: swap_dp(shard, k) for k in (6, 4, 2)}


def gather_whole(shard, side_rows):
    rows, cols = shard.shape[0] - side_rows, shard.shape[1]
    full = lax.all_gather(shard, "dp", axis=0)
    return jnp.concatenate(
        [full[:, :rows].reshape(-1, cols), full[:, rows:].reshape(-1, cols)], axis=0
    )


def scatter_y(sent, parts):
    return swap_dp(sent, 1) if parts == 8 else None


def scatter_z(kept, sent, received, side, parts):
    if parts != 8:
        whole = jnp.concatenate([kept, sent.astype(F32)], axis=1)
        whole = whole.reshape(parts, -1, whole.shape[2])
        if side is not None:
            whole = jnp.concatenate([whole, side], axis=1)
        return [lax.psum_scatter(whole.astype(BF16), "dp", scatter_dimension=0)]
    sums = kept + received.astype(F32)
    z = lax.axis_index("dp") // 2
    terms = [lax.dynamic_index_in_dim(sums, z, 0, keepdims=False)]
    for k in (3, 2, 1):
        sent = lax.dynamic_index_in_dim(sums, z ^ k, 0, keepdims=False).astype(BF16)
        terms.append(swap_dp(sent, 2 * k))
    return terms


def local(
    inputs,
    qkv_weight,
    qv_bias,
    proj_weight,
    proj_bias,
    fc_weight,
    fc_bias,
    out_weight,
    out_bias,
    attn_norm_gain,
    attn_norm_bias,
    mlp_norm_gain,
    mlp_norm_bias,
    cotangent,
):
    width = inputs.shape[1]
    rows = inputs.shape[0]
    share = proj_bias.shape[0]
    parts = width // share
    head_cols = qkv_weight.shape[2]
    pairs = head_cols // PAIR
    qkv_cols = 3 * head_cols
    hidden_cols = fc_weight.shape[1]
    place = lax.axis_index("tensor")
    core = place % 2
    is_low = place < 2
    is_first = core == 0

    def pick_x(low, high):
        return jnp.where(is_low, low, high)

    mlp_shard = jnp.concatenate([fc_weight, out_weight.T], axis=1)
    qv_row = jnp.pad(qv_bias.reshape(-1), (0, share - qv_bias.size))
    vectors = jnp.stack(
        [
            proj_bias,
            out_bias,
            attn_norm_gain,
            attn_norm_bias,
            mlp_norm_gain,
            mlp_norm_bias,
            fc_bias,
            qv_row,
        ]
    )
    qkv_shard = jnp.transpose(
        qkv_weight.reshape(3, share, pairs, PAIR), (1, 2, 0, 3)
    ).reshape(share, qkv_cols)
    attn_shard = jnp.concatenate([qkv_shard, proj_weight.T], axis=1)
    side_rows = 16
    vectors = jnp.pad(
        vectors.reshape(1, -1), ((0, side_rows - 1), (0, attn_shard.shape[1] - vectors.size))
    )
    attn_shard = jnp.concatenate([attn_shard, vectors], axis=0)

    input_x_sent = swap_x(inputs)
    input_core = swap_core(inputs)
    cot_x = swap_x(cotangent)
    blocks = []

    def assemble(late):
        input_x = tie(input_x_sent, *late)
        input_far = swap_core(input_x)
        low, high = pick_x(inputs, input_x), pick_x(input_x, inputs)
        far_low, far_high = pick_x(input_core, input_far), pick_x(input_far, input_core)
        sequence = jnp.concatenate(
            [
                jnp.where(is_first, low, far_low),
                jnp.where(is_first, far_low, low),
                jnp.where(is_first, high, far_high),
                jnp.where(is_first, far_high, high),
            ],
            axis=0,
        )
        blocks.extend([low, high, sequence])
        return (sequence,)

    if parts == 8:
        shares = {0: attn_shard, **gather_z(attn_shard)}
        mlp_shares = {0: mlp_shard, 1: swap_dp(mlp_shard, 1)}
        for k in (0, 2, 4, 6):
            shares[k + 1] = swap_dp(shares[k], 1)
        mlp_shares.update(gather_z(tie(mlp_shard, *(shares[k] for k in (2, 4, 6)))))
        behind = tuple(shares[k] for k in (6, 5, 3, 1))
        behind += (mlp_shares[1], mlp_shares[2], cot_x)
        for k in (2, 4):
            mlp_shares[k + 1] = swap_dp(mlp_shares[k], 1)
        attn_all = place_shares(
            lax.axis_index("dp"),
            [shares[k] for k in range(parts)],
            side_rows,
            assemble(behind),
        )
        early = (mlp_shares[3],)
    else:
        attn_all = gather_whole(attn_shard, side_rows)
        assemble((attn_all,))
        early = ()
    input_low, input_high, sequence = blocks
    attn_sib = swap_core(attn_all)
    vectors = attn_all[width:].reshape(parts, side_rows, -1)[:, 0, : 8 * share]
    vectors = vectors.reshape(parts, 8, share).transpose(1, 0, 2).reshape(8, width)
    columns = vectors.astype(F32)
    out_shift, gain_one = columns[1:2], columns[2:3]
    fc_shift_own = columns[6:7]
    fc_shift_sib = attn_sib[width:].reshape(parts, side_rows, -1)[:, 0, 6 * share : 7 * share]
    fc_shift_sib = fc_shift_sib.reshape(1, width).astype(F32)
    qv_shift = (
        columns[7]
        .reshape(parts, share)[:, : share // 2]
        .reshape(parts, 2, share // 4)
        .transpose(1, 0, 2)
        .reshape(2, head_cols)
    )
    qkv_shift = jnp.stack([qv_shift[0], jnp.zeros_like(qv_shift[0]), qv_shift[1]])
    qkv_shift = qkv_shift.reshape(3, pairs, PAIR).transpose(1, 0, 2).reshape(1, qkv_cols)
    proj_both = jnp.concatenate(
        [
            attn_all[:width, qkv_cols : qkv_cols + head_cols],
            attn_sib[:width, qkv_cols : qkv_cols + head_cols],
        ],
        axis=1,
    )

    normed_one, qkv = project(sequence, columns, qkv_shift, attn_all, rows)
    cots = [pick_x(cotangent, cot_x), pick_x(cot_x, cotangent)]

    inputs_two = [input_low, input_high]
    mixed, totals, mixed_own, mixed_sib, parts_two, received_two = [], [], [], [], [], []
    for half in range(2):
        half_mixed, half_totals = attend(
            qkv, half * 2 * rows, 2 * rows, rows, after=tuple(parts_two) + early * half
        )
        mixed.append(half_mixed)
        totals.append(half_totals)
        two = half_mixed.reshape(2, rows, head_cols)
        mine = jnp.where(is_first, two[0], two[1])
        received = swap_core(jnp.where(is_first, two[1], two[0]))
        both = jnp.concatenate([mine, received], axis=1)
        mixed_own.append(mine)
        mixed_sib.append(received)
        part = dot(both, proj_both, NT).astype(BF16)
        parts_two.append(part)
        received_two.append(swap_x(part))
    if parts == 8:
        mlp_shares[7] = swap_dp(mlp_shares[6], 1)
        mlp_all = place_shares(
            lax.axis_index("dp"),
            [mlp_shares[k] for k in range(parts)],
            0,
            (received_two[0], parts_two[1]),
        )
    else:
        mlp_all = gather_whole(mlp_shard, 0)
    mlp_sib = swap_core(mlp_all)
    residuals, normed_two, acts, grads_hidden, backs, out_parts = [], [], [], [], [], []
    fc_bias_sums = 0.0
    for half in range(2):
        residual, normed, act, grad_hidden, back, out_part, sums = feed(
            inputs_two[half],
            parts_two[half],
            received_two[half],
            cots[half],
            columns,
            fc_shift_own,
            fc_shift_sib,
            mlp_all,
            mlp_sib,
            after=(parts_two[1],),
        )
        residuals.append(residual)
        normed_two.append(normed)
        acts.append(act)
        grads_hidden.append(grad_hidden)
        backs.append(back)
        out_parts.append(out_part)
        fc_bias_sums = fc_bias_sums + sums[0]
    back_recv = [swap_x(back) for back in backs]

    sib_grads = feed_grads(
        normed_two, cots, grads_hidden, acts, hidden_cols, None, after=(back_recv[0],)
    )
    sib_received = swap_core(sib_grads)

    grad_residuals, branches, grads_mixed = [], [], []
    for half in range(2):
        grad_residual, branch, grad_both, sums_two = norm_two(
            backs[half],
            back_recv[half],
            residuals[half],
            cots[half],
            columns,
            proj_both,
            after=(sib_grads,) if half == 0 else (low_grads,),
        )
        grad_residuals.append(grad_residual)
        branches.append(branch)
        mine = grad_both[:, :head_cols]
        received = swap_core(grad_both[:, head_cols:])
        grads_mixed.append(
            jnp.concatenate(
                [jnp.where(is_first, mine, received), jnp.where(is_first, received, mine)], axis=0
            )
        )
        vec_two = sums_two if half == 0 else vec_two + sums_two
        if half == 0:
            grad_mlp = feed_grads(
                normed_two, cots, grads_hidden, acts, 0, sib_received, after=(branch,)
            )
            mlp_sum = lax.psum_scatter(grad_mlp, "dp", scatter_dimension=0, tiled=True)
            low_grads, _ = attend_back(
                qkv,
                mixed[0],
                grads_mixed[0],
                totals[0],
                None,
                0,
                rows,
                0,
                pairs,
                after=(grad_mlp,),
            )
    proj_sib = dot(branches[0], mixed_sib[0], TN) + dot(branches[1], mixed_sib[1], TN)
    proj_received = swap_core(proj_sib.astype(BF16))

    out_sent = tie(pick_x(out_parts[1], out_parts[0]), low_grads)
    out_recv = swap_x(out_sent)

    y = lax.axis_index("dp") % 2 if parts == 8 else jnp.zeros((), jnp.int32)
    place_ids = jnp.stack([place // 2, core]).astype(jnp.int32)
    full_grads, grads_received, side_sums, exchanges = [], [], [], []
    after = ()
    for pair in range(pairs):
        grad_pair, pair_sums, grad_sent = attend_back(
            qkv,
            mixed[1],
            grads_mixed[1],
            totals[1],
            low_grads,
            2 * rows,
            rows,
            pair,
            1,
            after=after,
            core=core,
        )
        full_grads.append(grad_pair)
        side_sums.append(pair_sums)
        if pair > 0 and parts == 8:
            grad_sent = tie(grad_sent, exchanges[-1][2])
        grads_received.append(swap_core(grad_sent))
        proj = (branches, mixed_own, proj_received) if pair == 0 else None
        if pair == 0:
            out_recv = tie(out_recv, grad_pair)
        kept, sent = weight_grads(y, normed_one, grad_pair, proj)
        received = scatter_y(sent, parts) if pair < pairs - 1 else None
        exchanges.append((kept, sent, received))
        after = (sent, out_recv)

    z_own, z_sent, vec_one = norm_one(
        place_ids,
        input_low,
        input_high,
        full_grads,
        grads_received,
        attn_all,
        attn_sib,
        after=(exchanges[-1][1],),
    )
    first_terms = scatter_z(*exchanges[0], side=None, parts=parts)
    z_recv = swap_x(z_sent)
    vec_two = vec_two + swap_core(vec_two)
    fc_bias_grad = fc_bias_sums[:hidden_cols] + swap_core(fc_bias_sums[hidden_cols:])

    vec_grads = jnp.concatenate(
        [
            vec_two[:2],
            vec_one[:2],
            vec_two[2:4],
            fc_bias_grad[None],
            jnp.zeros((1, width), F32),
        ],
        axis=0,
    )
    vec_blocks = vec_grads.reshape(8, parts, share).transpose(1, 0, 2)
    vec_blocks = jnp.pad(vec_blocks, ((0, 0), (0, 0), (0, 3 * PAIR - share)))
    pair_rows = jnp.pad(jnp.concatenate(side_sums, axis=0), ((0, 8 - pairs), (0, 0)))
    side = jnp.concatenate(
        [vec_blocks, jnp.broadcast_to(pair_rows[None], (parts, 8, 3 * PAIR))], axis=1
    )
    views = side.reshape((-1, 2) + side.shape[1:])
    side_kept = lax.dynamic_index_in_dim(views, y, 1, keepdims=False)
    side_sent = lax.dynamic_index_in_dim(views, 1 - y, 1, keepdims=False)
    terms = [first_terms]
    for pair in range(1, pairs):
        kept, sent, received = exchanges[pair]
        last = pair == pairs - 1
        if last and parts == 8:
            kept = jnp.concatenate([kept, side_kept], axis=1)
            sent = jnp.concatenate([sent, side_sent.astype(BF16)], axis=1)
            received = tie(scatter_y(sent, parts), *first_terms[1:])
        terms.append(scatter_z(kept, sent, received, side if last else None, parts))

    out_recv = tie(out_recv, z_sent)
    out_mine = pick_x(out_parts[0], out_parts[1])
    outputs = (
        pick_x(residuals[0], residuals[1])
        + out_mine.astype(F32)
        + out_recv.astype(F32)
        + out_shift
    ).astype(BF16)

    qkv_out, proj_out, six, fc_out, out_out = finish(
        terms, mlp_sum, share, head_cols, side_rows, after=(outputs, z_recv)
    )
    grad_inputs = norm_one_back(
        place_ids, inputs, z_own, tie(z_recv, six), grad_residuals, columns
    )
    one = six[2:4, :share]
    far = lax.ppermute(one, "tensor", [(i, i ^ 3) for i in range(4)])
    two = one + swap_core(one) + swap_x(one) + far
    piece = share // 4
    start = lax.axis_index("dp") * piece
    mine = lax.dynamic_index_in_dim(six[8 : 8 + pairs], start // PAIR, 0, keepdims=False)
    qv_out = lax.dynamic_slice_in_dim(mine.reshape(3, PAIR), start % PAIR, piece, 1)[0::2]
    return (
        outputs,
        grad_inputs,
        qkv_out,
        qv_out,
        proj_out,
        six[0, :share],
        fc_out,
        six[6, :share],
        out_out,
        six[1, :share],
        two[0],
        two[1],
        six[4, :share],
        six[5, :share],
    )


def solution(mesh):
    rows = P(("dp", "tensor"), None)
    vector = P("dp")
    wide = P(("tensor", "dp"))
    weights = (
        P(None, "dp", "tensor"),
        P(None, ("tensor", "dp")),
        P("tensor", "dp"),
        vector,
        P("dp", "tensor"),
        wide,
        P("tensor", "dp"),
        vector,
        vector,
        vector,
        vector,
        vector,
    )
    return jax.shard_map(
        local,
        mesh=mesh,
        in_specs=(rows, *weights, rows),
        out_specs=(rows, rows, *weights),
        check_vma=False,
    )
```
